256 devices in a mesh: dom: 128 (over y, z, x_hi, core), rep: 2 (over x_lo).
Axes of the slice: x: 4 (x_hi: 2, x_lo: 2; x = x_hi * 2 + x_lo), y: 4, z: 8, core: 2. Of those that a mesh axis runs over, the one named last changes fastest.
Arguments:
- left_table: float32 [131072, 400], P('dom'), may hold values from -3 to 3
- left_state: float32 [131072], P('dom'), may hold values from 0.01 to 1
- right_table: float32 [131072, 400], P('dom'), may hold values from -30 to 30
- right_state: float32 [131072], P('dom'), may hold values from 0.01 to 1
- rel_table: float32 [3072, 400], P(('dom', 'rep')), may hold values from -3 to 3
- rel_state: float32 [3072], P(('dom', 'rep')), may hold values from 0.01 to 1
- sources: int32 [1048576], P(('dom', 'rep')), may hold values from 0 to 1023
- relations: int32 [1048576], P(('dom', 'rep')), may hold values from 0 to 3071
- targets: int32 [1048576], P(('dom', 'rep')), may hold values from 0 to 1023
- bucket_counts: int32 [128], P('dom'), may hold values from 1 to 6144, as said below
- negatives: int32 [2048, 1024], P(('dom', 'rep')), may hold values from 0 to 1023
Outputs:
- left_next: float32 [131072, 400], P('dom')
- left_state_next: float32 [131072], P('dom')
- right_next: float32 [131072, 400], P('dom')
- right_state_next: float32 [131072], P('dom')
- rel_next: float32 [3072, 400], P(('dom', 'rep'))
- rel_state_next: float32 [3072], P(('dom', 'rep'))
The draws below stay inside these ranges and needn't reach their ends.
Inputs may be any that keep to these rules, and one draw needn't show every extreme that they name: The live edges of bucket d are its first bucket_counts[d] slots; one bucket has exactly 6144 live edges and another exactly 1.
All inputs are finite; a program needn't handle non-finite values.
Results may differ from the reference program's by a relative error of at most 0.004.
The reference program's roundings to bfloat16 on the way (of `neg_prob`) count: a program that leaves them out, or rounds other values in their place, can miss the bound.
Values sent between devices are 32-bit elements; how exact they have to be, the bound alone decides.
A program may use at most 128 MiB of HBM per device.

```python
import math
import jax
import jax.numpy as jnp
from jax import lax

D = 400
REL = 3072
NEG = 1024
GROUP = 512
E_PART = 1024
GROUPS_REP = 8
MOST = 6144
EDGES = 1048576
ENTITIES = 131072
N_DOM = 128


def draw_left_table(key, part):
    key = jax.random.fold_in(key, 11)
    return 0.5 * jnp.clip(jax.random.normal(key, (ENTITIES, D), jnp.float32), -6.0, 6.0)


def draw_right_table(key, part):
    key = jax.random.fold_in(key, 12)
    return 0.5 * jnp.clip(jax.random.normal(key, (ENTITIES, D), jnp.float32), -6.0, 6.0)


def draw_bucket_counts(key, part):
    key = jax.random.fold_in(key, 13)
    first_key, second_key, third_key = jax.random.split(key, 3)
    first = jax.random.randint(first_key, (N_DOM,), 0, MOST)
    second = jax.random.randint(second_key, (N_DOM,), 0, MOST)
    counts = 1 + MOST // 2 + first * second // (2 * MOST)
    picked = jax.random.randint(third_key, (), 0, N_DOM)
    places = jnp.arange(N_DOM)
    counts = jnp.where(places == picked, MOST, counts)
    counts = jnp.where(places == (picked + 1) % N_DOM, 1, counts)
    return counts.astype(jnp.int32)


def plant(result, rng, least, high):
    longest = result.shape.index(max(result.shape))
    spots = []
    for shift in (0, 1):
        where = [jax.random.randint(jax.random.fold_in(rng, axis), (), 0, length) for axis, length in enumerate(result.shape)]
        where[longest] = (where[longest] + shift) % result.shape[longest]
        spots.append(tuple(where))
    return result.at[spots[0]].set(least).at[spots[1]].set(high)


def steps_of(own_key, extent, cuts, smallest, high):
    loudness, own = 1.0, jax.random.fold_in(own_key, 6)
    for position, blocks in cuts:
        steps = jnp.exp(jax.random.uniform(jax.random.fold_in(own, position), (blocks,), jnp.float32, smallest / len(cuts), high / len(cuts)))
        loudness = loudness * jnp.repeat(steps, extent[position] // blocks).reshape([-1 if axis == position else 1 for axis in range(len(extent))])
    return loudness


def bell_draw(own_key, shape, width, bound, shards=(), kind=jnp.bfloat16):
    values = jax.random.normal(own_key, shape, jnp.float32) * width
    if len(shards) > 0:
        values = steps_of(own_key, shape, shards, -0.22, 0.18) * values
    return jnp.clip(values, min=-bound, max=bound).astype(kind)


def setup_inputs(seed: int = 0) -> dict:
    arg_keys = jax.random.split(jax.random.key(seed), 12)
    return {
        "left_table": draw_left_table(jax.random.fold_in(arg_keys[11], 71), 0),
        "left_state": jnp.clip(jnp.exp(math.log(1.0) - 4.6051702 * jax.random.uniform(arg_keys[1], (ENTITIES,), jnp.float32) ** steps_of(arg_keys[1], (ENTITIES,), ((0, 128),), -0.2, 0.2)), 0.01, 1.0),
        "right_table": draw_right_table(jax.random.fold_in(arg_keys[11], 71), 0),
        "right_state": jnp.clip(jnp.exp(math.log(1.0) - 4.6051702 * jax.random.uniform(arg_keys[3], (ENTITIES,), jnp.float32) ** steps_of(arg_keys[3], (ENTITIES,), ((0, 128),), -0.2, 0.2)), 0.01, 1.0),
        "rel_table": bell_draw(arg_keys[4], (REL, D), 0.5, 3.0, ((0, 256),), jnp.float32),
        "rel_state": jnp.clip(jnp.exp(math.log(1.0) - 4.6051702 * jax.random.uniform(arg_keys[5], (REL,), jnp.float32) ** steps_of(arg_keys[5], (REL,), ((0, 256),), -0.2, 0.2)), 0.01, 1.0),
        "sources": plant(jax.random.randint(arg_keys[6], (EDGES,), 0, E_PART), jax.random.fold_in(arg_keys[6], 1), 0, E_PART - 1).astype(jnp.int32),
        "relations": plant(jax.random.randint(arg_keys[7], (EDGES,), 0, REL), jax.random.fold_in(arg_keys[7], 1), 0, REL - 1).astype(jnp.int32),
        "targets": plant(jax.random.randint(arg_keys[8], (EDGES,), 0, E_PART), jax.random.fold_in(arg_keys[8], 1), 0, E_PART - 1).astype(jnp.int32),
        "bucket_counts": draw_bucket_counts(jax.random.fold_in(arg_keys[11], 71), 0),
        "negatives": plant(jax.random.randint(arg_keys[10], (N_DOM * 2 * GROUPS_REP, NEG), 0, E_PART), jax.random.fold_in(arg_keys[10], 1), 0, E_PART - 1).astype(jnp.int32),
    }


LEARNING_RATE = 0.3

def complex_product(first, second, conjugate):
    half = first.shape[-1] // 2
    first_re = first[..., :half]
    first_im = first[..., half:]
    second_re = second[..., :half]
    second_im = second[..., half:]
    if conjugate:
        second_im = -second_im
    return jnp.concatenate([first_re * second_re - first_im * second_im, first_re * second_im + first_im * second_re], axis=-1)

def adagrad(table, state, grad):
    new_state = state + lax.optimization_barrier(jnp.mean(grad * grad, axis=-1))
    return (table - LEARNING_RATE * grad / jnp.sqrt(new_state)[:, None], new_state)

def group_terms(left_part, right_part, rel_full, src, rel, dst, neg, live):
    heads = left_part[src]
    rel_rows = rel_full[rel]
    tails = right_part[dst]
    query = complex_product(heads, rel_rows, False)
    positive = lax.optimization_barrier(jnp.sum(query * tails, axis=-1))
    query_low = query.astype(jnp.bfloat16)
    negative_rows = right_part[neg].astype(jnp.bfloat16)
    scores = lax.dot_general(query_low, negative_rows, (((1,), (1,)), ((), ())), preferred_element_type=jnp.float32)
    top = jnp.maximum(positive, lax.optimization_barrier(jnp.max(scores, axis=1)))
    pos_exp = jnp.exp(positive - top)
    neg_exp = jnp.exp(scores - top[:, None])
    total = pos_exp + lax.optimization_barrier(jnp.sum(neg_exp, axis=1))
    weight = live / total
    pos_coef = pos_exp * weight - live
    neg_prob = (neg_exp * weight[:, None]).astype(jnp.bfloat16)
    d_query = pos_coef[:, None] * tails + jnp.dot(neg_prob, negative_rows, preferred_element_type=jnp.float32)
    d_negatives = lax.dot_general(neg_prob, query_low, (((0,), (0,)), ((), ())), preferred_element_type=jnp.float32)
    d_heads = complex_product(d_query, rel_rows, True)
    d_rel = complex_product(d_query, heads, True)
    d_tails = pos_coef[:, None] * query
    return (d_heads, d_rel, d_tails, d_negatives)

def add_group(grads, left_part, right_part, rel_full, src, rel, dst, neg, live):
    left_grad, right_grad, rel_grad = grads
    d_heads, d_rel, d_tails, d_negatives = group_terms(left_part, right_part, rel_full, src, rel, dst, neg, live)
    left_grad = left_grad.at[src].add(d_heads)
    right_grad = right_grad.at[dst].add(d_tails).at[neg].add(d_negatives)
    rel_grad = rel_grad.at[rel].add(d_rel)
    return (left_grad, right_grad, rel_grad)

def reference(left_table, left_state, right_table, right_state, rel_table, rel_state, sources, relations, targets, bucket_counts, negatives):
    blocks = 2 * GROUPS_REP
    lefts = left_table.reshape(N_DOM, E_PART, D)
    left_states = left_state.reshape(N_DOM, E_PART)
    rights = right_table.reshape(N_DOM, E_PART, D)
    right_states = right_state.reshape(N_DOM, E_PART)
    srcs = sources.reshape(N_DOM, blocks, GROUP)
    rels = relations.reshape(N_DOM, blocks, GROUP)
    dsts = targets.reshape(N_DOM, blocks, GROUP)
    negs = negatives.reshape(N_DOM, blocks, NEG)
    slots = jnp.arange(GROUP, dtype=jnp.int32)
    order = jnp.arange(blocks, dtype=jnp.int32)

    def bucket(rel_grad, inputs):
        left_part, left_st, right_part, right_st, src_b, rel_b, dst_b, neg_b, count = inputs

        def block(grads, pieces):
            index, src, rel, dst, neg = pieces
            live = (index * GROUP + slots < count).astype(jnp.float32)

            def work(carried):
                return add_group(carried, left_part, right_part, rel_table, src, rel, dst, neg, live)

            def keep(carried):
                return carried
            return (lax.cond(index * GROUP < count, work, keep, grads), None)
        start = (jnp.zeros_like(left_part), jnp.zeros_like(right_part), rel_grad)
        (left_grad, right_grad, rel_grad), unused = lax.scan(block, start, (order, src_b, rel_b, dst_b, neg_b))
        left_new, left_st_new = adagrad(left_part, left_st, left_grad)
        right_new, right_st_new = adagrad(right_part, right_st, right_grad)
        return (rel_grad, (left_new, left_st_new, right_new, right_st_new))
    rel_grad, results = lax.scan(bucket, jnp.zeros_like(rel_table), (lefts, left_states, rights, right_states, srcs, rels, dsts, negs, bucket_counts))
    left_next = results[0].reshape(ENTITIES, D)
    left_state_next = results[1].reshape(ENTITIES)
    right_next = jnp.roll(results[2].reshape(ENTITIES, D), E_PART, axis=0)
    right_state_next = jnp.roll(results[3].reshape(ENTITIES), E_PART, axis=0)
    rel_next, rel_state_next = adagrad(rel_table, rel_state, rel_grad)
    return (left_next, left_state_next, right_next, right_state_next, rel_next, rel_state_next)
```

```python
import jax
import jax.numpy as jnp
from jax import lax
from jax.experimental import pallas as pl
from jax.experimental.pallas import tpu as pltpu
from jax.sharding import PartitionSpec as P

RATE = 0.3
D, LANES = 400, 128
E_PART, GROUP, NEG = 1024, 512, 1024
CHUNK = 128
Y, Z, X = 4, 8, 4
SHARD = 48
MAJOR = 32
SLOTS = 4096
F32, BF16, I32 = jnp.float32, jnp.bfloat16, jnp.int32
MESH = pl.DeviceIdType.MESH
VMEM = pl.BlockSpec(memory_space=pltpu.VMEM)
SMEM = pl.BlockSpec(memory_space=pltpu.SMEM)
HBM = pl.BlockSpec(memory_space=pltpu.HBM)
LIMIT = 60 * 2**20


def tiles_of(ref, first, n):
    rows = pl.ds(first, n)
    lane = lax.broadcasted_iota(I32, (n, LANES), 1)
    a, b, c = (ref[rows, pl.ds(j * LANES, LANES)] for j in range(3))
    d = jnp.concatenate([ref[rows, pl.ds(384, 16)], jnp.zeros((n, LANES - 16), F32)], axis=1)
    b1, c1, d1 = (pltpu.roll(v, 56, 1) for v in (b, c, d))
    zero = jnp.zeros((n, LANES), F32)
    return (
        a,
        jnp.where(lane < 72, b, zero),
        jnp.where(lane < 56, b1, c1),
        jnp.where(lane < 56, c1, jnp.where(lane < 72, d1, zero)),
    )


def natural_of(tiles):
    a, b, c, d = tiles
    lane = lax.broadcasted_iota(I32, a.shape, 1)
    c1, d1 = (pltpu.roll(v, 72, 1) for v in (c, d))
    return (a, jnp.where(lane < 72, b, c1), jnp.where(lane < 72, c1, d1), d1[:, :16])


def place():
    dom, xl = lax.axis_index("dom"), lax.axis_index("rep")
    core = lax.rem(dom, 2)
    xh = lax.rem(dom // 2, 2)
    z = lax.rem(dom // 4, Z)
    y = dom // (4 * Z)
    return y, z, xh, core, xl


def device(y, z, xh, core, xl):
    return {"dom": ((y * Z + z) * 2 + xh) * 2 + core, "rep": xl}


def shift_x(xh, xl, k):
    x = lax.rem(xh * 2 + xl + k, X)
    return x // 2, lax.rem(x, 2)


def greet(peers):
    barrier = pltpu.get_barrier_semaphore()
    for peer in peers:
        pl.semaphore_signal(barrier, inc=1, device_id=peer, device_id_type=MESH)
    pl.semaphore_wait(barrier, len(peers))


def neighbours():
    y, z, xh, core, xl = place()
    sib = device(y, z, xh, 1 - core, xl)
    xs = [(*shift_x(xh, xl, k),) for k in range(1, X)]
    xdev = [device(y, z, a, core, b) for a, b in xs]
    ydev = [device(lax.rem(y + k, Y), z, xh, core, xl) for k in range(1, Y)]
    zdev = [device(y, lax.rem(z + k, Z), xh, core, xl) for k in range(1, Z)]
    return sib, xdev, ydev, zdev


def remote(src, dst, send, recv, to):
    copy = pltpu.make_async_remote_copy(
        src_ref=src, dst_ref=dst, send_sem=send, recv_sem=recv, device_id=to, device_id_type=MESH
    )
    copy.start()
    return copy


def family():
    y, z, xh, core, xl = place()
    dom = lax.axis_index("dom")
    twin = dom + 1 - 2 * core
    return {"dom": twin, "rep": xl}, {"dom": dom, "rep": 1 - xl}, {"dom": twin, "rep": 1 - xl}


def prepared(src, dst, send, recv, to):
    return pltpu.make_async_remote_copy(
        src_ref=src, dst_ref=dst, send_sem=send, recv_sem=recv, device_id=to, device_id_type=MESH
    )


def gather_kernel(
    shard, src, rel, dst, neg, count, left, right,
    full, src_all, rel_all, dst_all, neg_all, count_use, left_use, right_use,
    rows, count_rows, zs, zr, ps, pr, cs, cr, es, ea, eb, ts, tr, local,
):
    y, z, xh, core, xl = place()
    sib, xdev, ydev, zdev = neighbours()
    _, partner, diagonal = family()
    greet([sib, partner, diagonal] + xdev + ydev + zdev)
    lane = lax.broadcasted_iota(I32, (12, LANES), 1)
    for j, tile in enumerate(tiles_of(shard, 0, 12)):
        rows[pl.ds(j, 12, stride=4), :] = tile
    first = [remote(rows, full.at[y, z, xh, core, xl], zs.at[k], zr.at[k], zdev[k]) for k in range(Z - 1)]
    own = pltpu.make_async_copy(rows, full.at[y, z, xh, core, xl], local.at[0])
    own.start()
    count_rows[...] = jnp.full((8, LANES), count[0], I32)

    lists = [
        (v, w.at[pl.ds(xl * n, n)])
        for v, w, n in ((src, src_all, SLOTS), (rel, rel_all, SLOTS), (dst, dst_all, SLOTS), (neg, neg_all, 8))
    ]
    twin = {"dom": sib["dom"], "rep": core}
    same = {"dom": lax.axis_index("dom"), "rep": core}
    cross = [prepared(v, w, es.at[i], eb.at[i, xl], twin) for i, (v, w) in enumerate(lists)]
    straight = [prepared(v, w, es.at[4 + i], ea.at[i], same) for i, (v, w) in enumerate(lists)]
    stay = [pltpu.make_async_copy(v, w, local.at[1 + i]) for i, (v, w) in enumerate(lists)]
    things = ((count_rows, count_use), (left, left_use), (right, right_use))
    tables = [prepared(v, w, ts.at[i], tr.at[i], sib) for i, (v, w) in enumerate(things)]
    stay += [pltpu.make_async_copy(v, w, local.at[5 + i]) for i, (v, w) in enumerate(things)]
    for copy in cross:
        copy.start()

    @pl.when(core == xl)
    def _():
        for copy in tables + stay:
            copy.start()

    @pl.when(core != xl)
    def _():
        for copy in straight:
            copy.start()

    own.wait()
    for copy in first:
        copy.wait()
    halves = [pl.ds(0, SHARD // 2), pl.ds(SHARD // 2, SHARD // 2)]
    down = []

    def below(ref):
        i = len(down)
        down.append(remote(ref, ref, cs.at[i], cr.at[i], sib))

    below(full.at[y, :, xh, core, xl])
    second = []
    for half, devs in enumerate((ydev, xdev)):
        part = full.at[y, :, xh, core, xl, halves[half]]
        for k in range(3):
            i = half * 3 + k
            second.append(remote(part, part, ps.at[i], pr.at[i], devs[k]))
    for i, copy in enumerate(second):
        copy.wait()
    third = []
    for half, devs in enumerate((xdev, ydev)):
        part = full.at[:, :, xh, core, xl, halves[0]] if half == 0 else full.at[y, :, :, core, :, halves[1]]
        for k in range(3):
            i = 6 + half * 3 + k
            third.append(remote(part, part, ps.at[i], pr.at[i], devs[k]))
    for k in range(1, 4):
        below(full.at[lax.rem(y + 4 - k, Y), :, xh, core, xl, halves[0]])
        a, b = shift_x(xh, xl, X - k)
        below(full.at[y, :, a, core, b, halves[1]])
    for k in range(1, 4):
        third[k - 1].wait()
        a, b = shift_x(xh, xl, X - k)
        below(full.at[:, :, a, core, b, halves[0]])
        third[2 + k].wait()
        below(full.at[lax.rem(y + 4 - k, Y), :, :, core, :, halves[1]])
    for copy in down:
        copy.wait()
    for copy in cross:
        copy.wait_send()

    @pl.when(core == xl)
    def _():
        for copy in tables:
            copy.wait_send()
        for copy in straight:
            copy.wait_recv()
        for copy in stay:
            copy.wait()

    @pl.when(core != xl)
    def _():
        for copy in tables:
            copy.wait_recv()
        for copy in straight:
            copy.wait_send()
        for i, (v, w) in enumerate(lists):
            for sender in range(2):
                prepared(v, w, es.at[i], eb.at[i, sender], twin).wait_recv()


def gather(shard, src, rel, dst, neg, count, left, right):
    dma = lambda *n: pltpu.SemaphoreType.DMA(n)
    shape = jax.ShapeDtypeStruct
    return pl.pallas_call(
        gather_kernel,
        out_shape=(
            shape((Y, Z, 2, 2, 2, SHARD, LANES), F32),
            shape((2 * SLOTS,), I32), shape((2 * SLOTS,), I32), shape((2 * SLOTS,), I32),
            shape((16, NEG), I32), shape((8, LANES), I32),
            shape((D, E_PART), F32), shape((D, E_PART), F32),
        ),
        in_specs=[VMEM] + [HBM] * 4 + [SMEM] + [HBM] * 2,
        out_specs=(HBM,) * 8,
        scratch_shapes=[
            pltpu.VMEM((SHARD, LANES), F32), pltpu.VMEM((8, LANES), I32),
            dma(7), dma(7), dma(12), dma(12), dma(13), dma(13),
            dma(8), dma(4), dma(4, 2), dma(3), dma(3), dma(8),
        ],
        compiler_params=pltpu.CompilerParams(collective_id=0, has_side_effects=True, vmem_limit_bytes=LIMIT),
        name="gather_relations",
    )(shard, src, rel, dst, neg, count, left, right)


def product(a, b, conjugate):
    if conjugate:
        re = lambda i, j: a[i] * b[i] + a[j] * b[j]
        im = lambda i, j: a[j] * b[i] - a[i] * b[j]
    else:
        re = lambda i, j: a[i] * b[i] - a[j] * b[j]
        im = lambda i, j: a[i] * b[j] + a[j] * b[i]
    return (re(0, 2), re(1, 3), im(0, 2), im(1, 3))


def embedding_tiles(ref, g):
    at = pl.ds(pl.multiple_of(g * LANES, LANES), LANES)
    zero = jnp.zeros((56, LANES), F32)
    full = lambda i: ref[pl.ds(i, LANES), at]
    part = lambda i: jnp.concatenate([ref[pl.ds(i, 72), at], zero], axis=0)
    return full(0), part(128), full(200), part(328)


def compute_kernel(
    parity, counted, src, rel, dst, neg, left_hbm, right_hbm, rels_hbm,
    left_hbm_grad, right_hbm_grad, rel_hbm_grad,
    left, right, rels, left_turned, right_turned, left_grad, right_grad, rel_grad,
    left_rows, right_rows, right_low, low_turned, heads, relat, tails, q_low, prob, neg_t, sems,
):
    count, core = counted[0, 0], parity[0]
    n_blocks = (((count + GROUP - 1) >> 9) + 1 - core) >> 1
    loads = [
        pltpu.make_async_copy(v, w, sems.at[i])
        for i, (v, w) in enumerate(((left_hbm, left), (right_hbm, right), (rels_hbm, rels)))
    ]
    for copy in loads:
        copy.start()
    left_grad[...] = jnp.zeros_like(left_grad)
    right_grad[...] = jnp.zeros_like(right_grad)
    rel_grad[...] = jnp.zeros_like(rel_grad)
    neg_t[...] = jnp.zeros_like(neg_t)
    loads[0].wait()
    loads[1].wait()

    def prepare(g, _):
        first = pl.multiple_of(g * LANES, LANES)
        for j, tile in enumerate(embedding_tiles(left, g)):
            left_rows[pl.ds(4 * first + j, LANES, stride=4), :] = tile.T
        for j, tile in enumerate(embedding_tiles(right, g)):
            low_turned[pl.ds(j * LANES, LANES), pl.ds(first, LANES)] = tile.astype(BF16)
            tile = tile.T
            right_rows[pl.ds(4 * first + j, LANES, stride=4), :] = tile
            right_low[pl.ds(first, LANES), pl.ds(j * LANES, LANES)] = tile.astype(BF16)
        return 0

    lax.fori_loop(0, E_PART // LANES, prepare, 0)
    loads[2].wait()
    unroll = 16

    def block(i, _):
        b = 2 * i + core

        def edges(i):
            at = b * GROUP + i * unroll
            for u in range(unroll):
                yield i * unroll + u, [
                    pl.ds(pl.multiple_of(4 * ids[at + u], 4), 4) for ids in (src, rel, dst)
                ]

        def fetch(i, _):
            for e, (s, r, t) in edges(i):
                to = pl.ds(pl.multiple_of(4 * e, 4), 4)
                heads[to, :] = left_rows[s, :]
                relat[to, :] = rels[r, :]
                tails[to, :] = right_rows[t, :]
            return 0

        lax.fori_loop(0, GROUP // unroll, fetch, 0)

        named = neg[pl.ds(b, 1), :]
        high = (lax.broadcasted_iota(I32, (16, NEG), 0) == (named >> 7)).astype(F32).astype(BF16)
        low = (lax.broadcasted_iota(I32, (LANES, NEG), 0) == (named & 127)).astype(F32).astype(BF16)
        table = lax.dot_general(high, low, (((1,), (1,)), ((), ())), preferred_element_type=F32)
        counts = jnp.concatenate([table[h : h + 1, :] for h in range(E_PART // LANES)], axis=1)
        bias = jnp.where(counts > 0, 0.0, -jnp.inf)

        for ch in range(GROUP // CHUNK):
            rows = pl.ds(ch * CHUNK, CHUNK)
            at = [pl.ds(4 * ch * CHUNK + j, CHUNK, stride=4) for j in range(4)]
            h = [heads[a, :] for a in at]
            r = [relat[a, :] for a in at]
            t = [tails[a, :] for a in at]
            q = product(h, r, False)
            positive = jnp.sum(q[0] * t[0] + q[1] * t[1] + q[2] * t[2] + q[3] * t[3], axis=1, keepdims=True)
            ql = jnp.concatenate([x.astype(BF16) for x in q], axis=1)
            q_low[rows, :] = ql
            scores = jnp.dot(ql, low_turned[...], preferred_element_type=F32) + bias
            slot = b * GROUP + ch * CHUNK + lax.broadcasted_iota(I32, (CHUNK, 1), 0)
            live = (slot < count).astype(F32)
            top = jnp.maximum(positive, jnp.max(scores, axis=1, keepdims=True))
            pos_exp = jnp.exp(positive - top)
            neg_exp = jnp.exp(scores - top)
            total = pos_exp + jnp.sum(neg_exp * counts, axis=1, keepdims=True)
            weight = live / total
            pos_coef = pos_exp * weight - live
            p = (neg_exp * weight).astype(BF16)
            prob[rows, :] = p
            many = p.astype(F32) * counts
            many_high = many.astype(BF16)
            many_low = (many - many_high.astype(F32)).astype(BF16)
            d = jnp.dot(many_high, right_low[...], preferred_element_type=F32) + jnp.dot(
                many_low, right_low[...], preferred_element_type=F32
            )
            dq = [d[:, j * LANES : (j + 1) * LANES] + pos_coef * t[j] for j in range(4)]
            for a, x, y, z in zip(at, product(dq, r, True), product(dq, h, True), q):
                heads[a, :] = x
                relat[a, :] = y
                tails[a, :] = pos_coef * z

        neg_t[...] += counts * lax.dot_general(
            q_low[...], prob[...], (((0,), (0,)), ((), ())), preferred_element_type=F32
        )

        def scatter(i, _):
            for e, (s, r, t) in edges(i):
                of = pl.ds(pl.multiple_of(4 * e, 4), 4)
                for to, grads, terms in ((s, left_grad, heads), (r, rel_grad, relat), (t, right_grad, tails)):
                    grads[to, :] += terms[of, :]
            return 0

        lax.fori_loop(0, GROUP // unroll, scatter, 0)
        return 0

    lax.fori_loop(0, n_blocks, block, 0)
    rel_out = pltpu.make_async_copy(rel_grad, rel_hbm_grad, sems.at[2])
    rel_out.start()

    def finish(g, _):
        first = pl.multiple_of(g * LANES, LANES)
        to = pl.ds(first, LANES)
        for j, (start, size) in enumerate(((0, 128), (128, 72), (200, 128), (328, 72))):
            at = pl.ds(4 * first + j, LANES, stride=4)
            left_turned[pl.ds(start, size), to] = left_grad[at, :].T[:size]
            right_turned[pl.ds(start, size), to] = (
                right_grad[at, :].T[:size] + neg_t[pl.ds(j * LANES, size), to]
            )
        return 0

    lax.fori_loop(0, E_PART // LANES, finish, 0)
    outs = [
        pltpu.make_async_copy(left_turned, left_hbm_grad, sems.at[0]),
        pltpu.make_async_copy(right_turned, right_hbm_grad, sems.at[1]),
    ]
    for copy in outs:
        copy.start()
    for copy in outs:
        copy.wait()
    rel_out.wait()


def compute(parity, counted, src, rel, dst, neg, left, right, rels):
    shape = jax.ShapeDtypeStruct
    n = rels.shape[0]
    table = pltpu.VMEM((D, E_PART), F32)
    rows = pltpu.VMEM((4 * E_PART, LANES), F32)
    block = pltpu.VMEM((4 * GROUP, LANES), F32)
    return pl.pallas_call(
        compute_kernel,
        out_shape=(shape((D, E_PART), F32), shape((D, E_PART), F32), shape((n, LANES), F32)),
        in_specs=[SMEM] * 5 + [VMEM] + [HBM] * 3,
        out_specs=(HBM,) * 3,
        scratch_shapes=[
            table, table, pltpu.VMEM((n, LANES), F32), table, table, rows, rows, pltpu.VMEM((n, LANES), F32),
            rows, rows,
            pltpu.VMEM((E_PART, 512), BF16), pltpu.VMEM((512, E_PART), BF16),
            block, block, block,
            pltpu.VMEM((GROUP, 512), BF16), pltpu.VMEM((GROUP, E_PART), BF16), pltpu.VMEM((512, E_PART), F32),
            pltpu.SemaphoreType.DMA((3,)),
        ],
        compiler_params=pltpu.CompilerParams(vmem_limit_bytes=LIMIT),
        cost_estimate=pl.CostEstimate(flops=20 * 10**9, bytes_accessed=10**8, transcendentals=10**6),
        name="blocks",
    )(parity, counted, src, rel, dst, neg, left, right, rels)


def exchange_kernel(
    left_grad, right_grad, rel_grad,
    left_sum, right_sum, rel_mine,
    left_own, left_sib, right_own, right_sib, acc, from_core, big0, big1, small0, small1, from_x,
    ls, lr, ss, sr, cs, cr, ps, pr, zs, zr, xs, xr, local,
):
    y, z, xh, core, xl = place()
    sib, xdev, ydev, zdev = neighbours()
    _, partner, diagonal = family()
    dom = lax.axis_index("dom")
    n_dom = 4 * Y * Z
    pair = dom - core
    barrier = pltpu.get_barrier_semaphore()
    peers = [sib, partner, diagonal] + xdev + ydev + zdev
    for peer in peers:
        pl.semaphore_signal(barrier, inc=1, device_id=peer, device_id_type=MESH)

    @pl.when(core == 0)
    def _():
        for k in (2, 1):
            behind = {"dom": lax.rem(dom + n_dom - k, n_dom), "rep": 1}
            pl.semaphore_signal(barrier, inc=1, device_id=behind, device_id_type=MESH)

    pl.semaphore_wait(barrier, len(peers) + 2 * xl)

    half = D // 2
    mine, other = pl.ds(core * half, half), pl.ds((1 - core) * half, half)
    pairs = []
    for i, (grad, own, recv) in enumerate(((left_grad, left_own, left_sib), (right_grad, right_own, right_sib))):
        keep = pltpu.make_async_copy(grad.at[mine], own, local.at[i])
        keep.start()
        pairs.append((remote(grad.at[other], recv, ss.at[i], sr.at[i], sib), keep))
    down = remote(rel_grad.at[:, :, :, 1 - core], from_core, cs, cr, sib)
    keep_rel = pltpu.make_async_copy(rel_grad.at[:, :, :, core], acc, local.at[2])
    keep_rel.start()

    left_to = pair + xl
    right_to = lax.rem(pair + xl + 1, n_dom)
    sends, stays = [], []
    for i, (own, recv, out, to) in enumerate(
        ((left_own, left_sib, left_sum, left_to), (right_own, right_sib, right_sum, right_to))
    ):
        for copy in pairs[i]:
            copy.wait()

        def add(j, _):
            at = pl.ds(pl.multiple_of(8 * j, 8), 8)
            own[at, :] += recv[at, :]
            return 0

        lax.fori_loop(0, half // 8, add, 0)
        part = out.at[mine]
        far = prepared(own, part, ls.at[i, 0], lr.at[i, core, 0], {"dom": to, "rep": 1 - xl})
        near = prepared(own, part, ls.at[i, 1], lr.at[i, core, 1], {"dom": to, "rep": xl})
        stay = pltpu.make_async_copy(own, part, local.at[3 + i])
        far.start()
        self_too = to == dom

        @pl.when(self_too)
        def _():
            stay.start()

        @pl.when(jnp.logical_not(self_too))
        def _():
            near.start()

        sends.append((far, near, stay, self_too))

    keep_rel.wait()
    down.wait()

    def add_core(i, _):
        acc[i // Z, lax.rem(i, Z)] += from_core[i // Z, lax.rem(i, Z)]
        return 0

    lax.fori_loop(0, Y * Z, add_core, 0)

    cut = [pl.ds(0, MAJOR), pl.ds(MAJOR, SHARD - MAJOR)]
    one = []
    for k in range(1, Y):
        t = lax.rem(y + k, Y)
        one.append(remote(acc.at[t, :, :, :, cut[0]], big0.at[k - 1], ps.at[k - 1], pr.at[k - 1], ydev[k - 1]))
    for k in range(1, Z):
        t = lax.rem(z + k, Z)
        one.append(remote(acc.at[:, t, :, :, cut[1]], big1.at[k - 1], zs.at[k - 1], zr.at[k - 1], zdev[k - 1]))
    for copy in one:
        copy.wait()

    def add_y(i, _):
        acc[y, i, :, :, cut[0]] += big0[0, i] + big0[1, i] + big0[2, i]
        return 0

    lax.fori_loop(0, Z, add_y, 0)

    def add_z(i, _):
        total = acc[i, z, :, :, cut[1]]
        for k in range(Z - 1):
            total = total + big1[k, i]
        acc[i, z, :, :, cut[1]] = total
        return 0

    lax.fori_loop(0, Y, add_z, 0)
    two = []
    for k in range(1, Z):
        t = lax.rem(z + k, Z)
        two.append(remote(acc.at[y, t, :, :, cut[0]], small0.at[k - 1], zs.at[6 + k], zr.at[6 + k], zdev[k - 1]))
    for k in range(1, Y):
        t = lax.rem(y + k, Y)
        two.append(remote(acc.at[t, z, :, :, cut[1]], small1.at[k - 1], ps.at[2 + k], pr.at[2 + k], ydev[k - 1]))
    for copy in two:
        copy.wait()
    total = acc[y, z, :, :, cut[0]]
    for k in range(Z - 1):
        total = total + small0[k]
    acc[y, z, :, :, cut[0]] = total
    acc[y, z, :, :, cut[1]] += small1[0] + small1[1] + small1[2]
    three = []
    for k in range(1, X):
        a, b = shift_x(xh, xl, k)
        three.append(remote(acc.at[y, z, a, b], from_x.at[k - 1], xs.at[k - 1], xr.at[k - 1], xdev[k - 1]))
    for copy in three:
        copy.wait()
    rel_mine[...] = acc[y, z, xh, xl] + from_x[0] + from_x[1] + from_x[2]

    for far, near, stay, self_too in sends:
        far.wait_send()

        @pl.when(self_too)
        def _():
            stay.wait()

        @pl.when(jnp.logical_not(self_too))
        def _():
            near.wait_send()

    for i, owner in ((0, core), (1, 1 - core)):
        own, out = ((left_own, left_sum), (right_own, right_sum))[i]
        for sender in range(2):
            part = out.at[pl.ds(sender * half, half)]
            local_chip = owner == xl
            to_self = jnp.logical_and(local_chip, jnp.logical_and(sender == core, jnp.logical_or(i == 0, core == 1)))
            came = lambda kind: prepared(own, part, ls.at[i, 0], lr.at[i, sender, kind], sib)

            @pl.when(jnp.logical_not(local_chip))
            def _():
                came(0).wait_recv()

            @pl.when(jnp.logical_and(local_chip, jnp.logical_not(to_self)))
            def _():
                came(1).wait_recv()


def exchange(left_grad, right_grad, rel_grad):
    dma = lambda *n: pltpu.SemaphoreType.DMA(n)
    shape = jax.ShapeDtypeStruct
    table = shape((D, E_PART), F32)
    half = pltpu.VMEM((D // 2, E_PART), F32)
    minor = SHARD - MAJOR
    return pl.pallas_call(
        exchange_kernel,
        out_shape=(table, table, shape((SHARD, LANES), F32)),
        in_specs=[HBM] * 3,
        out_specs=(HBM, HBM, VMEM),
        scratch_shapes=[half] * 4
        + [
            pltpu.VMEM((Y, Z, 2, 2, SHARD, LANES), F32),
            pltpu.VMEM((Y, Z, 2, 2, SHARD, LANES), F32),
            pltpu.VMEM((Y - 1, Z, 2, 2, MAJOR, LANES), F32),
            pltpu.VMEM((Z - 1, Y, 2, 2, minor, LANES), F32),
            pltpu.VMEM((Z - 1, 2, 2, MAJOR, LANES), F32),
            pltpu.VMEM((Y - 1, 2, 2, minor, LANES), F32),
            pltpu.VMEM((X - 1, SHARD, LANES), F32),
            dma(2, 2), dma(2, 2, 2), dma(2), dma(2),
            pltpu.SemaphoreType.DMA, pltpu.SemaphoreType.DMA,
            dma(6), dma(6), dma(14), dma(14), dma(3), dma(3), dma(5),
        ],
        compiler_params=pltpu.CompilerParams(collective_id=1, has_side_effects=True, vmem_limit_bytes=LIMIT),
        name="exchange_gradients",
    )(left_grad, right_grad, rel_grad)


def update_kernel(
    left, left_state, left_sum, right, right_state, right_sum, rel, rel_state, rel_grad,
    left_next, left_state_next, right_next, right_state_next, rel_next, rel_state_next,
):
    for table, state, total, after, state_after in (
        (left, left_state, left_sum, left_next, left_state_next),
        (right, right_state, right_sum, right_next, right_state_next),
    ):
        grad = total[...]
        fresh = state[...] + jnp.sum(grad * grad, axis=0, keepdims=True) * (1.0 / D)
        state_after[...] = fresh
        after[...] = table[...] - grad * (RATE / jnp.sqrt(fresh))

    @pl.when(pl.program_id(0) == 0)
    def _():
        n = rel.shape[0]
        same = lax.broadcasted_iota(I32, (n, n), 0) == lax.broadcasted_iota(I32, (n, n), 1)
        column = lambda row: jnp.sum(jnp.where(same, jnp.broadcast_to(row, (n, n)), 0.0), axis=1, keepdims=True)
        across = lambda col: jnp.sum(jnp.where(same, jnp.broadcast_to(col, (n, n)), 0.0), axis=0, keepdims=True)
        grad = [rel_grad[pl.ds(j, n, stride=4), :] for j in range(4)]
        square = jnp.sum(sum(v * v for v in grad), axis=1, keepdims=True) * (1.0 / D)
        fresh = column(rel_state[...]) + square
        rel_state_next[...] = across(fresh)
        scale = RATE / jnp.sqrt(fresh)
        for j, change in enumerate(natural_of([v * scale for v in grad])):
            cols = pl.ds(j * LANES, change.shape[1])
            rel_next[:, cols] = rel[:, cols] - change


def update(left, left_state, left_sum, right, right_state, right_sum, rel, rel_state, rel_grad):
    wide = 2 * LANES
    table = pl.BlockSpec((D, wide), lambda g: (0, g))
    state = pl.BlockSpec((1, wide), lambda g: (0, g))
    whole = lambda shape: pl.BlockSpec(shape, lambda g: (0, 0))
    shape = jax.ShapeDtypeStruct
    big, row = shape((D, E_PART), F32), shape((1, E_PART), F32)
    return pl.pallas_call(
        update_kernel,
        grid=(E_PART // wide,),
        out_shape=(big, row, big, row, shape(rel.shape, F32), shape(rel_state.shape, F32)),
        in_specs=[table, state, table] * 2 + [whole(rel.shape), whole(rel_state.shape), whole((SHARD, LANES))],
        out_specs=(table, state, table, state, whole(rel.shape), whole(rel_state.shape)),
        compiler_params=pltpu.CompilerParams(vmem_limit_bytes=LIMIT),
        name="adagrad",
    )(left, left_state, left_sum, right, right_state, right_sum, rel, rel_state, rel_grad)


def shards(
    left_table, left_state, right_table, right_state, rel_table, rel_state,
    sources, relations, targets, bucket_counts, negatives,
):
    left, right = left_table.T, right_table.T
    rels, src, rel, dst, neg, counted, left_use, right_use = gather(
        rel_table, sources, relations, targets, negatives, bucket_counts, left, right
    )
    n_dom = 4 * Y * Z
    route = [((i - 1) % n_dom, i) for i in range(n_dom)]
    held, held_state, rels = lax.optimization_barrier((right_table, right_state, rels))
    held = lax.ppermute(held, "dom", route)
    held_state = lax.ppermute(held_state, "dom", route)
    parity = lax.rem(lax.axis_index("dom"), 2).reshape(1)
    left_grad, right_grad, rel_grad = compute(
        parity, counted, src, rel, dst, neg, left_use, right_use, rels.reshape(-1, LANES)
    )
    left_sum, right_sum, rel_mine = exchange(
        left_grad, right_grad, rel_grad.reshape(Y, Z, 2, 2, 2, SHARD, LANES)
    )
    left_next, left_after, right_next, right_after, rel_next, rel_after = update(
        left, left_state[None], left_sum, held.T, held_state[None], right_sum, rel_table, rel_state[None], rel_mine
    )
    return left_next.T, left_after[0], right_next.T, right_after[0], rel_next, rel_after[0]


def solution(mesh):
    both = P(("dom", "rep"))
    rows = P(("dom", "rep"), None)
    table, state = P("dom", None), P("dom")
    return jax.shard_map(
        shards,
        mesh=mesh,
        in_specs=(table, state, table, state, rows, both, both, both, both, state, rows),
        out_specs=(table, state, table, state, rows, both),
        check_vma=False,
    )
```

```python
import jax
import jax.numpy as jnp
from jax import lax
from jax.experimental import pallas as pl
from jax.experimental.pallas import tpu as pltpu
from jax.sharding import PartitionSpec as P

RATE = 0.3
D, LANES = 400, 128
E_PART, GROUP, NEG = 1024, 512, 1024
CHUNK = 128
Y, Z, X = 4, 8, 4
SHARD = 48
SLOTS = 4096
F32, BF16, I32 = jnp.float32, jnp.bfloat16, jnp.int32
MESH = pl.DeviceIdType.MESH
VMEM = pl.BlockSpec(memory_space=pltpu.VMEM)
SMEM = pl.BlockSpec(memory_space=pltpu.SMEM)
HBM = pl.BlockSpec(memory_space=pltpu.HBM)
LIMIT = 60 * 2**20


def tiles_of(ref, first, n):
    rows = pl.ds(first, n)
    lane = lax.broadcasted_iota(I32, (n, LANES), 1)
    a, b, c = (ref[rows, pl.ds(j * LANES, LANES)] for j in range(3))
    d = jnp.concatenate([ref[rows, pl.ds(384, 16)], jnp.zeros((n, LANES - 16), F32)], axis=1)
    b1, c1, d1 = (pltpu.roll(v, 56, 1) for v in (b, c, d))
    zero = jnp.zeros((n, LANES), F32)
    return (
        a,
        jnp.where(lane < 72, b, zero),
        jnp.where(lane < 56, b1, c1),
        jnp.where(lane < 56, c1, jnp.where(lane < 72, d1, zero)),
    )


def natural_of(tiles):
    a, b, c, d = tiles
    lane = lax.broadcasted_iota(I32, a.shape, 1)
    c1, d1 = (pltpu.roll(v, 72, 1) for v in (c, d))
    return (a, jnp.where(lane < 72, b, c1), jnp.where(lane < 72, c1, d1), d1[:, :16])


def place():
    dom, xl = lax.axis_index("dom"), lax.axis_index("rep")
    core = lax.rem(dom, 2)
    xh = lax.rem(dom // 2, 2)
    z = lax.rem(dom // 4, Z)
    y = dom // (4 * Z)
    return y, z, xh, core, xl


def device(y, z, xh, core, xl):
    return {"dom": ((y * Z + z) * 2 + xh) * 2 + core, "rep": xl}


def shift_x(xh, xl, k):
    x = lax.rem(xh * 2 + xl + k, X)
    return x // 2, lax.rem(x, 2)


def greet(peers):
    barrier = pltpu.get_barrier_semaphore()
    for peer in peers:
        pl.semaphore_signal(barrier, inc=1, device_id=peer, device_id_type=MESH)
    pl.semaphore_wait(barrier, len(peers))


def neighbours():
    y, z, xh, core, xl = place()
    sib = device(y, z, xh, 1 - core, xl)
    xs = [(*shift_x(xh, xl, k),) for k in range(1, X)]
    xdev = [device(y, z, a, core, b) for a, b in xs]
    ydev = [device(lax.rem(y + k, Y), z, xh, core, xl) for k in range(1, Y)]
    zdev = [device(y, lax.rem(z + k, Z), xh, core, xl) for k in range(1, Z)]
    return sib, xdev, ydev, zdev


def remote(src, dst, send, recv, to):
    copy = pltpu.make_async_remote_copy(
        src_ref=src, dst_ref=dst, send_sem=send, recv_sem=recv, device_id=to, device_id_type=MESH
    )
    copy.start()
    return copy


def family():
    y, z, xh, core, xl = place()
    dom = lax.axis_index("dom")
    twin = dom + 1 - 2 * core
    return {"dom": twin, "rep": xl}, {"dom": dom, "rep": 1 - xl}, {"dom": twin, "rep": 1 - xl}


def prepared(src, dst, send, recv, to):
    return pltpu.make_async_remote_copy(
        src_ref=src, dst_ref=dst, send_sem=send, recv_sem=recv, device_id=to, device_id_type=MESH
    )


def gather_kernel(
    shard, src, rel, dst, neg, count, left, right,
    full, src_all, rel_all, dst_all, neg_all, count_use, left_use, right_use,
    rows, count_rows, zs, zr, ps, pr, cs, cr, es, ea, eb, ts, tr, local,
):
    y, z, xh, core, xl = place()
    sib, xdev, ydev, zdev = neighbours()
    _, partner, diagonal = family()
    greet([sib, partner, diagonal] + xdev + ydev + zdev)
    for j, tile in enumerate(tiles_of(shard, 0, 12)):
        rows[pl.ds(j, 12, stride=4), :] = tile
    first = [remote(rows, full.at[y, z, xh, core, xl], zs.at[k], zr.at[k], zdev[k]) for k in range(Z - 1)]
    own = pltpu.make_async_copy(rows, full.at[y, z, xh, core, xl], local.at[0])
    own.start()
    count_rows[...] = jnp.full((8, LANES), count[0], I32)

    lists = [
        (v, w.at[pl.ds(xl * n, n)])
        for v, w, n in ((src, src_all, SLOTS), (rel, rel_all, SLOTS), (dst, dst_all, SLOTS), (neg, neg_all, 8))
    ]
    twin = {"dom": sib["dom"], "rep": core}
    same = {"dom": lax.axis_index("dom"), "rep": core}
    cross = [prepared(v, w, es.at[i], eb.at[i, xl], twin) for i, (v, w) in enumerate(lists)]
    straight = [prepared(v, w, es.at[4 + i], ea.at[i], same) for i, (v, w) in enumerate(lists)]
    stay = [pltpu.make_async_copy(v, w, local.at[1 + i]) for i, (v, w) in enumerate(lists)]
    things = ((count_rows, count_use), (left, left_use), (right, right_use))
    tables = [prepared(v, w, ts.at[i], tr.at[i], sib) for i, (v, w) in enumerate(things)]
    stay.append(pltpu.make_async_copy(count_rows, count_use, local.at[5]))
    for copy in cross:
        copy.start()

    @pl.when(core == xl)
    def _():
        for copy in tables + stay:
            copy.start()

    @pl.when(core != xl)
    def _():
        for copy in straight:
            copy.start()

    own.wait()
    for copy in first:
        copy.wait()
    halves = [pl.ds(0, SHARD // 2), pl.ds(SHARD // 2, SHARD // 2)]
    down = []

    def below(ref):
        i = len(down)
        down.append(remote(ref, ref, cs.at[i], cr.at[i], sib))

    below(full.at[y, :, xh, core, xl])
    second = []
    for half, devs in enumerate((ydev, xdev)):
        part = full.at[y, :, xh, core, xl, halves[half]]
        for k in range(3):
            i = half * 3 + k
            second.append(remote(part, part, ps.at[i], pr.at[i], devs[k]))
    for i, copy in enumerate(second):
        copy.wait()
    third = []
    for half, devs in enumerate((xdev, ydev)):
        part = full.at[:, :, xh, core, xl, halves[0]] if half == 0 else full.at[y, :, :, core, :, halves[1]]
        for k in range(3):
            i = 6 + half * 3 + k
            third.append(remote(part, part, ps.at[i], pr.at[i], devs[k]))
    for k in range(1, 4):
        below(full.at[lax.rem(y + 4 - k, Y), :, xh, core, xl, halves[0]])
        a, b = shift_x(xh, xl, X - k)
        below(full.at[y, :, a, core, b, halves[1]])
    for k in range(1, 4):
        third[k - 1].wait()
        a, b = shift_x(xh, xl, X - k)
        below(full.at[:, :, a, core, b, halves[0]])
        third[2 + k].wait()
        below(full.at[lax.rem(y + 4 - k, Y), :, :, core, :, halves[1]])
    for copy in down:
        copy.wait()
    for copy in cross:
        copy.wait_send()

    @pl.when(core == xl)
    def _():
        for copy in tables:
            copy.wait_send()
        for copy in straight:
            copy.wait_recv()
        for copy in stay:
            copy.wait()

    @pl.when(core != xl)
    def _():
        for copy in tables:
            copy.wait_recv()
        for copy in straight:
            copy.wait_send()
        for i, (v, w) in enumerate(lists):
            for sender in range(2):
                prepared(v, w, es.at[i], eb.at[i, sender], twin).wait_recv()


def gather(shard, src, rel, dst, neg, count, left, right):
    dma = lambda *n: pltpu.SemaphoreType.DMA(n)
    shape = jax.ShapeDtypeStruct
    return pl.pallas_call(
        gather_kernel,
        out_shape=(
            shape((Y, Z, 2, 2, 2, SHARD, LANES), F32),
            shape((2 * SLOTS,), I32), shape((2 * SLOTS,), I32), shape((2 * SLOTS,), I32),
            shape((16, NEG), I32), shape((8, LANES), I32),
            shape((D, E_PART), F32), shape((D, E_PART), F32),
        ),
        in_specs=[VMEM] + [HBM] * 4 + [SMEM] + [HBM] * 2,
        out_specs=(HBM,) * 8,
        scratch_shapes=[
            pltpu.VMEM((SHARD, LANES), F32), pltpu.VMEM((8, LANES), I32),
            dma(7), dma(7), dma(12), dma(12), dma(13), dma(13),
            dma(8), dma(4), dma(4, 2), dma(3), dma(3), dma(6),
        ],
        compiler_params=pltpu.CompilerParams(collective_id=0, has_side_effects=True, vmem_limit_bytes=LIMIT),
        name="gather_relations",
    )(shard, src, rel, dst, neg, count, left, right)


def product(a, b, conjugate):
    if conjugate:
        re = lambda i, j: a[i] * b[i] + a[j] * b[j]
        im = lambda i, j: a[j] * b[i] - a[i] * b[j]
    else:
        re = lambda i, j: a[i] * b[i] - a[j] * b[j]
        im = lambda i, j: a[i] * b[j] + a[j] * b[i]
    return (re(0, 2), re(1, 3), im(0, 2), im(1, 3))


def embedding_tiles(ref, g):
    at = pl.ds(pl.multiple_of(g * LANES, LANES), LANES)
    zero = jnp.zeros((56, LANES), F32)
    full = lambda i: ref[pl.ds(i, LANES), at]
    part = lambda i: jnp.concatenate([ref[pl.ds(i, 72), at], zero], axis=0)
    return full(0), part(128), full(200), part(328)


def compute_kernel(
    spot, counted, src, rel, dst, neg, left_here, right_here, left_sent, right_sent, rels_hbm,
    left_hbm_grad, right_hbm_grad, rel_hbm_grad,
    left, right, rels, left_turned, right_turned, left_grad, right_grad, rel_grad,
    left_rows, right_rows, right_low, low_turned, heads, relat, tails, q_low, prob, neg_t, sems,
):
    count, core, at_home = counted[0, 0], spot[0], spot[1]
    n_blocks = (((count + GROUP - 1) >> 9) + 1 - core) >> 1
    tables = ((left_here, left_sent, left), (right_here, right_sent, right))
    loads = [pltpu.make_async_copy(v, w, sems.at[i]) for i, (v, _, w) in enumerate(tables)]
    loads.append(pltpu.make_async_copy(rels_hbm, rels, sems.at[2]))

    @pl.when(at_home == 1)
    def _():
        for copy in loads[:2]:
            copy.start()

    @pl.when(at_home == 0)
    def _():
        for i, (_, v, w) in enumerate(tables):
            pltpu.make_async_copy(v, w, sems.at[i]).start()

    loads[2].start()
    left_grad[...] = jnp.zeros_like(left_grad)
    right_grad[...] = jnp.zeros_like(right_grad)
    rel_grad[...] = jnp.zeros_like(rel_grad)
    neg_t[...] = jnp.zeros_like(neg_t)
    loads[0].wait()
    loads[1].wait()

    def prepare(g, _):
        first = pl.multiple_of(g * LANES, LANES)
        for j, tile in enumerate(embedding_tiles(left, g)):
            left_rows[pl.ds(4 * first + j, LANES, stride=4), :] = tile.T
        for j, tile in enumerate(embedding_tiles(right, g)):
            low_turned[pl.ds(j * LANES, LANES), pl.ds(first, LANES)] = tile.astype(BF16)
            tile = tile.T
            right_rows[pl.ds(4 * first + j, LANES, stride=4), :] = tile
            right_low[pl.ds(first, LANES), pl.ds(j * LANES, LANES)] = tile.astype(BF16)
        return 0

    lax.fori_loop(0, E_PART // LANES, prepare, 0)
    loads[2].wait()
    unroll = 16

    def block(i, _):
        b = 2 * i + core

        def edges(i):
            at = b * GROUP + i * unroll
            for u in range(unroll):
                yield i * unroll + u, [
                    pl.ds(pl.multiple_of(4 * ids[at + u], 4), 4) for ids in (src, rel, dst)
                ]

        def fetch(i, _):
            for e, (s, r, t) in edges(i):
                to = pl.ds(pl.multiple_of(4 * e, 4), 4)
                heads[to, :] = left_rows[s, :]
                relat[to, :] = rels[r, :]
                tails[to, :] = right_rows[t, :]
            return 0

        lax.fori_loop(0, GROUP // unroll, fetch, 0)

        named = neg[pl.ds(b, 1), :]
        high = (lax.broadcasted_iota(I32, (16, NEG), 0) == (named >> 7)).astype(F32).astype(BF16)
        low = (lax.broadcasted_iota(I32, (LANES, NEG), 0) == (named & 127)).astype(F32).astype(BF16)
        table = lax.dot_general(high, low, (((1,), (1,)), ((), ())), preferred_element_type=F32)
        counts = jnp.concatenate([table[h : h + 1, :] for h in range(E_PART // LANES)], axis=1)
        bias = jnp.where(counts > 0, 0.0, -jnp.inf)

        for ch in range(GROUP // CHUNK):
            rows = pl.ds(ch * CHUNK, CHUNK)
            at = [pl.ds(4 * ch * CHUNK + j, CHUNK, stride=4) for j in range(4)]
            h = [heads[a, :] for a in at]
            r = [relat[a, :] for a in at]
            t = [tails[a, :] for a in at]
            q = product(h, r, False)
            positive = jnp.sum(q[0] * t[0] + q[1] * t[1] + q[2] * t[2] + q[3] * t[3], axis=1, keepdims=True)
            ql = jnp.concatenate([x.astype(BF16) for x in q], axis=1)
            q_low[rows, :] = ql
            scores = jnp.dot(ql, low_turned[...], preferred_element_type=F32) + bias
            slot = b * GROUP + ch * CHUNK + lax.broadcasted_iota(I32, (CHUNK, 1), 0)
            live = (slot < count).astype(F32)
            top = jnp.maximum(positive, jnp.max(scores, axis=1, keepdims=True))
            pos_exp = jnp.exp(positive - top)
            neg_exp = jnp.exp(scores - top)
            total = pos_exp + jnp.sum(neg_exp * counts, axis=1, keepdims=True)
            weight = live / total
            pos_coef = pos_exp * weight - live
            p = (neg_exp * weight).astype(BF16)
            prob[rows, :] = p
            many = p.astype(F32) * counts
            many_high = many.astype(BF16)
            many_low = (many - many_high.astype(F32)).astype(BF16)
            d = jnp.dot(many_high, right_low[...], preferred_element_type=F32) + jnp.dot(
                many_low, right_low[...], preferred_element_type=F32
            )
            dq = [d[:, j * LANES : (j + 1) * LANES] + pos_coef * t[j] for j in range(4)]
            for a, x, y, z in zip(at, product(dq, r, True), product(dq, h, True), q):
                heads[a, :] = x
                relat[a, :] = y
                tails[a, :] = pos_coef * z

        neg_t[...] += counts * lax.dot_general(
            q_low[...], prob[...], (((0,), (0,)), ((), ())), preferred_element_type=F32
        )

        def scatter(i, _):
            for e, (s, r, t) in edges(i):
                of = pl.ds(pl.multiple_of(4 * e, 4), 4)
                for to, grads, terms in ((s, left_grad, heads), (r, rel_grad, relat), (t, right_grad, tails)):
                    grads[to, :] += terms[of, :]
            return 0

        lax.fori_loop(0, GROUP // unroll, scatter, 0)
        return 0

    lax.fori_loop(0, n_blocks, block, 0)
    rel_out = pltpu.make_async_copy(rel_grad, rel_hbm_grad, sems.at[2])
    rel_out.start()

    def finish(g, _):
        first = pl.multiple_of(g * LANES, LANES)
        to = pl.ds(first, LANES)
        for j, (start, size) in enumerate(((0, 128), (128, 72), (200, 128), (328, 72))):
            at = pl.ds(4 * first + j, LANES, stride=4)
            left_turned[pl.ds(start, size), to] = left_grad[at, :].T[:size]
            right_turned[pl.ds(start, size), to] = (
                right_grad[at, :].T[:size] + neg_t[pl.ds(j * LANES, size), to]
            )
        return 0

    lax.fori_loop(0, E_PART // LANES, finish, 0)
    outs = [
        pltpu.make_async_copy(left_turned, left_hbm_grad, sems.at[0]),
        pltpu.make_async_copy(right_turned, right_hbm_grad, sems.at[1]),
    ]
    for copy in outs:
        copy.start()
    for copy in outs:
        copy.wait()
    rel_out.wait()


def compute(spot, counted, src, rel, dst, neg, left, right, left_sent, right_sent, rels):
    shape = jax.ShapeDtypeStruct
    n = rels.shape[0]
    table = pltpu.VMEM((D, E_PART), F32)
    rows = pltpu.VMEM((4 * E_PART, LANES), F32)
    block = pltpu.VMEM((4 * GROUP, LANES), F32)
    return pl.pallas_call(
        compute_kernel,
        out_shape=(shape((D, E_PART), F32), shape((D, E_PART), F32), shape((n, LANES), F32)),
        in_specs=[SMEM] * 5 + [VMEM] + [HBM] * 5,
        out_specs=(HBM,) * 3,
        scratch_shapes=[
            table, table, pltpu.VMEM((n, LANES), F32), table, table, rows, rows, pltpu.VMEM((n, LANES), F32),
            rows, rows,
            pltpu.VMEM((E_PART, 512), BF16), pltpu.VMEM((512, E_PART), BF16),
            block, block, block,
            pltpu.VMEM((GROUP, 512), BF16), pltpu.VMEM((GROUP, E_PART), BF16), pltpu.VMEM((512, E_PART), F32),
            pltpu.SemaphoreType.DMA((3,)),
        ],
        compiler_params=pltpu.CompilerParams(vmem_limit_bytes=LIMIT),
        cost_estimate=pl.CostEstimate(flops=20 * 10**9, bytes_accessed=10**8, transcendentals=10**6),
        name="blocks",
    )(spot, counted, src, rel, dst, neg, left, right, left_sent, right_sent, rels)


def exchange_kernel(
    left_grad, right_grad, rel_grad,
    left_sum, right_sum, rel_mine,
    left_own, left_sib, right_own, right_sib, acc, from_core, from_y, from_x, from_z,
    ls, lr, ss, sr, cs, cr, ys, yr, xs, xr, zs, zr, local,
):
    y, z, xh, core, xl = place()
    sib, xdev, ydev, zdev = neighbours()
    _, partner, diagonal = family()
    dom = lax.axis_index("dom")
    n_dom = 4 * Y * Z
    pair = dom - core
    barrier = pltpu.get_barrier_semaphore()
    peers = [sib, partner, diagonal] + xdev + ydev + zdev
    for peer in peers:
        pl.semaphore_signal(barrier, inc=1, device_id=peer, device_id_type=MESH)

    @pl.when(core == 0)
    def _():
        for k in (2, 1):
            behind = {"dom": lax.rem(dom + n_dom - k, n_dom), "rep": 1}
            pl.semaphore_signal(barrier, inc=1, device_id=behind, device_id_type=MESH)

    pl.semaphore_wait(barrier, len(peers) + 2 * xl)

    half = D // 2
    mine, other = pl.ds(core * half, half), pl.ds((1 - core) * half, half)
    pairs = []
    for i, (grad, own, recv) in enumerate(((left_grad, left_own, left_sib), (right_grad, right_own, right_sib))):
        keep = pltpu.make_async_copy(grad.at[mine], own, local.at[i])
        keep.start()
        pairs.append((remote(grad.at[other], recv, ss.at[i], sr.at[i], sib), keep))
    cut = [pl.ds(0, SHARD // 2), pl.ds(SHARD // 2, SHARD // 2)]
    down = [
        remote(rel_grad.at[:, :, :, 1 - core, :, c], from_core.at[:, :, :, :, c], cs.at[i], cr.at[i], sib)
        for i, c in enumerate(cut)
    ]
    keep_rel = pltpu.make_async_copy(rel_grad.at[:, :, :, core], acc, local.at[2])
    keep_rel.start()

    left_to = pair + xl
    right_to = lax.rem(pair + xl + 1, n_dom)
    sends, stays = [], []
    for i, (own, recv, out, to) in enumerate(
        ((left_own, left_sib, left_sum, left_to), (right_own, right_sib, right_sum, right_to))
    ):
        for copy in pairs[i]:
            copy.wait()

        def add(j, _):
            at = pl.ds(pl.multiple_of(8 * j, 8), 8)
            own[at, :] += recv[at, :]
            return 0

        lax.fori_loop(0, half // 8, add, 0)
        part = out.at[mine]
        far = prepared(own, part, ls.at[i, 0], lr.at[i, core, 0], {"dom": to, "rep": 1 - xl})
        near = prepared(own, part, ls.at[i, 1], lr.at[i, core, 1], {"dom": to, "rep": xl})
        stay = pltpu.make_async_copy(own, part, local.at[3 + i])
        far.start()
        self_too = to == dom

        @pl.when(self_too)
        def _():
            stay.start()

        @pl.when(jnp.logical_not(self_too))
        def _():
            near.start()

        sends.append((far, near, stay, self_too))

    keep_rel.wait()
    by_y, by_x, by_z = [], [], []
    for i, c in enumerate(cut):
        down[i].wait()

        def add_core(n, _):
            at = (n // Z, lax.rem(n, Z), slice(None), slice(None), c)
            acc[at] += from_core[at]
            return 0

        lax.fori_loop(0, Y * Z, add_core, 0)
        by_y.append([])
        for k in range(1, Y):
            t, n = lax.rem(y + k, Y), 3 * i + k - 1
            by_y[i].append(remote(acc.at[t, :, :, :, c], from_y.at[n], ys.at[n], yr.at[n], ydev[k - 1]))
    for i, c in enumerate(cut):
        for copy in by_y[i]:
            copy.wait()

        def add_y(n, _):
            acc[y, n, :, :, c] += from_y[3 * i, n] + from_y[3 * i + 1, n] + from_y[3 * i + 2, n]
            return 0

        lax.fori_loop(0, Z, add_y, 0)
        by_x.append([])
        for k in range(1, X):
            (a, b), n = shift_x(xh, xl, k), 3 * i + k - 1
            by_x[i].append(remote(acc.at[y, :, a, b, c], from_x.at[n], xs.at[n], xr.at[n], xdev[k - 1]))
    for i, c in enumerate(cut):
        for copy in by_x[i]:
            copy.wait()

        def add_x(n, _):
            acc[y, n, xh, xl, c] += from_x[3 * i, n] + from_x[3 * i + 1, n] + from_x[3 * i + 2, n]
            return 0

        lax.fori_loop(0, Z, add_x, 0)
        by_z.append([])
        for k in range(1, Z):
            t, n = lax.rem(z + k, Z), 7 * i + k - 1
            by_z[i].append(remote(acc.at[y, t, xh, xl, c], from_z.at[n], zs.at[n], zr.at[n], zdev[k - 1]))
    for i, c in enumerate(cut):
        for copy in by_z[i]:
            copy.wait()
        total = acc[y, z, xh, xl, c]
        for k in range(Z - 1):
            total = total + from_z[7 * i + k]
        rel_mine[c, :] = total

    for far, near, stay, self_too in sends:
        far.wait_send()

        @pl.when(self_too)
        def _():
            stay.wait()

        @pl.when(jnp.logical_not(self_too))
        def _():
            near.wait_send()

    for i, owner in ((0, core), (1, 1 - core)):
        own, out = ((left_own, left_sum), (right_own, right_sum))[i]
        for sender in range(2):
            part = out.at[pl.ds(sender * half, half)]
            local_chip = owner == xl
            to_self = jnp.logical_and(local_chip, jnp.logical_and(sender == core, jnp.logical_or(i == 0, core == 1)))
            came = lambda kind: prepared(own, part, ls.at[i, 0], lr.at[i, sender, kind], sib)

            @pl.when(jnp.logical_not(local_chip))
            def _():
                came(0).wait_recv()

            @pl.when(jnp.logical_and(local_chip, jnp.logical_not(to_self)))
            def _():
                came(1).wait_recv()


def exchange(left_grad, right_grad, rel_grad):
    dma = lambda *n: pltpu.SemaphoreType.DMA(n)
    shape = jax.ShapeDtypeStruct
    table = shape((D, E_PART), F32)
    half = pltpu.VMEM((D // 2, E_PART), F32)
    return pl.pallas_call(
        exchange_kernel,
        out_shape=(table, table, shape((SHARD, LANES), F32)),
        in_specs=[HBM] * 3,
        out_specs=(HBM, HBM, VMEM),
        scratch_shapes=[half] * 4
        + [
            pltpu.VMEM((Y, Z, 2, 2, SHARD, LANES), F32),
            pltpu.VMEM((Y, Z, 2, 2, SHARD, LANES), F32),
            pltpu.VMEM((6, Z, 2, 2, SHARD // 2, LANES), F32),
            pltpu.VMEM((6, Z, SHARD // 2, LANES), F32),
            pltpu.VMEM((14, SHARD // 2, LANES), F32),
            dma(2, 2), dma(2, 2, 2), dma(2), dma(2),
            dma(2), dma(2), dma(6), dma(6), dma(6), dma(6), dma(14), dma(14), dma(5),
        ],
        compiler_params=pltpu.CompilerParams(collective_id=1, has_side_effects=True, vmem_limit_bytes=LIMIT),
        name="exchange_gradients",
    )(left_grad, right_grad, rel_grad)


def update_kernel(
    left, left_state, left_sum, right, right_state, right_sum, rel, rel_state, rel_grad,
    left_next, left_state_next, right_next, right_state_next, rel_next, rel_state_next,
):
    for table, state, total, after, state_after in (
        (left, left_state, left_sum, left_next, left_state_next),
        (right, right_state, right_sum, right_next, right_state_next),
    ):
        grad = total[...]
        fresh = state[...] + jnp.sum(grad * grad, axis=0, keepdims=True) * (1.0 / D)
        state_after[...] = fresh
        after[...] = table[...] - grad * (RATE / jnp.sqrt(fresh))

    @pl.when(pl.program_id(0) == 0)
    def _():
        n = rel.shape[0]
        same = lax.broadcasted_iota(I32, (n, n), 0) == lax.broadcasted_iota(I32, (n, n), 1)
        column = lambda row: jnp.sum(jnp.where(same, jnp.broadcast_to(row, (n, n)), 0.0), axis=1, keepdims=True)
        across = lambda col: jnp.sum(jnp.where(same, jnp.broadcast_to(col, (n, n)), 0.0), axis=0, keepdims=True)
        grad = [rel_grad[pl.ds(j, n, stride=4), :] for j in range(4)]
        square = jnp.sum(sum(v * v for v in grad), axis=1, keepdims=True) * (1.0 / D)
        fresh = column(rel_state[...]) + square
        rel_state_next[...] = across(fresh)
        scale = RATE / jnp.sqrt(fresh)
        for j, change in enumerate(natural_of([v * scale for v in grad])):
            cols = pl.ds(j * LANES, change.shape[1])
            rel_next[:, cols] = rel[:, cols] - change


def update(left, left_state, left_sum, right, right_state, right_sum, rel, rel_state, rel_grad):
    wide = 2 * LANES
    table = pl.BlockSpec((D, wide), lambda g: (0, g))
    state = pl.BlockSpec((1, wide), lambda g: (0, g))
    whole = lambda shape: pl.BlockSpec(shape, lambda g: (0, 0))
    shape = jax.ShapeDtypeStruct
    big, row = shape((D, E_PART), F32), shape((1, E_PART), F32)
    return pl.pallas_call(
        update_kernel,
        grid=(E_PART // wide,),
        out_shape=(big, row, big, row, shape(rel.shape, F32), shape(rel_state.shape, F32)),
        in_specs=[table, state, table] * 2 + [whole(rel.shape), whole(rel_state.shape), whole((SHARD, LANES))],
        out_specs=(table, state, table, state, whole(rel.shape), whole(rel_state.shape)),
        compiler_params=pltpu.CompilerParams(vmem_limit_bytes=LIMIT),
        name="adagrad",
    )(left, left_state, left_sum, right, right_state, right_sum, rel, rel_state, rel_grad)


def shards(
    left_table, left_state, right_table, right_state, rel_table, rel_state,
    sources, relations, targets, bucket_counts, negatives,
):
    left, right = left_table.T, right_table.T
    rels, src, rel, dst, neg, counted, left_use, right_use = gather(
        rel_table, sources, relations, targets, negatives, bucket_counts, left, right
    )
    n_dom = 4 * Y * Z
    route = [((i - 1) % n_dom, i) for i in range(n_dom)]
    held, held_state, rels = lax.optimization_barrier((right_table, right_state, rels))
    held = lax.ppermute(held, "dom", route)
    held_state = lax.ppermute(held_state, "dom", route)
    core = lax.rem(lax.axis_index("dom"), 2)
    spot = jnp.stack([core, (core == lax.axis_index("rep")).astype(I32)])
    left_grad, right_grad, rel_grad = compute(
        spot, counted, src, rel, dst, neg, left, right, left_use, right_use, rels.reshape(-1, LANES)
    )
    left_sum, right_sum, rel_mine = exchange(
        left_grad, right_grad, rel_grad.reshape(Y, Z, 2, 2, 2, SHARD, LANES)
    )
    left_next, left_after, right_next, right_after, rel_next, rel_after = update(
        left, left_state[None], left_sum, held.T, held_state[None], right_sum, rel_table, rel_state[None], rel_mine
    )
    return left_next.T, left_after[0], right_next.T, right_after[0], rel_next, rel_after[0]


def solution(mesh):
    both = P(("dom", "rep"))
    rows = P(("dom", "rep"), None)
    table, state = P("dom", None), P("dom")
    return jax.shard_map(
        shards,
        mesh=mesh,
        in_specs=(table, state, table, state, rows, both, both, both, both, state, rows),
        out_specs=(table, state, table, state, rows, both),
        check_vma=False,
    )
```

```python
import jax
import jax.numpy as jnp
from jax import lax
from jax.experimental import pallas as pl
from jax.experimental.pallas import tpu as pltpu
from jax.sharding import PartitionSpec as P

RATE = 0.3
D, LANES = 400, 128
E_PART, GROUP, NEG = 1024, 512, 1024
CHUNK = 512
Y, Z, X = 4, 8, 4
SHARD = 48
SLOTS = 4096
F32, BF16, I32 = jnp.float32, jnp.bfloat16, jnp.int32
MESH = pl.DeviceIdType.MESH
VMEM = pl.BlockSpec(memory_space=pltpu.VMEM)
SMEM = pl.BlockSpec(memory_space=pltpu.SMEM)
HBM = pl.BlockSpec(memory_space=pltpu.HBM)
LIMIT = 60 * 2**20


def tiles_of(ref, first, n):
    rows = pl.ds(first, n)
    lane = lax.broadcasted_iota(I32, (n, LANES), 1)
    a, b, c = (ref[rows, pl.ds(j * LANES, LANES)] for j in range(3))
    d = jnp.concatenate([ref[rows, pl.ds(384, 16)], jnp.zeros((n, LANES - 16), F32)], axis=1)
    b1, c1, d1 = (pltpu.roll(v, 56, 1) for v in (b, c, d))
    zero = jnp.zeros((n, LANES), F32)
    return (
        a,
        jnp.where(lane < 72, b, zero),
        jnp.where(lane < 56, b1, c1),
        jnp.where(lane < 56, c1, jnp.where(lane < 72, d1, zero)),
    )


def natural_of(tiles):
    a, b, c, d = tiles
    lane = lax.broadcasted_iota(I32, a.shape, 1)
    c1, d1 = (pltpu.roll(v, 72, 1) for v in (c, d))
    return (a, jnp.where(lane < 72, b, c1), jnp.where(lane < 72, c1, d1), d1[:, :16])


def place():
    dom, xl = lax.axis_index("dom"), lax.axis_index("rep")
    core = lax.rem(dom, 2)
    xh = lax.rem(dom // 2, 2)
    z = lax.rem(dom // 4, Z)
    y = dom // (4 * Z)
    return y, z, xh, core, xl


def device(y, z, xh, core, xl):
    return {"dom": ((y * Z + z) * 2 + xh) * 2 + core, "rep": xl}


def shift_x(xh, xl, k):
    x = lax.rem(xh * 2 + xl + k, X)
    return x // 2, lax.rem(x, 2)


def greet(peers):
    barrier = pltpu.get_barrier_semaphore()
    for peer in peers:
        pl.semaphore_signal(barrier, inc=1, device_id=peer, device_id_type=MESH)
    pl.semaphore_wait(barrier, len(peers))


def neighbours():
    y, z, xh, core, xl = place()
    sib = device(y, z, xh, 1 - core, xl)
    xs = [(*shift_x(xh, xl, k),) for k in range(1, X)]
    xdev = [device(y, z, a, core, b) for a, b in xs]
    ydev = [device(lax.rem(y + k, Y), z, xh, core, xl) for k in range(1, Y)]
    zdev = [device(y, lax.rem(z + k, Z), xh, core, xl) for k in range(1, Z)]
    return sib, xdev, ydev, zdev


def remote(src, dst, send, recv, to):
    copy = pltpu.make_async_remote_copy(
        src_ref=src, dst_ref=dst, send_sem=send, recv_sem=recv, device_id=to, device_id_type=MESH
    )
    copy.start()
    return copy


def family():
    y, z, xh, core, xl = place()
    dom = lax.axis_index("dom")
    twin = dom + 1 - 2 * core
    return {"dom": twin, "rep": xl}, {"dom": dom, "rep": 1 - xl}, {"dom": twin, "rep": 1 - xl}


def prepared(src, dst, send, recv, to):
    return pltpu.make_async_remote_copy(
        src_ref=src, dst_ref=dst, send_sem=send, recv_sem=recv, device_id=to, device_id_type=MESH
    )


def gather_kernel(
    shard, src, rel, dst, neg, count, left, right,
    full, src_all, rel_all, dst_all, neg_all, count_use, left_use, right_use,
    rows, count_rows, zs, zr, ps, pr, cs, cr, es, ea, eb, ts, tr, local,
):
    y, z, xh, core, xl = place()
    sib, xdev, ydev, zdev = neighbours()
    _, partner, diagonal = family()
    greet([sib, partner, diagonal] + xdev + ydev + zdev)
    for j, tile in enumerate(tiles_of(shard, 0, 12)):
        rows[pl.ds(j, 12, stride=4), :] = tile
    first = [remote(rows, full.at[y, z, xh, core, xl], zs.at[k], zr.at[k], zdev[k]) for k in range(Z - 1)]
    own = pltpu.make_async_copy(rows, full.at[y, z, xh, core, xl], local.at[0])
    own.start()
    count_rows[...] = jnp.full((8, LANES), count[0], I32)

    lists = [
        (v, w.at[pl.ds(xl * n, n)])
        for v, w, n in ((src, src_all, SLOTS), (rel, rel_all, SLOTS), (dst, dst_all, SLOTS), (neg, neg_all, 8))
    ]
    twin = {"dom": sib["dom"], "rep": core}
    same = {"dom": lax.axis_index("dom"), "rep": core}
    cross = [prepared(v, w, es.at[i], eb.at[i, xl], twin) for i, (v, w) in enumerate(lists)]
    straight = [prepared(v, w, es.at[4 + i], ea.at[i], same) for i, (v, w) in enumerate(lists)]
    stay = [pltpu.make_async_copy(v, w, local.at[1 + i]) for i, (v, w) in enumerate(lists)]
    things = ((count_rows, count_use), (left, left_use), (right, right_use))
    tables = [prepared(v, w, ts.at[i], tr.at[i], sib) for i, (v, w) in enumerate(things)]
    stay.append(pltpu.make_async_copy(count_rows, count_use, local.at[5]))
    for copy in cross:
        copy.start()

    @pl.when(core == xl)
    def _():
        for copy in tables + stay:
            copy.start()

    @pl.when(core != xl)
    def _():
        for copy in straight:
            copy.start()

    own.wait()
    for copy in first:
        copy.wait()
    halves = [pl.ds(0, SHARD // 2), pl.ds(SHARD // 2, SHARD // 2)]
    down = []

    def below(ref):
        i = len(down)
        down.append(remote(ref, ref, cs.at[i], cr.at[i], sib))

    below(full.at[y, :, xh, core, xl])
    second = []
    for half, devs in enumerate((ydev, xdev)):
        part = full.at[y, :, xh, core, xl, halves[half]]
        for k in range(3):
            i = half * 3 + k
            second.append(remote(part, part, ps.at[i], pr.at[i], devs[k]))
    for i, copy in enumerate(second):
        copy.wait()
    third = []
    for half, devs in enumerate((xdev, ydev)):
        part = full.at[:, :, xh, core, xl, halves[0]] if half == 0 else full.at[y, :, :, core, :, halves[1]]
        for k in range(3):
            i = 6 + half * 3 + k
            third.append(remote(part, part, ps.at[i], pr.at[i], devs[k]))
    for k in range(1, 4):
        below(full.at[lax.rem(y + 4 - k, Y), :, xh, core, xl, halves[0]])
        a, b = shift_x(xh, xl, X - k)
        below(full.at[y, :, a, core, b, halves[1]])
    for k in range(1, 4):
        third[k - 1].wait()
        a, b = shift_x(xh, xl, X - k)
        below(full.at[:, :, a, core, b, halves[0]])
        third[2 + k].wait()
        below(full.at[lax.rem(y + 4 - k, Y), :, :, core, :, halves[1]])
    for copy in down:
        copy.wait()
    for copy in cross:
        copy.wait_send()

    @pl.when(core == xl)
    def _():
        for copy in tables:
            copy.wait_send()
        for copy in straight:
            copy.wait_recv()
        for copy in stay:
            copy.wait()

    @pl.when(core != xl)
    def _():
        for copy in tables:
            copy.wait_recv()
        for copy in straight:
            copy.wait_send()
        for i, (v, w) in enumerate(lists):
            for sender in range(2):
                prepared(v, w, es.at[i], eb.at[i, sender], twin).wait_recv()


def gather(shard, src, rel, dst, neg, count, left, right):
    dma = lambda *n: pltpu.SemaphoreType.DMA(n)
    shape = jax.ShapeDtypeStruct
    return pl.pallas_call(
        gather_kernel,
        out_shape=(
            shape((Y, Z, 2, 2, 2, SHARD, LANES), F32),
            shape((2 * SLOTS,), I32), shape((2 * SLOTS,), I32), shape((2 * SLOTS,), I32),
            shape((16, NEG), I32), shape((8, LANES), I32),
            shape((D, E_PART), F32), shape((D, E_PART), F32),
        ),
        in_specs=[VMEM] + [HBM] * 4 + [SMEM] + [HBM] * 2,
        out_specs=(HBM,) * 8,
        scratch_shapes=[
            pltpu.VMEM((SHARD, LANES), F32), pltpu.VMEM((8, LANES), I32),
            dma(7), dma(7), dma(12), dma(12), dma(13), dma(13),
            dma(8), dma(4), dma(4, 2), dma(3), dma(3), dma(6),
        ],
        compiler_params=pltpu.CompilerParams(collective_id=0, has_side_effects=True, vmem_limit_bytes=LIMIT),
        name="gather_relations",
    )(shard, src, rel, dst, neg, count, left, right)


def product(a, b, conjugate):
    if conjugate:
        re = lambda i, j: a[i] * b[i] + a[j] * b[j]
        im = lambda i, j: a[j] * b[i] - a[i] * b[j]
    else:
        re = lambda i, j: a[i] * b[i] - a[j] * b[j]
        im = lambda i, j: a[i] * b[j] + a[j] * b[i]
    return (re(0, 2), re(1, 3), im(0, 2), im(1, 3))


def embedding_tiles(ref, g):
    at = pl.ds(pl.multiple_of(g * LANES, LANES), LANES)
    zero = jnp.zeros((56, LANES), F32)
    full = lambda i: ref[pl.ds(i, LANES), at]
    part = lambda i: jnp.concatenate([ref[pl.ds(i, 72), at], zero], axis=0)
    return full(0), part(128), full(200), part(328)


def compute_kernel(
    spot, counted, src_hbm, rel_hbm, dst_hbm, neg, left_here, right_here, left_sent, right_sent, rels_hbm,
    left_hbm_grad, right_hbm_grad, rel_hbm_grad,
    left, right, rels, left_turned, right_turned, left_grad, right_grad, rel_grad,
    left_rows, right_rows, right_low, low_turned, heads, relat, tails, q_low, prob, neg_t, src, rel, dst, ids_in, sems, id_sems,
):
    count, core, at_home = counted[0, 0], spot[0], spot[1]
    n_blocks = (((count + GROUP - 1) >> 9) + 1 - core) >> 1
    tables = ((left_here, left_sent, left), (right_here, right_sent, right))
    loads = [pltpu.make_async_copy(v, w, sems.at[i]) for i, (v, _, w) in enumerate(tables)]
    loads.append(pltpu.make_async_copy(rels_hbm, rels, sems.at[2]))

    @pl.when(at_home == 1)
    def _():
        for copy in loads[:2]:
            copy.start()

    @pl.when(at_home == 0)
    def _():
        for i, (_, v, w) in enumerate(tables):
            pltpu.make_async_copy(v, w, sems.at[i]).start()

    loads[2].start()
    scaled = []
    for i, (v, w) in enumerate(((src_hbm, src), (rel_hbm, rel), (dst_hbm, dst))):
        held = ids_in.at[pl.ds(2 * SLOTS * i, 2 * SLOTS)]
        scaled.append((held, pltpu.make_async_copy(v, held, id_sems.at[i]), pltpu.make_async_copy(held, w, id_sems.at[i])))
        scaled[i][1].start()
    for held, came, goes in scaled:
        came.wait()
        held[...] = held[...] * 4
        goes.start()
    left_grad[...] = jnp.zeros_like(left_grad)
    right_grad[...] = jnp.zeros_like(right_grad)
    rel_grad[...] = jnp.zeros_like(rel_grad)
    neg_t[...] = jnp.zeros_like(neg_t)
    loads[0].wait()
    loads[1].wait()

    def prepare(g, _):
        first = pl.multiple_of(g * LANES, LANES)
        for j, tile in enumerate(embedding_tiles(left, g)):
            left_rows[pl.ds(4 * first + j, LANES, stride=4), :] = tile.T
        for j, tile in enumerate(embedding_tiles(right, g)):
            low_turned[pl.ds(j * LANES, LANES), pl.ds(first, LANES)] = tile.astype(BF16)
            tile = tile.T
            right_rows[pl.ds(4 * first + j, LANES, stride=4), :] = tile
            right_low[pl.ds(first, LANES), pl.ds(j * LANES, LANES)] = tile.astype(BF16)
        return 0

    lax.fori_loop(0, E_PART // LANES, prepare, 0)
    loads[2].wait()
    unroll = 32

    def rows_of(b, e):
        return [pl.ds(pl.multiple_of(ids[b * GROUP + e], 4), 4) for ids in (src, rel, dst)]

    def fetch(b, slot, e):
        s, r, t = rows_of(b, e)
        to = pl.ds(pl.multiple_of(slot + 4 * e, 4), 4)
        heads[to, :] = left_rows[s, :]
        relat[to, :] = rels[r, :]
        tails[to, :] = right_rows[t, :]

    for _, _, goes in scaled:
        goes.wait()

    def first_fetch(n, _):
        for u in range(unroll):
            fetch(core, 0, n * unroll + u)
        return 0

    lax.fori_loop(0, GROUP // unroll, first_fetch, 0)

    def block(i, _):
        b = 2 * i + core
        slot = pl.multiple_of(lax.rem(i, 2) * 4 * GROUP, 4 * GROUP)
        after = pl.multiple_of(4 * GROUP - slot, 4 * GROUP)

        named = neg[pl.ds(b, 1), :]
        high = (lax.broadcasted_iota(I32, (16, NEG), 0) == (named >> 7)).astype(F32).astype(BF16)
        low = (lax.broadcasted_iota(I32, (LANES, NEG), 0) == (named & 127)).astype(F32).astype(BF16)
        table = lax.dot_general(high, low, (((1,), (1,)), ((), ())), preferred_element_type=F32)
        counts = jnp.concatenate([table[h : h + 1, :] for h in range(E_PART // LANES)], axis=1)
        bias = jnp.where(counts > 0, 0.0, -jnp.inf)

        for ch in range(GROUP // CHUNK):
            rows = pl.ds(ch * CHUNK, CHUNK)
            at = [pl.ds(slot + 4 * ch * CHUNK + j, CHUNK, stride=4) for j in range(4)]
            h = [heads[a, :] for a in at]
            r = [relat[a, :] for a in at]
            t = [tails[a, :] for a in at]
            q = product(h, r, False)
            positive = jnp.sum(q[0] * t[0] + q[1] * t[1] + q[2] * t[2] + q[3] * t[3], axis=1, keepdims=True)
            ql = jnp.concatenate([x.astype(BF16) for x in q], axis=1)
            q_low[rows, :] = ql
            scores = jnp.dot(ql, low_turned[...], preferred_element_type=F32) + bias
            place_in = b * GROUP + ch * CHUNK + lax.broadcasted_iota(I32, (CHUNK, 1), 0)
            live = (place_in < count).astype(F32)
            top = jnp.maximum(positive, jnp.max(scores, axis=1, keepdims=True))
            pos_exp = jnp.exp(positive - top)
            neg_exp = jnp.exp(scores - top)
            total = pos_exp + jnp.sum(neg_exp * counts, axis=1, keepdims=True)
            weight = live / total
            pos_coef = pos_exp * weight - live
            p = (neg_exp * weight).astype(BF16)
            prob[rows, :] = p
            many = p.astype(F32) * counts
            many_high = many.astype(BF16)
            many_low = (many - many_high.astype(F32)).astype(BF16)
            d = jnp.dot(many_high, right_low[...], preferred_element_type=F32) + jnp.dot(
                many_low, right_low[...], preferred_element_type=F32
            )
            dq = [d[:, j * LANES : (j + 1) * LANES] + pos_coef * t[j] for j in range(4)]
            for a, x, y, z in zip(at, product(dq, r, True), product(dq, h, True), q):
                heads[a, :] = x
                relat[a, :] = y
                tails[a, :] = pos_coef * z

        neg_t[...] += counts * lax.dot_general(
            q_low[...], prob[...], (((0,), (0,)), ((), ())), preferred_element_type=F32
        )

        def scatter(n, _):
            for u in range(unroll):
                e = n * unroll + u
                of = pl.ds(pl.multiple_of(slot + 4 * e, 4), 4)
                for to, total, terms in zip(rows_of(b, e), (left_grad, rel_grad, right_grad), (heads, relat, tails)):
                    total[to, :] += terms[of, :]
                fetch(b + 2, after, e)
            return 0

        lax.fori_loop(0, GROUP // unroll, scatter, 0)
        return 0

    lax.fori_loop(0, n_blocks, block, 0)
    rel_out = pltpu.make_async_copy(rel_grad, rel_hbm_grad, sems.at[2])
    rel_out.start()

    def finish(g, _):
        first = pl.multiple_of(g * LANES, LANES)
        to = pl.ds(first, LANES)
        for j, (start, size) in enumerate(((0, 128), (128, 72), (200, 128), (328, 72))):
            at = pl.ds(4 * first + j, LANES, stride=4)
            left_turned[pl.ds(start, size), to] = left_grad[at, :].T[:size]
            right_turned[pl.ds(start, size), to] = (
                right_grad[at, :].T[:size] + neg_t[pl.ds(j * LANES, size), to]
            )
        return 0

    lax.fori_loop(0, E_PART // LANES, finish, 0)
    outs = [
        pltpu.make_async_copy(left_turned, left_hbm_grad, sems.at[0]),
        pltpu.make_async_copy(right_turned, right_hbm_grad, sems.at[1]),
    ]
    for copy in outs:
        copy.start()
    for copy in outs:
        copy.wait()
    rel_out.wait()


def compute(spot, counted, src, rel, dst, neg, left, right, left_sent, right_sent, rels):
    shape = jax.ShapeDtypeStruct
    n = rels.shape[0]
    table = pltpu.VMEM((D, E_PART), F32)
    rows = pltpu.VMEM((4 * E_PART, LANES), F32)
    block = pltpu.VMEM((8 * GROUP, LANES), F32)
    return pl.pallas_call(
        compute_kernel,
        out_shape=(shape((D, E_PART), F32), shape((D, E_PART), F32), shape((n, LANES), F32)),
        in_specs=[SMEM] * 2 + [HBM] * 3 + [VMEM] + [HBM] * 5,
        out_specs=(HBM,) * 3,
        scratch_shapes=[
            table, table, pltpu.VMEM((n, LANES), F32), table, table, rows, rows, pltpu.VMEM((n, LANES), F32),
            rows, rows,
            pltpu.VMEM((E_PART, 512), BF16), pltpu.VMEM((512, E_PART), BF16),
            block, block, block,
            pltpu.VMEM((GROUP, 512), BF16), pltpu.VMEM((GROUP, E_PART), BF16), pltpu.VMEM((512, E_PART), F32),
            pltpu.SMEM((2 * SLOTS,), I32), pltpu.SMEM((2 * SLOTS,), I32), pltpu.SMEM((2 * SLOTS,), I32),
            pltpu.VMEM((6 * SLOTS,), I32),
            pltpu.SemaphoreType.DMA((3,)), pltpu.SemaphoreType.DMA((3,)),
        ],
        compiler_params=pltpu.CompilerParams(vmem_limit_bytes=LIMIT),
        cost_estimate=pl.CostEstimate(flops=20 * 10**9, bytes_accessed=10**8, transcendentals=10**6),
        name="blocks",
    )(spot, counted, src, rel, dst, neg, left, right, left_sent, right_sent, rels)


def exchange_kernel(
    left_grad, right_grad, rel_grad,
    left_sum, right_sum, rel_mine,
    left_own, left_sib, right_own, right_sib, acc, from_core,
    from_y0, from_y2, from_x0, from_x2, from_z0, from_z2, low_z, low_y, low_x,
    ls, lr, ss, sr, cs, cr, ys, yr, xs, xr, zs, zr, local,
):
    y, z, xh, core, xl = place()
    sib, xdev, ydev, zdev = neighbours()
    _, partner, diagonal = family()
    dom = lax.axis_index("dom")
    n_dom = 4 * Y * Z
    pair = dom - core
    barrier = pltpu.get_barrier_semaphore()
    peers = [sib, partner, diagonal] + xdev + ydev + zdev
    for peer in peers:
        pl.semaphore_signal(barrier, inc=1, device_id=peer, device_id_type=MESH)

    @pl.when(core == 0)
    def _():
        for k in (2, 1):
            behind = {"dom": lax.rem(dom + n_dom - k, n_dom), "rep": 1}
            pl.semaphore_signal(barrier, inc=1, device_id=behind, device_id_type=MESH)

    pl.semaphore_wait(barrier, len(peers) + 2 * xl)

    half = D // 2
    mine, other = pl.ds(core * half, half), pl.ds((1 - core) * half, half)
    pairs = []
    for i, (grad, own, recv) in enumerate(((left_grad, left_own, left_sib), (right_grad, right_own, right_sib))):
        keep = pltpu.make_async_copy(grad.at[mine], own, local.at[i])
        keep.start()
        pairs.append((remote(grad.at[other], recv, ss.at[i], sr.at[i], sib), keep))
    cut = [pl.ds(0, 24), pl.ds(24, 8), pl.ds(32, 16)]
    down = [
        remote(rel_grad.at[:, :, :, 1 - core, :, c], from_core.at[:, :, :, :, c], cs.at[i], cr.at[i], sib)
        for i, c in enumerate(cut)
    ]
    keep_rel = pltpu.make_async_copy(rel_grad.at[:, :, :, core], acc, local.at[2])
    keep_rel.start()

    left_to = pair + xl
    right_to = lax.rem(pair + xl + 1, n_dom)
    sends, stays = [], []
    for i, (own, recv, out, to) in enumerate(
        ((left_own, left_sib, left_sum, left_to), (right_own, right_sib, right_sum, right_to))
    ):
        for copy in pairs[i]:
            copy.wait()

        def add(j, _):
            at = pl.ds(pl.multiple_of(8 * j, 8), 8)
            own[at, :] += recv[at, :]
            return 0

        lax.fori_loop(0, half // 8, add, 0)
        part = out.at[mine]
        far = prepared(own, part, ls.at[i, 0], lr.at[i, core, 0], {"dom": to, "rep": 1 - xl})
        near = prepared(own, part, ls.at[i, 1], lr.at[i, core, 1], {"dom": to, "rep": xl})
        stay = pltpu.make_async_copy(own, part, local.at[3 + i])
        far.start()
        self_too = to == dom

        @pl.when(self_too)
        def _():
            stay.start()

        @pl.when(jnp.logical_not(self_too))
        def _():
            near.start()

        sends.append((far, near, stay, self_too))

    keep_rel.wait()
    by_y, by_x, by_z = {}, {}, {}
    wide = (from_y0, None, from_y2)
    middle = (from_x0, None, from_x2)
    last = (from_z0, None, from_z2)
    for i, c in enumerate(cut):
        down[i].wait()

        def add_core(n, _):
            at = (n // Z, lax.rem(n, Z), slice(None), slice(None), c)
            acc[at] += from_core[at]
            return 0

        lax.fori_loop(0, Y * Z, add_core, 0)
        if i == 1:
            by_z[i] = [
                remote(acc.at[:, lax.rem(z + k, Z), :, :, c], low_z.at[k - 1], zs.at[6 + k], zr.at[6 + k], zdev[k - 1])
                for k in range(1, Z)
            ]
            continue
        by_y[i] = []
        for k in range(1, Y):
            t, n = lax.rem(y + k, Y), 3 * i + k - 1
            by_y[i].append(remote(acc.at[t, :, :, :, c], wide[i].at[k - 1], ys.at[n], yr.at[n], ydev[k - 1]))
    for i in (0, 2):
        c, came = cut[i], wide[i]
        for copy in by_y[i]:
            copy.wait()

        def add_y(n, _):
            acc[y, n, :, :, c] += came[0, n] + came[1, n] + came[2, n]
            return 0

        lax.fori_loop(0, Z, add_y, 0)
        by_x[i] = []
        for k in range(1, X):
            (a, b), n = shift_x(xh, xl, k), 3 * i + k - 1
            by_x[i].append(remote(acc.at[y, :, a, b, c], middle[i].at[k - 1], xs.at[n], xr.at[n], xdev[k - 1]))
    c = cut[1]
    for copy in by_z[1]:
        copy.wait()

    def add_z(n, _):
        total = acc[n, z, :, :, c]
        for k in range(Z - 1):
            total = total + low_z[k, n]
        acc[n, z, :, :, c] = total
        return 0

    lax.fori_loop(0, Y, add_z, 0)
    by_y[1] = [
        remote(acc.at[lax.rem(y + k, Y), z, :, :, c], low_y.at[k - 1], ys.at[2 + k], yr.at[2 + k], ydev[k - 1])
        for k in range(1, Y)
    ]
    for i in (0, 2):
        c, came = cut[i], middle[i]
        for copy in by_x[i]:
            copy.wait()

        def add_x(n, _):
            acc[y, n, xh, xl, c] += came[0, n] + came[1, n] + came[2, n]
            return 0

        lax.fori_loop(0, Z, add_x, 0)
        by_z[i] = []
        for k in range(1, Z):
            t, n = lax.rem(z + k, Z), 7 * i + k - 1
            by_z[i].append(remote(acc.at[y, t, xh, xl, c], last[i].at[k - 1], zs.at[n], zr.at[n], zdev[k - 1]))
    c = cut[1]
    for copy in by_y[1]:
        copy.wait()
    acc[y, z, :, :, c] += low_y[0] + low_y[1] + low_y[2]
    by_x[1] = []
    for k in range(1, X):
        a, b = shift_x(xh, xl, k)
        by_x[1].append(remote(acc.at[y, z, a, b, c], low_x.at[k - 1], xs.at[2 + k], xr.at[2 + k], xdev[k - 1]))
    for i in (0, 2):
        c = cut[i]
        for copy in by_z[i]:
            copy.wait()
        total = acc[y, z, xh, xl, c]
        for k in range(Z - 1):
            total = total + last[i][k]
        rel_mine[c, :] = total
    for copy in by_x[1]:
        copy.wait()
    rel_mine[cut[1], :] = acc[y, z, xh, xl, cut[1]] + low_x[0] + low_x[1] + low_x[2]

    for far, near, stay, self_too in sends:
        far.wait_send()

        @pl.when(self_too)
        def _():
            stay.wait()

        @pl.when(jnp.logical_not(self_too))
        def _():
            near.wait_send()

    for i, owner in ((0, core), (1, 1 - core)):
        own, out = ((left_own, left_sum), (right_own, right_sum))[i]
        for sender in range(2):
            part = out.at[pl.ds(sender * half, half)]
            local_chip = owner == xl
            to_self = jnp.logical_and(local_chip, jnp.logical_and(sender == core, jnp.logical_or(i == 0, core == 1)))
            came = lambda kind: prepared(own, part, ls.at[i, 0], lr.at[i, sender, kind], sib)

            @pl.when(jnp.logical_not(local_chip))
            def _():
                came(0).wait_recv()

            @pl.when(jnp.logical_and(local_chip, jnp.logical_not(to_self)))
            def _():
                came(1).wait_recv()


def exchange(left_grad, right_grad, rel_grad):
    dma = lambda *n: pltpu.SemaphoreType.DMA(n)
    shape = jax.ShapeDtypeStruct
    table = shape((D, E_PART), F32)
    half = pltpu.VMEM((D // 2, E_PART), F32)
    return pl.pallas_call(
        exchange_kernel,
        out_shape=(table, table, shape((SHARD, LANES), F32)),
        in_specs=[HBM] * 3,
        out_specs=(HBM, HBM, VMEM),
        scratch_shapes=[half] * 4
        + [
            pltpu.VMEM((Y, Z, 2, 2, SHARD, LANES), F32),
            pltpu.VMEM((Y, Z, 2, 2, SHARD, LANES), F32),
            pltpu.VMEM((3, Z, 2, 2, 24, LANES), F32), pltpu.VMEM((3, Z, 2, 2, 16, LANES), F32),
            pltpu.VMEM((3, Z, 24, LANES), F32), pltpu.VMEM((3, Z, 16, LANES), F32),
            pltpu.VMEM((7, 24, LANES), F32), pltpu.VMEM((7, 16, LANES), F32),
            pltpu.VMEM((7, Y, 2, 2, 8, LANES), F32), pltpu.VMEM((3, 2, 2, 8, LANES), F32), pltpu.VMEM((3, 8, LANES), F32),
            dma(2, 2), dma(2, 2, 2), dma(2), dma(2),
            dma(3), dma(3), dma(9), dma(9), dma(9), dma(9), dma(21), dma(21), dma(5),
        ],
        compiler_params=pltpu.CompilerParams(collective_id=1, has_side_effects=True, vmem_limit_bytes=LIMIT),
        name="exchange_gradients",
    )(left_grad, right_grad, rel_grad)


def update_kernel(
    left, left_state, left_sum, right, right_state, right_sum, rel, rel_state, rel_grad,
    left_next, left_state_next, right_next, right_state_next, rel_next, rel_state_next,
):
    for table, state, total, after, state_after in (
        (left, left_state, left_sum, left_next, left_state_next),
        (right, right_state, right_sum, right_next, right_state_next),
    ):
        grad = total[...]
        fresh = state[...] + jnp.sum(grad * grad, axis=0, keepdims=True) * (1.0 / D)
        state_after[...] = fresh
        after[...] = table[...] - grad * (RATE / jnp.sqrt(fresh))

    @pl.when(pl.program_id(0) == 0)
    def _():
        n = rel.shape[0]
        same = lax.broadcasted_iota(I32, (n, n), 0) == lax.broadcasted_iota(I32, (n, n), 1)
        column = lambda row: jnp.sum(jnp.where(same, jnp.broadcast_to(row, (n, n)), 0.0), axis=1, keepdims=True)
        across = lambda col: jnp.sum(jnp.where(same, jnp.broadcast_to(col, (n, n)), 0.0), axis=0, keepdims=True)
        grad = [rel_grad[pl.ds(j, n, stride=4), :] for j in range(4)]
        square = jnp.sum(sum(v * v for v in grad), axis=1, keepdims=True) * (1.0 / D)
        fresh = column(rel_state[...]) + square
        rel_state_next[...] = across(fresh)
        scale = RATE / jnp.sqrt(fresh)
        for j, change in enumerate(natural_of([v * scale for v in grad])):
            cols = pl.ds(j * LANES, change.shape[1])
            rel_next[:, cols] = rel[:, cols] - change


def update(left, left_state, left_sum, right, right_state, right_sum, rel, rel_state, rel_grad):
    wide = 2 * LANES
    table = pl.BlockSpec((D, wide), lambda g: (0, g))
    state = pl.BlockSpec((1, wide), lambda g: (0, g))
    whole = lambda shape: pl.BlockSpec(shape, lambda g: (0, 0))
    shape = jax.ShapeDtypeStruct
    big, row = shape((D, E_PART), F32), shape((1, E_PART), F32)
    return pl.pallas_call(
        update_kernel,
        grid=(E_PART // wide,),
        out_shape=(big, row, big, row, shape(rel.shape, F32), shape(rel_state.shape, F32)),
        in_specs=[table, state, table] * 2 + [whole(rel.shape), whole(rel_state.shape), whole((SHARD, LANES))],
        out_specs=(table, state, table, state, whole(rel.shape), whole(rel_state.shape)),
        compiler_params=pltpu.CompilerParams(vmem_limit_bytes=LIMIT),
        name="adagrad",
    )(left, left_state, left_sum, right, right_state, right_sum, rel, rel_state, rel_grad)


def shards(
    left_table, left_state, right_table, right_state, rel_table, rel_state,
    sources, relations, targets, bucket_counts, negatives,
):
    left, right = left_table.T, right_table.T
    rels, src, rel, dst, neg, counted, left_use, right_use = gather(
        rel_table, sources, relations, targets, negatives, bucket_counts, left, right
    )
    n_dom = 4 * Y * Z
    route = [((i - 1) % n_dom, i) for i in range(n_dom)]
    held, held_state, rels = lax.optimization_barrier((right_table, right_state, rels))
    held = lax.ppermute(held, "dom", route)
    held_state = lax.ppermute(held_state, "dom", route)
    core = lax.rem(lax.axis_index("dom"), 2)
    spot = jnp.stack([core, (core == lax.axis_index("rep")).astype(I32)])
    left_grad, right_grad, rel_grad = compute(
        spot, counted, src, rel, dst, neg, left, right, left_use, right_use, rels.reshape(-1, LANES)
    )
    left_sum, right_sum, rel_mine = exchange(
        left_grad, right_grad, rel_grad.reshape(Y, Z, 2, 2, 2, SHARD, LANES)
    )
    left_next, left_after, right_next, right_after, rel_next, rel_after = update(
        left, left_state[None], left_sum, held.T, held_state[None], right_sum, rel_table, rel_state[None], rel_mine
    )
    return left_next.T, left_after[0], right_next.T, right_after[0], rel_next, rel_after[0]


def solution(mesh):
    both = P(("dom", "rep"))
    rows = P(("dom", "rep"), None)
    table, state = P("dom", None), P("dom")
    return jax.shard_map(
        shards,
        mesh=mesh,
        in_specs=(table, state, table, state, rows, both, both, both, both, state, rows),
        out_specs=(table, state, table, state, rows, both),
        check_vma=False,
    )
```

```python
import jax
import jax.numpy as jnp
from jax import lax
from jax.experimental import pallas as pl
from jax.experimental.pallas import tpu as pltpu
from jax.sharding import PartitionSpec as P

RATE = 0.3
D, LANES = 400, 128
E_PART, GROUP, NEG = 1024, 512, 1024
CHUNK = 512
Y, Z, X = 4, 8, 4
SHARD = 48
SLOTS = 4096
F32, BF16, I32 = jnp.float32, jnp.bfloat16, jnp.int32
MESH = pl.DeviceIdType.MESH
VMEM = pl.BlockSpec(memory_space=pltpu.VMEM)
SMEM = pl.BlockSpec(memory_space=pltpu.SMEM)
HBM = pl.BlockSpec(memory_space=pltpu.HBM)
LIMIT = 60 * 2**20


def tiles_of(ref, first, n):
    rows = pl.ds(first, n)
    lane = lax.broadcasted_iota(I32, (n, LANES), 1)
    a, b, c = (ref[rows, pl.ds(j * LANES, LANES)] for j in range(3))
    d = jnp.concatenate([ref[rows, pl.ds(384, 16)], jnp.zeros((n, LANES - 16), F32)], axis=1)
    b1, c1, d1 = (pltpu.roll(v, 56, 1) for v in (b, c, d))
    zero = jnp.zeros((n, LANES), F32)
    return (
        a,
        jnp.where(lane < 72, b, zero),
        jnp.where(lane < 56, b1, c1),
        jnp.where(lane < 56, c1, jnp.where(lane < 72, d1, zero)),
    )


def natural_of(tiles):
    a, b, c, d = tiles
    lane = lax.broadcasted_iota(I32, a.shape, 1)
    c1, d1 = (pltpu.roll(v, 72, 1) for v in (c, d))
    return (a, jnp.where(lane < 72, b, c1), jnp.where(lane < 72, c1, d1), d1[:, :16])


def place():
    dom, xl = lax.axis_index("dom"), lax.axis_index("rep")
    core = lax.rem(dom, 2)
    xh = lax.rem(dom // 2, 2)
    z = lax.rem(dom // 4, Z)
    y = dom // (4 * Z)
    return y, z, xh, core, xl


def device(y, z, xh, core, xl):
    return {"dom": ((y * Z + z) * 2 + xh) * 2 + core, "rep": xl}


def shift_x(xh, xl, k):
    x = lax.rem(xh * 2 + xl + k, X)
    return x // 2, lax.rem(x, 2)


def greet(peers):
    barrier = pltpu.get_barrier_semaphore()
    for peer in peers:
        pl.semaphore_signal(barrier, inc=1, device_id=peer, device_id_type=MESH)
    pl.semaphore_wait(barrier, len(peers))


def neighbours():
    y, z, xh, core, xl = place()
    sib = device(y, z, xh, 1 - core, xl)
    xs = [(*shift_x(xh, xl, k),) for k in range(1, X)]
    xdev = [device(y, z, a, core, b) for a, b in xs]
    ydev = [device(lax.rem(y + k, Y), z, xh, core, xl) for k in range(1, Y)]
    zdev = [device(y, lax.rem(z + k, Z), xh, core, xl) for k in range(1, Z)]
    return sib, xdev, ydev, zdev


def remote(src, dst, send, recv, to):
    copy = pltpu.make_async_remote_copy(
        src_ref=src, dst_ref=dst, send_sem=send, recv_sem=recv, device_id=to, device_id_type=MESH
    )
    copy.start()
    return copy


def family():
    y, z, xh, core, xl = place()
    dom = lax.axis_index("dom")
    twin = dom + 1 - 2 * core
    return {"dom": twin, "rep": xl}, {"dom": dom, "rep": 1 - xl}, {"dom": twin, "rep": 1 - xl}


def prepared(src, dst, send, recv, to):
    return pltpu.make_async_remote_copy(
        src_ref=src, dst_ref=dst, send_sem=send, recv_sem=recv, device_id=to, device_id_type=MESH
    )


def gather_kernel(
    shard, src, rel, dst, neg, count, left, right,
    full, src_all, rel_all, dst_all, neg_all, count_use, spot, left_use, right_use,
    rows, count_rows, zs, zr, ps, pr, cs, cr, es, ea, eb, ts, tr, local,
):
    y, z, xh, core, xl = place()
    sib, xdev, ydev, zdev = neighbours()
    _, partner, diagonal = family()
    greet([sib, partner, diagonal] + xdev + ydev + zdev)
    for j, tile in enumerate(tiles_of(shard, 0, 12)):
        rows[pl.ds(j, 12, stride=4), :] = tile
    first = [remote(rows, full.at[y, z, xh, core, xl], zs.at[k], zr.at[k], zdev[k]) for k in range(Z - 1)]
    own = pltpu.make_async_copy(rows, full.at[y, z, xh, core, xl], local.at[0])
    own.start()
    count_rows[...] = jnp.full((8, LANES), count[0], I32)
    line = lax.broadcasted_iota(I32, (8, LANES), 0)
    spot[...] = jnp.where(line == 0, core, jnp.where(core == xl, 1, 0))

    lists = [
        (v, w.at[pl.ds(xl * n, n)])
        for v, w, n in ((src, src_all, SLOTS), (rel, rel_all, SLOTS), (dst, dst_all, SLOTS), (neg, neg_all, 8))
    ]
    twin = {"dom": sib["dom"], "rep": core}
    same = {"dom": lax.axis_index("dom"), "rep": core}
    cross = [prepared(v, w, es.at[i], eb.at[i, xl], twin) for i, (v, w) in enumerate(lists)]
    straight = [prepared(v, w, es.at[4 + i], ea.at[i], same) for i, (v, w) in enumerate(lists)]
    stay = [pltpu.make_async_copy(v, w, local.at[1 + i]) for i, (v, w) in enumerate(lists)]
    things = ((count_rows, count_use), (left, left_use), (right, right_use))
    tables = [prepared(v, w, ts.at[i], tr.at[i], sib) for i, (v, w) in enumerate(things)]
    stay.append(pltpu.make_async_copy(count_rows, count_use, local.at[5]))
    for copy in cross:
        copy.start()

    @pl.when(core == xl)
    def _():
        for copy in tables + stay:
            copy.start()

    @pl.when(core != xl)
    def _():
        for copy in straight:
            copy.start()

    own.wait()
    for copy in first:
        copy.wait()
    halves = [pl.ds(0, SHARD // 2), pl.ds(SHARD // 2, SHARD // 2)]
    down = []

    def below(ref):
        i = len(down)
        down.append(remote(ref, ref, cs.at[i], cr.at[i], sib))

    below(full.at[y, :, xh, core, xl])
    second = []
    for half, devs in enumerate((ydev, xdev)):
        part = full.at[y, :, xh, core, xl, halves[half]]
        for k in range(3):
            i = half * 3 + k
            second.append(remote(part, part, ps.at[i], pr.at[i], devs[k]))
    for i, copy in enumerate(second):
        copy.wait()
    low, high = 0, 1

    def part(half, k, which):
        if half == 0:
            a, b = shift_x(xh, xl, k)
            return full.at[pl.ds(2 * which, 2), :, a, core, b, halves[0]]
        return full.at[lax.rem(y + k, Y), pl.ds(4 * which, 4), :, core, :, halves[1]]

    third = {}
    ends = ((xdev[0], xdev[2]), (ydev[0], ydev[2]))

    def ring(half, k, which, up):
        i = 6 + len(third)
        ref = part(half, k, which)
        third[half, k, which, up] = remote(ref, ref, ps.at[i], pr.at[i], ends[half][1 - up])

    for up, which in ((1, low), (0, high), (1, high), (0, low)):
        for half in range(2):
            ring(half, 0, which, up)
    for k in range(1, 4):
        below(full.at[lax.rem(y + 4 - k, Y), :, xh, core, xl, halves[0]])
        a, b = shift_x(xh, xl, X - k)
        below(full.at[y, :, a, core, b, halves[1]])
    for half in range(2):
        third[half, 0, low, 1].wait()
        ring(half, 3, low, 1)
        third[half, 0, high, 0].wait()
        ring(half, 1, high, 0)
        below(part(half, 3, low))
        below(part(half, 1, high))
    for half in range(2):
        third[half, 0, high, 1].wait()
        below(part(half, 3, high))
        third[half, 0, low, 0].wait()
        below(part(half, 1, low))
    for half in range(2):
        third[half, 3, low, 1].wait()
        below(part(half, 2, low))
        third[half, 1, high, 0].wait()
        below(part(half, 2, high))
    for copy in down:
        copy.wait()
    for copy in cross:
        copy.wait_send()

    @pl.when(core == xl)
    def _():
        for copy in tables:
            copy.wait_send()
        for copy in straight:
            copy.wait_recv()
        for copy in stay:
            copy.wait()

    @pl.when(core != xl)
    def _():
        for copy in tables:
            copy.wait_recv()
        for copy in straight:
            copy.wait_send()
        for i, (v, w) in enumerate(lists):
            for sender in range(2):
                prepared(v, w, es.at[i], eb.at[i, sender], twin).wait_recv()


def gather(shard, src, rel, dst, neg, count, left, right):
    dma = lambda *n: pltpu.SemaphoreType.DMA(n)
    shape = jax.ShapeDtypeStruct
    return pl.pallas_call(
        gather_kernel,
        out_shape=(
            shape((Y, Z, 2, 2, 2, SHARD, LANES), F32),
            shape((2 * SLOTS,), I32), shape((2 * SLOTS,), I32), shape((2 * SLOTS,), I32),
            shape((16, NEG), I32), shape((8, LANES), I32), shape((8, LANES), I32),
            shape((D, E_PART), F32), shape((D, E_PART), F32),
        ),
        in_specs=[VMEM] + [HBM] * 4 + [SMEM] + [HBM] * 2,
        out_specs=(HBM,) * 6 + (VMEM,) + (HBM,) * 2,
        scratch_shapes=[
            pltpu.VMEM((SHARD, LANES), F32), pltpu.VMEM((8, LANES), I32),
            dma(7), dma(7), dma(18), dma(18), dma(19), dma(19),
            dma(8), dma(4), dma(4, 2), dma(3), dma(3), dma(6),
        ],
        compiler_params=pltpu.CompilerParams(collective_id=0, has_side_effects=True, vmem_limit_bytes=LIMIT),
        name="gather_relations",
    )(shard, src, rel, dst, neg, count, left, right)


def product(a, b, conjugate):
    if conjugate:
        re = lambda i, j: a[i] * b[i] + a[j] * b[j]
        im = lambda i, j: a[j] * b[i] - a[i] * b[j]
    else:
        re = lambda i, j: a[i] * b[i] - a[j] * b[j]
        im = lambda i, j: a[i] * b[j] + a[j] * b[i]
    return (re(0, 2), re(1, 3), im(0, 2), im(1, 3))


def embedding_tiles(ref, g):
    at = pl.ds(pl.multiple_of(g * LANES, LANES), LANES)
    zero = jnp.zeros((56, LANES), F32)
    full = lambda i: ref[pl.ds(i, LANES), at]
    part = lambda i: jnp.concatenate([ref[pl.ds(i, 72), at], zero], axis=0)
    return full(0), part(128), full(200), part(328)


def compute_kernel(
    spot, counted, src_hbm, rel_hbm, dst_hbm, neg, left_here, right_here, left_sent, right_sent, rels_hbm,
    left_hbm_grad, right_hbm_grad, rel_hbm_grad,
    left, right, rels, left_turned, right_turned, left_grad, right_grad, rel_grad,
    left_rows, right_rows, right_low, low_turned, heads, relat, tails, q_low, prob, neg_t, src, rel, dst, ids_in, sems, id_sems,
):
    count, core, at_home = counted[0, 0], spot[0, 0], spot[1, 0]
    n_blocks = (((count + GROUP - 1) >> 9) + 1 - core) >> 1
    tables = ((left_here, left_sent, left), (right_here, right_sent, right))
    loads = [pltpu.make_async_copy(v, w, sems.at[i]) for i, (v, _, w) in enumerate(tables)]
    loads.append(pltpu.make_async_copy(rels_hbm, rels, sems.at[2]))

    @pl.when(at_home == 1)
    def _():
        for copy in loads[:2]:
            copy.start()

    @pl.when(at_home == 0)
    def _():
        for i, (_, v, w) in enumerate(tables):
            pltpu.make_async_copy(v, w, sems.at[i]).start()

    loads[2].start()
    scaled = []
    for i, (v, w) in enumerate(((src_hbm, src), (rel_hbm, rel), (dst_hbm, dst))):
        held = ids_in.at[pl.ds(2 * SLOTS * i, 2 * SLOTS)]
        scaled.append((held, pltpu.make_async_copy(v, held, id_sems.at[i]), pltpu.make_async_copy(held, w, id_sems.at[i])))
        scaled[i][1].start()
    for held, came, goes in scaled:
        came.wait()
        held[...] = held[...] * 4
        goes.start()
    left_grad[...] = jnp.zeros_like(left_grad)
    right_grad[...] = jnp.zeros_like(right_grad)
    rel_grad[...] = jnp.zeros_like(rel_grad)
    neg_t[...] = jnp.zeros_like(neg_t)
    loads[0].wait()
    loads[1].wait()

    def prepare(g, _):
        first = pl.multiple_of(g * LANES, LANES)
        for j, tile in enumerate(embedding_tiles(left, g)):
            left_rows[pl.ds(4 * first + j, LANES, stride=4), :] = tile.T
        for j, tile in enumerate(embedding_tiles(right, g)):
            low_turned[pl.ds(j * LANES, LANES), pl.ds(first, LANES)] = tile.astype(BF16)
            tile = tile.T
            right_rows[pl.ds(4 * first + j, LANES, stride=4), :] = tile
            right_low[pl.ds(first, LANES), pl.ds(j * LANES, LANES)] = tile.astype(BF16)
        return 0

    lax.fori_loop(0, E_PART // LANES, prepare, 0)
    loads[2].wait()
    unroll = 32

    def rows_of(b, e):
        return [pl.ds(pl.multiple_of(ids[b * GROUP + e], 4), 4) for ids in (src, rel, dst)]

    def fetch(b, slot, e):
        s, r, t = rows_of(b, e)
        to = pl.ds(pl.multiple_of(slot + 4 * e, 4), 4)
        heads[to, :] = left_rows[s, :]
        relat[to, :] = rels[r, :]
        tails[to, :] = right_rows[t, :]

    for _, _, goes in scaled:
        goes.wait()

    def first_fetch(n, _):
        for u in range(unroll):
            fetch(core, 0, n * unroll + u)
        return 0

    lax.fori_loop(0, GROUP // unroll, first_fetch, 0)

    def block(i, _):
        b = 2 * i + core
        slot = pl.multiple_of(lax.rem(i, 2) * 4 * GROUP, 4 * GROUP)
        after = pl.multiple_of(4 * GROUP - slot, 4 * GROUP)

        named = neg[pl.ds(b, 1), :]
        high = (lax.broadcasted_iota(I32, (16, NEG), 0) == (named >> 7)).astype(F32).astype(BF16)
        low = (lax.broadcasted_iota(I32, (LANES, NEG), 0) == (named & 127)).astype(F32).astype(BF16)
        table = lax.dot_general(high, low, (((1,), (1,)), ((), ())), preferred_element_type=F32)
        counts = jnp.concatenate([table[h : h + 1, :] for h in range(E_PART // LANES)], axis=1)
        bias = jnp.where(counts > 0, 0.0, -jnp.inf)

        for ch in range(GROUP // CHUNK):
            rows = pl.ds(ch * CHUNK, CHUNK)
            at = [pl.ds(slot + 4 * ch * CHUNK + j, CHUNK, stride=4) for j in range(4)]
            h = [heads[a, :] for a in at]
            r = [relat[a, :] for a in at]
            t = [tails[a, :] for a in at]
            q = product(h, r, False)
            positive = jnp.sum(q[0] * t[0] + q[1] * t[1] + q[2] * t[2] + q[3] * t[3], axis=1, keepdims=True)
            ql = jnp.concatenate([x.astype(BF16) for x in q], axis=1)
            q_low[rows, :] = ql
            scores = jnp.dot(ql, low_turned[...], preferred_element_type=F32) + bias
            place_in = b * GROUP + ch * CHUNK + lax.broadcasted_iota(I32, (CHUNK, 1), 0)
            live = (place_in < count).astype(F32)
            top = jnp.maximum(positive, jnp.max(scores, axis=1, keepdims=True))
            pos_exp = jnp.exp(positive - top)
            neg_exp = jnp.exp(scores - top)
            total = pos_exp + jnp.sum(neg_exp * counts, axis=1, keepdims=True)
            weight = live / total
            pos_coef = pos_exp * weight - live
            p = (neg_exp * weight).astype(BF16)
            prob[rows, :] = p
            many = p.astype(F32) * counts
            many_high = many.astype(BF16)
            many_low = (many - many_high.astype(F32)).astype(BF16)
            d = jnp.dot(many_high, right_low[...], preferred_element_type=F32) + jnp.dot(
                many_low, right_low[...], preferred_element_type=F32
            )
            dq = [d[:, j * LANES : (j + 1) * LANES] + pos_coef * t[j] for j in range(4)]
            for a, x, y, z in zip(at, product(dq, r, True), product(dq, h, True), q):
                heads[a, :] = x
                relat[a, :] = y
                tails[a, :] = pos_coef * z

        neg_t[...] += counts * lax.dot_general(
            q_low[...], prob[...], (((0,), (0,)), ((), ())), preferred_element_type=F32
        )

        def scatter(n, _):
            for u in range(unroll):
                e = n * unroll + u
                of = pl.ds(pl.multiple_of(slot + 4 * e, 4), 4)
                for to, total, terms in zip(rows_of(b, e), (left_grad, rel_grad, right_grad), (heads, relat, tails)):
                    total[to, :] += terms[of, :]
                fetch(b + 2, after, e)
            return 0

        lax.fori_loop(0, GROUP // unroll, scatter, 0)
        return 0

    lax.fori_loop(0, n_blocks, block, 0)
    rel_out = pltpu.make_async_copy(rel_grad, rel_hbm_grad, sems.at[2])
    rel_out.start()

    def finish(g, _):
        first = pl.multiple_of(g * LANES, LANES)
        to = pl.ds(first, LANES)
        for j, (start, size) in enumerate(((0, 128), (128, 72), (200, 128), (328, 72))):
            at = pl.ds(4 * first + j, LANES, stride=4)
            left_turned[pl.ds(start, size), to] = left_grad[at, :].T[:size]
            right_turned[pl.ds(start, size), to] = (
                right_grad[at, :].T[:size] + neg_t[pl.ds(j * LANES, size), to]
            )
        return 0

    lax.fori_loop(0, E_PART // LANES, finish, 0)
    outs = [
        pltpu.make_async_copy(left_turned, left_hbm_grad, sems.at[0]),
        pltpu.make_async_copy(right_turned, right_hbm_grad, sems.at[1]),
    ]
    for copy in outs:
        copy.start()
    for copy in outs:
        copy.wait()
    rel_out.wait()


def compute(spot, counted, src, rel, dst, neg, left, right, left_sent, right_sent, rels):
    shape = jax.ShapeDtypeStruct
    n = rels.shape[0]
    table = pltpu.VMEM((D, E_PART), F32)
    rows = pltpu.VMEM((4 * E_PART, LANES), F32)
    block = pltpu.VMEM((8 * GROUP, LANES), F32)
    return pl.pallas_call(
        compute_kernel,
        out_shape=(shape((D, E_PART), F32), shape((D, E_PART), F32), shape((n, LANES), F32)),
        in_specs=[SMEM] * 2 + [HBM] * 3 + [VMEM] + [HBM] * 5,
        out_specs=(HBM,) * 3,
        scratch_shapes=[
            table, table, pltpu.VMEM((n, LANES), F32), table, table, rows, rows, pltpu.VMEM((n, LANES), F32),
            rows, rows,
            pltpu.VMEM((E_PART, 512), BF16), pltpu.VMEM((512, E_PART), BF16),
            block, block, block,
            pltpu.VMEM((GROUP, 512), BF16), pltpu.VMEM((GROUP, E_PART), BF16), pltpu.VMEM((512, E_PART), F32),
            pltpu.SMEM((2 * SLOTS,), I32), pltpu.SMEM((2 * SLOTS,), I32), pltpu.SMEM((2 * SLOTS,), I32),
            pltpu.VMEM((6 * SLOTS,), I32),
            pltpu.SemaphoreType.DMA((3,)), pltpu.SemaphoreType.DMA((3,)),
        ],
        compiler_params=pltpu.CompilerParams(vmem_limit_bytes=LIMIT),
        cost_estimate=pl.CostEstimate(flops=20 * 10**9, bytes_accessed=10**8, transcendentals=10**6),
        name="blocks",
    )(spot, counted, src, rel, dst, neg, left, right, left_sent, right_sent, rels)


def exchange_kernel(
    left_grad, right_grad, rel_grad,
    left_sum, right_sum, rel_mine,
    left_own, left_sib, right_own, right_sib, acc, from_core,
    on_up0, on_down0, came_up0, came_down0, on_up2, on_down2, came_up2, came_down2, from_x0, from_x2, from_z0, from_z2, low_z, low_y, low_x,
    ls, lr, ss, sr, cs, cr, ys, yr, xs, xr, zs, zr, local,
):
    y, z, xh, core, xl = place()
    sib, xdev, ydev, zdev = neighbours()
    _, partner, diagonal = family()
    dom = lax.axis_index("dom")
    n_dom = 4 * Y * Z
    pair = dom - core
    barrier = pltpu.get_barrier_semaphore()
    peers = [sib, partner, diagonal] + xdev + ydev + zdev
    for peer in peers:
        pl.semaphore_signal(barrier, inc=1, device_id=peer, device_id_type=MESH)

    @pl.when(core == 0)
    def _():
        for k in (2, 1):
            behind = {"dom": lax.rem(dom + n_dom - k, n_dom), "rep": 1}
            pl.semaphore_signal(barrier, inc=1, device_id=behind, device_id_type=MESH)

    pl.semaphore_wait(barrier, len(peers) + 2 * xl)

    half = D // 2
    mine, other = pl.ds(core * half, half), pl.ds((1 - core) * half, half)
    pairs = []
    for i, (grad, own, recv) in enumerate(((left_grad, left_own, left_sib), (right_grad, right_own, right_sib))):
        keep = pltpu.make_async_copy(grad.at[mine], own, local.at[i])
        keep.start()
        pairs.append((remote(grad.at[other], recv, ss.at[i], sr.at[i], sib), keep))
    cut = [pl.ds(0, 24), pl.ds(24, 8), pl.ds(32, 16)]
    down = [
        remote(rel_grad.at[:, :, :, 1 - core, :, c], from_core.at[:, :, :, :, c], cs.at[i], cr.at[i], sib)
        for i, c in enumerate(cut)
    ]
    keep_rel = pltpu.make_async_copy(rel_grad.at[:, :, :, core], acc, local.at[2])
    keep_rel.start()

    left_to = pair + xl
    right_to = lax.rem(pair + xl + 1, n_dom)
    sends, stays = [], []
    for i, (own, recv, out, to) in enumerate(
        ((left_own, left_sib, left_sum, left_to), (right_own, right_sib, right_sum, right_to))
    ):
        for copy in pairs[i]:
            copy.wait()

        def add(j, _):
            at = pl.ds(pl.multiple_of(8 * j, 8), 8)
            own[at, :] += recv[at, :]
            return 0

        lax.fori_loop(0, half // 8, add, 0)
        part = out.at[mine]
        far = prepared(own, part, ls.at[i, 0], lr.at[i, core, 0], {"dom": to, "rep": 1 - xl})
        near = prepared(own, part, ls.at[i, 1], lr.at[i, core, 1], {"dom": to, "rep": xl})
        stay = pltpu.make_async_copy(own, part, local.at[3 + i])
        far.start()
        self_too = to == dom

        @pl.when(self_too)
        def _():
            stay.start()

        @pl.when(jnp.logical_not(self_too))
        def _():
            near.start()

        sends.append((far, near, stay, self_too))

    keep_rel.wait()
    by_y, by_x, by_z = {0: [], 2: []}, {}, {}
    on_up, on_down = (on_up0, None, on_up2), (on_down0, None, on_down2)
    came_up, came_down = (came_up0, None, came_up2), (came_down0, None, came_down2)
    up, far, below = (lax.rem(y + k, Y) for k in range(1, Y))
    lo, hi = pl.ds(0, 4), pl.ds(4, 4)

    def passing(i, src, dst, to):
        n = 3 * i + len(by_y[i])
        by_y[i].append(remote(src, dst, ys.at[n], yr.at[n], to))

    middle = (from_x0, None, from_x2)
    last = (from_z0, None, from_z2)
    for i, c in enumerate(cut):
        down[i].wait()

        def add_core(n, _):
            at = (n // Z, lax.rem(n, Z), slice(None), slice(None), c)
            acc[at] += from_core[at]
            return 0

        lax.fori_loop(0, Y * Z, add_core, 0)
        if i == 1:
            by_z[i] = [
                remote(acc.at[:, lax.rem(z + k, Z), :, :, c], low_z.at[k - 1], zs.at[6 + k], zr.at[6 + k], zdev[k - 1])
                for k in range(1, Z)
            ]
            continue
        passing(i, acc.at[far, lo, :, :, c], on_up[i], ydev[0])
        passing(i, acc.at[far, hi, :, :, c], on_down[i], ydev[2])
        passing(i, acc.at[up, hi, :, :, c], came_up[i].at[hi], ydev[0])
        passing(i, acc.at[below, lo, :, :, c], came_down[i].at[lo], ydev[2])
    for i in (0, 2):
        c, one, two = cut[i], on_up[i], on_down[i]
        by_y[i][0].wait()

        def add_up(n, _):
            acc[up, n, :, :, c] += one[n]
            return 0

        lax.fori_loop(0, 4, add_up, 0)
        passing(i, acc.at[up, lo, :, :, c], came_up[i].at[lo], ydev[0])
        by_y[i][1].wait()

        def add_down(n, _):
            acc[below, 4 + n, :, :, c] += two[n]
            return 0

        lax.fori_loop(0, 4, add_down, 0)
        passing(i, acc.at[below, hi, :, :, c], came_down[i].at[hi], ydev[2])
    for i in (0, 2):
        c, one, two = cut[i], came_up[i], came_down[i]
        for copy in by_y[i][2:]:
            copy.wait()

        def add_y(n, _):
            acc[y, n, :, :, c] += one[n] + two[n]
            return 0

        lax.fori_loop(0, Z, add_y, 0)
        by_x[i] = []
        for k in range(1, X):
            (a, b), n = shift_x(xh, xl, k), 3 * i + k - 1
            by_x[i].append(remote(acc.at[y, :, a, b, c], middle[i].at[k - 1], xs.at[n], xr.at[n], xdev[k - 1]))
    c = cut[1]
    for copy in by_z[1]:
        copy.wait()

    def add_z(n, _):
        total = acc[n, z, :, :, c]
        for k in range(Z - 1):
            total = total + low_z[k, n]
        acc[n, z, :, :, c] = total
        return 0

    lax.fori_loop(0, Y, add_z, 0)
    by_y[1] = [
        remote(acc.at[lax.rem(y + k, Y), z, :, :, c], low_y.at[k - 1], ys.at[11 + k], yr.at[11 + k], ydev[k - 1])
        for k in range(1, Y)
    ]
    for i in (0, 2):
        c, came = cut[i], middle[i]
        for copy in by_x[i]:
            copy.wait()

        def add_x(n, _):
            acc[y, n, xh, xl, c] += came[0, n] + came[1, n] + came[2, n]
            return 0

        lax.fori_loop(0, Z, add_x, 0)
        by_z[i] = []
        for k in range(1, Z):
            t, n = lax.rem(z + k, Z), 7 * i + k - 1
            by_z[i].append(remote(acc.at[y, t, xh, xl, c], last[i].at[k - 1], zs.at[n], zr.at[n], zdev[k - 1]))
    c = cut[1]
    for copy in by_y[1]:
        copy.wait()
    acc[y, z, :, :, c] += low_y[0] + low_y[1] + low_y[2]
    by_x[1] = []
    for k in range(1, X):
        a, b = shift_x(xh, xl, k)
        by_x[1].append(remote(acc.at[y, z, a, b, c], low_x.at[k - 1], xs.at[2 + k], xr.at[2 + k], xdev[k - 1]))
    for i in (0, 2):
        c = cut[i]
        for copy in by_z[i]:
            copy.wait()
        total = acc[y, z, xh, xl, c]
        for k in range(Z - 1):
            total = total + last[i][k]
        rel_mine[c, :] = total
    for copy in by_x[1]:
        copy.wait()
    rel_mine[cut[1], :] = acc[y, z, xh, xl, cut[1]] + low_x[0] + low_x[1] + low_x[2]

    for far, near, stay, self_too in sends:
        far.wait_send()

        @pl.when(self_too)
        def _():
            stay.wait()

        @pl.when(jnp.logical_not(self_too))
        def _():
            near.wait_send()

    for i, owner in ((0, core), (1, 1 - core)):
        own, out = ((left_own, left_sum), (right_own, right_sum))[i]
        for sender in range(2):
            part = out.at[pl.ds(sender * half, half)]
            local_chip = owner == xl
            to_self = jnp.logical_and(local_chip, jnp.logical_and(sender == core, jnp.logical_or(i == 0, core == 1)))
            came = lambda kind: prepared(own, part, ls.at[i, 0], lr.at[i, sender, kind], sib)

            @pl.when(jnp.logical_not(local_chip))
            def _():
                came(0).wait_recv()

            @pl.when(jnp.logical_and(local_chip, jnp.logical_not(to_self)))
            def _():
                came(1).wait_recv()


def exchange(left_grad, right_grad, rel_grad):
    dma = lambda *n: pltpu.SemaphoreType.DMA(n)
    shape = jax.ShapeDtypeStruct
    table = shape((D, E_PART), F32)
    half = pltpu.VMEM((D // 2, E_PART), F32)
    return pl.pallas_call(
        exchange_kernel,
        out_shape=(table, table, shape((SHARD, LANES), F32)),
        in_specs=[HBM] * 3,
        out_specs=(HBM, HBM, VMEM),
        scratch_shapes=[half] * 4
        + [
            pltpu.VMEM((Y, Z, 2, 2, SHARD, LANES), F32),
            pltpu.VMEM((Y, Z, 2, 2, SHARD, LANES), F32),
            *(pltpu.VMEM((n, 2, 2, rows, LANES), F32) for rows in (24, 16) for n in (4, 4, Z, Z)),
            pltpu.VMEM((3, Z, 24, LANES), F32), pltpu.VMEM((3, Z, 16, LANES), F32),
            pltpu.VMEM((7, 24, LANES), F32), pltpu.VMEM((7, 16, LANES), F32),
            pltpu.VMEM((7, Y, 2, 2, 8, LANES), F32), pltpu.VMEM((3, 2, 2, 8, LANES), F32), pltpu.VMEM((3, 8, LANES), F32),
            dma(2, 2), dma(2, 2, 2), dma(2), dma(2),
            dma(3), dma(3), dma(15), dma(15), dma(9), dma(9), dma(21), dma(21), dma(5),
        ],
        compiler_params=pltpu.CompilerParams(collective_id=1, has_side_effects=True, vmem_limit_bytes=LIMIT),
        name="exchange_gradients",
    )(left_grad, right_grad, rel_grad)


def update_kernel(
    left_hbm, left_state, left_sum_hbm, right_hbm, right_state, right_sum_hbm, rel, rel_state, rel_grad,
    left_next_hbm, left_state_next, right_next_hbm, right_state_next, rel_next, rel_state_next,
    left, left_sum, left_next, right, right_sum, right_next, in_sems, out_sems,
):
    wide = 2 * LANES
    parts = [pl.ds(g * wide, wide) for g in range(E_PART // wide)]
    sides = (
        (left_hbm, left_sum_hbm, left_next_hbm, left, left_sum, left_next, left_state, left_state_next),
        (right_hbm, right_sum_hbm, right_next_hbm, right, right_sum, right_next, right_state, right_state_next),
    )
    loads, stores = [], []
    for i, side in enumerate(sides):
        for g, at in enumerate(parts):
            loads.append([
                pltpu.make_async_copy(side[k].at[:, at], side[3 + k].at[:, at], in_sems.at[i, g, k]) for k in range(2)
            ])
            for copy in loads[-1]:
                copy.start()
    n = rel.shape[0]
    same = lax.broadcasted_iota(I32, (n, n), 0) == lax.broadcasted_iota(I32, (n, n), 1)
    column = lambda row: jnp.sum(jnp.where(same, jnp.broadcast_to(row, (n, n)), 0.0), axis=1, keepdims=True)
    across = lambda col: jnp.sum(jnp.where(same, jnp.broadcast_to(col, (n, n)), 0.0), axis=0, keepdims=True)
    grad = [rel_grad[pl.ds(j, n, stride=4), :] for j in range(4)]
    square = jnp.sum(sum(v * v for v in grad), axis=1, keepdims=True) * (1.0 / D)
    fresh = column(rel_state[...]) + square
    rel_state_next[...] = across(fresh)
    scale = RATE / jnp.sqrt(fresh)
    for j, change in enumerate(natural_of([v * scale for v in grad])):
        cols = pl.ds(j * LANES, change.shape[1])
        rel_next[:, cols] = rel[:, cols] - change
    for i, (_, _, after_hbm, table, total, after, state, state_after) in enumerate(sides):
        for g, at in enumerate(parts):
            for copy in loads[i * len(parts) + g]:
                copy.wait()
            grad = total[:, at]
            fresh = state[:, at] + jnp.sum(grad * grad, axis=0, keepdims=True) * (1.0 / D)
            state_after[:, at] = fresh
            after[:, at] = table[:, at] - grad * (RATE / jnp.sqrt(fresh))
            stores.append(pltpu.make_async_copy(after.at[:, at], after_hbm.at[:, at], out_sems.at[i, g]))
            stores[-1].start()
    for copy in stores:
        copy.wait()


def update(left, left_state, left_sum, right, right_state, right_sum, rel, rel_state, rel_grad):
    shape = jax.ShapeDtypeStruct
    big, row = shape((D, E_PART), F32), shape((1, E_PART), F32)
    side = [HBM, VMEM, HBM]
    return pl.pallas_call(
        update_kernel,
        out_shape=(big, row, big, row, shape(rel.shape, F32), shape(rel_state.shape, F32)),
        in_specs=side * 2 + [VMEM] * 3,
        out_specs=(HBM, VMEM, HBM, VMEM, VMEM, VMEM),
        scratch_shapes=[pltpu.VMEM((D, E_PART), F32)] * 6
        + [pltpu.SemaphoreType.DMA((2, 4, 2)), pltpu.SemaphoreType.DMA((2, 4))],
        compiler_params=pltpu.CompilerParams(vmem_limit_bytes=LIMIT),
        name="adagrad",
    )(left, left_state, left_sum, right, right_state, right_sum, rel, rel_state, rel_grad)


def shards(
    left_table, left_state, right_table, right_state, rel_table, rel_state,
    sources, relations, targets, bucket_counts, negatives,
):
    left, right = left_table.T, right_table.T
    rels, src, rel, dst, neg, counted, spot, left_use, right_use = gather(
        rel_table, sources, relations, targets, negatives, bucket_counts, left, right
    )
    n_dom = 4 * Y * Z
    route = [((i - 1) % n_dom, i) for i in range(n_dom)]
    held, held_state, rels = lax.optimization_barrier((right_table, right_state, rels))
    held = lax.ppermute(held, "dom", route)
    held_state = lax.ppermute(held_state, "dom", route)
    left_grad, right_grad, rel_grad = compute(
        spot, counted, src, rel, dst, neg, left, right, left_use, right_use, rels.reshape(-1, LANES)
    )
    left_sum, right_sum, rel_mine = exchange(
        left_grad, right_grad, rel_grad.reshape(Y, Z, 2, 2, 2, SHARD, LANES)
    )
    left_next, left_after, right_next, right_after, rel_next, rel_after = update(
        left, left_state[None], left_sum, held.T, held_state[None], right_sum, rel_table, rel_state[None], rel_mine
    )
    return left_next.T, left_after[0], right_next.T, right_after[0], rel_next, rel_after[0]


def solution(mesh):
    both = P(("dom", "rep"))
    rows = P(("dom", "rep"), None)
    table, state = P("dom", None), P("dom")
    return jax.shard_map(
        shards,
        mesh=mesh,
        in_specs=(table, state, table, state, rows, both, both, both, both, state, rows),
        out_specs=(table, state, table, state, rows, both),
        check_vma=False,
    )
```

```python
import jax
import jax.numpy as jnp
from jax import lax
from jax.experimental import pallas as pl
from jax.experimental.pallas import tpu as pltpu
from jax.sharding import PartitionSpec as P

RATE = 0.3
D, LANES = 400, 128
E_PART, GROUP, NEG = 1024, 512, 1024
CHUNK = 512
Y, Z, X = 4, 8, 4
SHARD = 48
SLOTS = 4096
F32, BF16, I32 = jnp.float32, jnp.bfloat16, jnp.int32
MESH = pl.DeviceIdType.MESH
VMEM = pl.BlockSpec(memory_space=pltpu.VMEM)
SMEM = pl.BlockSpec(memory_space=pltpu.SMEM)
HBM = pl.BlockSpec(memory_space=pltpu.HBM)
LIMIT = 63 * 2**20


def tiles_of(ref, first, n):
    rows = pl.ds(first, n)
    lane = lax.broadcasted_iota(I32, (n, LANES), 1)
    a, b, c = (ref[rows, pl.ds(j * LANES, LANES)] for j in range(3))
    d = jnp.concatenate([ref[rows, pl.ds(384, 16)], jnp.zeros((n, LANES - 16), F32)], axis=1)
    b1, c1, d1 = (pltpu.roll(v, 56, 1) for v in (b, c, d))
    zero = jnp.zeros((n, LANES), F32)
    return (
        a,
        jnp.where(lane < 72, b, zero),
        jnp.where(lane < 56, b1, c1),
        jnp.where(lane < 56, c1, jnp.where(lane < 72, d1, zero)),
    )


def natural_of(tiles):
    a, b, c, d = tiles
    lane = lax.broadcasted_iota(I32, a.shape, 1)
    c1, d1 = (pltpu.roll(v, 72, 1) for v in (c, d))
    return (a, jnp.where(lane < 72, b, c1), jnp.where(lane < 72, c1, d1), d1[:, :16])


def place():
    dom, xl = lax.axis_index("dom"), lax.axis_index("rep")
    core = lax.rem(dom, 2)
    xh = lax.rem(dom // 2, 2)
    z = lax.rem(dom // 4, Z)
    y = dom // (4 * Z)
    return y, z, xh, core, xl


def device(y, z, xh, core, xl):
    return {"dom": ((y * Z + z) * 2 + xh) * 2 + core, "rep": xl}


def shift_x(xh, xl, k):
    x = lax.rem(xh * 2 + xl + k, X)
    return x // 2, lax.rem(x, 2)


def greet(peers):
    barrier = pltpu.get_barrier_semaphore()
    for peer in peers:
        pl.semaphore_signal(barrier, inc=1, device_id=peer, device_id_type=MESH)
    pl.semaphore_wait(barrier, len(peers))


def neighbours():
    y, z, xh, core, xl = place()
    sib = device(y, z, xh, 1 - core, xl)
    xs = [(*shift_x(xh, xl, k),) for k in range(1, X)]
    xdev = [device(y, z, a, core, b) for a, b in xs]
    ydev = [device(lax.rem(y + k, Y), z, xh, core, xl) for k in range(1, Y)]
    zdev = [device(y, lax.rem(z + k, Z), xh, core, xl) for k in range(1, Z)]
    return sib, xdev, ydev, zdev


def remote(src, dst, send, recv, to):
    copy = pltpu.make_async_remote_copy(
        src_ref=src, dst_ref=dst, send_sem=send, recv_sem=recv, device_id=to, device_id_type=MESH
    )
    copy.start()
    return copy


def family():
    y, z, xh, core, xl = place()
    dom = lax.axis_index("dom")
    twin = dom + 1 - 2 * core
    return {"dom": twin, "rep": xl}, {"dom": dom, "rep": 1 - xl}, {"dom": twin, "rep": 1 - xl}


def prepared(src, dst, send, recv, to):
    return pltpu.make_async_remote_copy(
        src_ref=src, dst_ref=dst, send_sem=send, recv_sem=recv, device_id=to, device_id_type=MESH
    )


def gather_kernel(
    shard, src, rel, dst, neg, count, left, right,
    full, src_all, rel_all, dst_all, neg_all, count_use, spot, left_use, right_use,
    rows, count_rows, zs, zr, ps, pr, cs, cr, es, ea, eb, ts, tr, local,
):
    y, z, xh, core, xl = place()
    sib, xdev, ydev, zdev = neighbours()
    _, partner, diagonal = family()
    greet([sib, partner, diagonal] + xdev + ydev + zdev)
    for j, tile in enumerate(tiles_of(shard, 0, 12)):
        rows[pl.ds(j, 12, stride=4), :] = tile
    first = [remote(rows, full.at[y, z, xh, core, xl], zs.at[k], zr.at[k], zdev[k]) for k in range(Z - 1)]
    own = pltpu.make_async_copy(rows, full.at[y, z, xh, core, xl], local.at[0])
    own.start()
    count_rows[...] = jnp.full((8, LANES), count[0], I32)
    line = lax.broadcasted_iota(I32, (8, LANES), 0)
    spot[...] = jnp.where(line == 0, core, jnp.where(core == xl, 1, 0))

    lists = [
        (v, w.at[pl.ds(xl * n, n)])
        for v, w, n in ((src, src_all, SLOTS), (rel, rel_all, SLOTS), (dst, dst_all, SLOTS), (neg, neg_all, 8))
    ]
    twin = {"dom": sib["dom"], "rep": core}
    same = {"dom": lax.axis_index("dom"), "rep": core}
    cross = [prepared(v, w, es.at[i], eb.at[i, xl], twin) for i, (v, w) in enumerate(lists)]
    straight = [prepared(v, w, es.at[4 + i], ea.at[i], same) for i, (v, w) in enumerate(lists)]
    stay = [pltpu.make_async_copy(v, w, local.at[1 + i]) for i, (v, w) in enumerate(lists)]
    things = ((count_rows, count_use), (left, left_use), (right, right_use))
    tables = [prepared(v, w, ts.at[i], tr.at[i], sib) for i, (v, w) in enumerate(things)]
    stay.append(pltpu.make_async_copy(count_rows, count_use, local.at[5]))
    for copy in cross:
        copy.start()

    @pl.when(core == xl)
    def _():
        for copy in tables + stay:
            copy.start()

    @pl.when(core != xl)
    def _():
        for copy in straight:
            copy.start()

    own.wait()
    for copy in first:
        copy.wait()
    halves = [pl.ds(0, SHARD // 2), pl.ds(SHARD // 2, SHARD // 2)]
    down = []

    def below(ref):
        i = len(down)
        down.append(remote(ref, ref, cs.at[i], cr.at[i], sib))

    below(full.at[y, :, xh, core, xl])
    second = []
    for half, devs in enumerate((ydev, xdev)):
        part = full.at[y, :, xh, core, xl, halves[half]]
        for k in range(3):
            i = half * 3 + k
            second.append(remote(part, part, ps.at[i], pr.at[i], devs[k]))
    for i, copy in enumerate(second):
        copy.wait()
    low, high = 0, 1

    def part(half, k, which):
        if half == 0:
            a, b = shift_x(xh, xl, k)
            return full.at[pl.ds(2 * which, 2), :, a, core, b, halves[0]]
        return full.at[lax.rem(y + k, Y), pl.ds(4 * which, 4), :, core, :, halves[1]]

    third = {}
    ends = ((xdev[0], xdev[2]), (ydev[0], ydev[2]))

    def ring(half, k, which, up):
        i = 6 + len(third)
        ref = part(half, k, which)
        third[half, k, which, up] = remote(ref, ref, ps.at[i], pr.at[i], ends[half][1 - up])

    for up, which in ((1, low), (0, high), (1, high), (0, low)):
        for half in range(2):
            ring(half, 0, which, up)
    for k in range(1, 4):
        below(full.at[lax.rem(y + 4 - k, Y), :, xh, core, xl, halves[0]])
        a, b = shift_x(xh, xl, X - k)
        below(full.at[y, :, a, core, b, halves[1]])
    for half in range(2):
        third[half, 0, low, 1].wait()
        ring(half, 3, low, 1)
        third[half, 0, high, 0].wait()
        ring(half, 1, high, 0)
        below(part(half, 3, low))
        below(part(half, 1, high))
    for half in range(2):
        third[half, 0, high, 1].wait()
        below(part(half, 3, high))
        third[half, 0, low, 0].wait()
        below(part(half, 1, low))
    for half in range(2):
        third[half, 3, low, 1].wait()
        below(part(half, 2, low))
        third[half, 1, high, 0].wait()
        below(part(half, 2, high))
    for copy in down:
        copy.wait()
    for copy in cross:
        copy.wait_send()

    @pl.when(core == xl)
    def _():
        for copy in tables:
            copy.wait_send()
        for copy in straight:
            copy.wait_recv()
        for copy in stay:
            copy.wait()

    @pl.when(core != xl)
    def _():
        for copy in tables:
            copy.wait_recv()
        for copy in straight:
            copy.wait_send()
        for i, (v, w) in enumerate(lists):
            for sender in range(2):
                prepared(v, w, es.at[i], eb.at[i, sender], twin).wait_recv()


def gather(shard, src, rel, dst, neg, count, left, right):
    dma = lambda *n: pltpu.SemaphoreType.DMA(n)
    shape = jax.ShapeDtypeStruct
    return pl.pallas_call(
        gather_kernel,
        out_shape=(
            shape((Y, Z, 2, 2, 2, SHARD, LANES), F32),
            shape((2 * SLOTS,), I32), shape((2 * SLOTS,), I32), shape((2 * SLOTS,), I32),
            shape((16, NEG), I32), shape((8, LANES), I32), shape((8, LANES), I32),
            shape((D, E_PART), F32), shape((D, E_PART), F32),
        ),
        in_specs=[VMEM] + [HBM] * 4 + [SMEM] + [HBM] * 2,
        out_specs=(HBM,) * 6 + (VMEM,) + (HBM,) * 2,
        scratch_shapes=[
            pltpu.VMEM((SHARD, LANES), F32), pltpu.VMEM((8, LANES), I32),
            dma(7), dma(7), dma(18), dma(18), dma(19), dma(19),
            dma(8), dma(4), dma(4, 2), dma(3), dma(3), dma(6),
        ],
        compiler_params=pltpu.CompilerParams(collective_id=0, has_side_effects=True, vmem_limit_bytes=LIMIT),
        name="gather_relations",
    )(shard, src, rel, dst, neg, count, left, right)


def product(a, b, conjugate):
    if conjugate:
        re = lambda i, j: a[i] * b[i] + a[j] * b[j]
        im = lambda i, j: a[j] * b[i] - a[i] * b[j]
    else:
        re = lambda i, j: a[i] * b[i] - a[j] * b[j]
        im = lambda i, j: a[i] * b[j] + a[j] * b[i]
    return (re(0, 2), re(1, 3), im(0, 2), im(1, 3))


def embedding_tiles(ref, g):
    at = pl.ds(pl.multiple_of(g * LANES, LANES), LANES)
    zero = jnp.zeros((56, LANES), F32)
    full = lambda i: ref[pl.ds(i, LANES), at]
    part = lambda i: jnp.concatenate([ref[pl.ds(i, 72), at], zero], axis=0)
    return full(0), part(128), full(200), part(328)


def compute_kernel(
    spot, counted, src_hbm, rel_hbm, dst_hbm, neg, left_here, right_here, left_sent, right_sent, rels_hbm,
    left_hbm_grad, right_hbm_grad, rel_hbm_grad,
    left, right, rels, left_turned, right_turned, left_grad, right_grad, rel_grad,
    left_rows, right_rows, right_low, low_turned, heads, relat, tails, q_low, prob, neg_t, src, rel, dst, ids_in, sems, id_sems,
):
    count, core, at_home = counted[0, 0], spot[0, 0], spot[1, 0]
    n_blocks = (((count + GROUP - 1) >> 9) + 1 - core) >> 1
    tables = ((left_here, left_sent, left), (right_here, right_sent, right))
    loads = [pltpu.make_async_copy(v, w, sems.at[i]) for i, (v, _, w) in enumerate(tables)]
    loads.append(pltpu.make_async_copy(rels_hbm, rels, sems.at[2]))

    @pl.when(at_home == 1)
    def _():
        for copy in loads[:2]:
            copy.start()

    @pl.when(at_home == 0)
    def _():
        for i, (_, v, w) in enumerate(tables):
            pltpu.make_async_copy(v, w, sems.at[i]).start()

    loads[2].start()
    scaled = []
    for i, (v, w) in enumerate(((src_hbm, src), (rel_hbm, rel), (dst_hbm, dst))):
        held = ids_in.at[pl.ds(2 * SLOTS * i, 2 * SLOTS)]
        scaled.append((held, pltpu.make_async_copy(v, held, id_sems.at[i]), pltpu.make_async_copy(held, w, id_sems.at[i])))
        scaled[i][1].start()
    for held, came, goes in scaled:
        came.wait()
        held[...] = held[...] * 4
        goes.start()
    left_grad[...] = jnp.zeros_like(left_grad)
    right_grad[...] = jnp.zeros_like(right_grad)
    rel_grad[...] = jnp.zeros_like(rel_grad)
    neg_t[...] = jnp.zeros_like(neg_t)
    loads[0].wait()
    loads[1].wait()

    def prepare(g, _):
        first = pl.multiple_of(g * LANES, LANES)
        for j, tile in enumerate(embedding_tiles(left, g)):
            left_rows[pl.ds(4 * first + j, LANES, stride=4), :] = tile.T
        for j, tile in enumerate(embedding_tiles(right, g)):
            low_turned[pl.ds(j * LANES, LANES), pl.ds(first, LANES)] = tile.astype(BF16)
            tile = tile.T
            right_rows[pl.ds(4 * first + j, LANES, stride=4), :] = tile
            right_low[pl.ds(first, LANES), pl.ds(j * LANES, LANES)] = tile.astype(BF16)
        return 0

    lax.fori_loop(0, E_PART // LANES, prepare, 0, unroll=True)
    loads[2].wait()
    unroll = 32

    def rows_of(b, e):
        return [pl.ds(pl.multiple_of(ids[b * GROUP + e], 4), 4) for ids in (src, rel, dst)]

    def fetch(b, slot, e):
        s, r, t = rows_of(b, e)
        to = pl.ds(pl.multiple_of(slot + 4 * e, 4), 4)
        heads[to, :] = left_rows[s, :]
        relat[to, :] = rels[r, :]
        tails[to, :] = right_rows[t, :]

    for _, _, goes in scaled:
        goes.wait()

    def first_fetch(n, _):
        for u in range(unroll):
            fetch(core, 0, n * unroll + u)
        return 0

    lax.fori_loop(0, GROUP // unroll, first_fetch, 0)

    def block(i, _):
        b = 2 * i + core
        slot = pl.multiple_of(lax.rem(i, 2) * 4 * GROUP, 4 * GROUP)
        after = pl.multiple_of(4 * GROUP - slot, 4 * GROUP)

        named = neg[pl.ds(b, 1), :]
        high = (lax.broadcasted_iota(I32, (16, NEG), 0) == (named >> 7)).astype(F32).astype(BF16)
        low = (lax.broadcasted_iota(I32, (LANES, NEG), 0) == (named & 127)).astype(F32).astype(BF16)
        table = lax.dot_general(high, low, (((1,), (1,)), ((), ())), preferred_element_type=F32)
        counts = jnp.concatenate([table[h : h + 1, :] for h in range(E_PART // LANES)], axis=1)
        bias = jnp.where(counts > 0, 0.0, -jnp.inf)

        for ch in range(GROUP // CHUNK):
            rows = pl.ds(ch * CHUNK, CHUNK)
            at = [pl.ds(slot + 4 * ch * CHUNK + j, CHUNK, stride=4) for j in range(4)]
            h = [heads[a, :] for a in at]
            r = [relat[a, :] for a in at]
            t = [tails[a, :] for a in at]
            q = product(h, r, False)
            positive = jnp.sum(q[0] * t[0] + q[1] * t[1] + q[2] * t[2] + q[3] * t[3], axis=1, keepdims=True)
            ql = jnp.concatenate([x.astype(BF16) for x in q], axis=1)
            q_low[rows, :] = ql
            scores = jnp.dot(ql, low_turned[...], preferred_element_type=F32) + bias
            place_in = b * GROUP + ch * CHUNK + lax.broadcasted_iota(I32, (CHUNK, 1), 0)
            live = (place_in < count).astype(F32)
            top = jnp.maximum(positive, jnp.max(scores, axis=1, keepdims=True))
            pos_exp = jnp.exp(positive - top)
            neg_exp = jnp.exp(scores - top)
            total = pos_exp + jnp.sum(neg_exp * counts, axis=1, keepdims=True)
            weight = live / total
            pos_coef = pos_exp * weight - live
            p = (neg_exp * weight).astype(BF16)
            prob[rows, :] = p
            many = p.astype(F32) * counts
            many_high = many.astype(BF16)
            many_low = (many - many_high.astype(F32)).astype(BF16)
            d = jnp.dot(many_high, right_low[...], preferred_element_type=F32) + jnp.dot(
                many_low, right_low[...], preferred_element_type=F32
            )
            dq = [d[:, j * LANES : (j + 1) * LANES] + pos_coef * t[j] for j in range(4)]
            for a, x, y, z in zip(at, product(dq, r, True), product(dq, h, True), q):
                heads[a, :] = x
                relat[a, :] = y
                tails[a, :] = pos_coef * z

        neg_t[...] += counts * lax.dot_general(
            q_low[...], prob[...], (((0,), (0,)), ((), ())), preferred_element_type=F32
        )

        def scatter(n, _):
            for u in range(unroll):
                e = n * unroll + u
                of = pl.ds(pl.multiple_of(slot + 4 * e, 4), 4)
                for to, total, terms in zip(rows_of(b, e), (left_grad, rel_grad, right_grad), (heads, relat, tails)):
                    total[to, :] += terms[of, :]
                fetch(b + 2, after, e)
            return 0

        lax.fori_loop(0, GROUP // unroll, scatter, 0)
        return 0

    lax.fori_loop(0, n_blocks, block, 0)
    rel_out = pltpu.make_async_copy(rel_grad, rel_hbm_grad, sems.at[2])
    rel_out.start()

    def finish(g, _):
        first = pl.multiple_of(g * LANES, LANES)
        to = pl.ds(first, LANES)
        for j, (start, size) in enumerate(((0, 128), (128, 72), (200, 128), (328, 72))):
            at = pl.ds(4 * first + j, LANES, stride=4)
            left_turned[pl.ds(start, size), to] = left_grad[at, :].T[:size]
            right_turned[pl.ds(start, size), to] = (
                right_grad[at, :].T[:size] + neg_t[pl.ds(j * LANES, size), to]
            )
        return 0

    lax.fori_loop(0, E_PART // LANES, finish, 0, unroll=True)
    outs = [
        pltpu.make_async_copy(left_turned, left_hbm_grad, sems.at[0]),
        pltpu.make_async_copy(right_turned, right_hbm_grad, sems.at[1]),
    ]
    for copy in outs:
        copy.start()
    for copy in outs:
        copy.wait()
    rel_out.wait()


def compute(spot, counted, src, rel, dst, neg, left, right, left_sent, right_sent, rels):
    shape = jax.ShapeDtypeStruct
    n = rels.shape[0]
    table = pltpu.VMEM((D, E_PART), F32)
    rows = pltpu.VMEM((4 * E_PART, LANES), F32)
    block = pltpu.VMEM((8 * GROUP, LANES), F32)
    return pl.pallas_call(
        compute_kernel,
        out_shape=(shape((D, E_PART), F32), shape((D, E_PART), F32), shape((n, LANES), F32)),
        in_specs=[SMEM] * 2 + [HBM] * 3 + [VMEM] + [HBM] * 5,
        out_specs=(HBM,) * 3,
        scratch_shapes=[
            table, table, pltpu.VMEM((n, LANES), F32), table, table, rows, rows, pltpu.VMEM((n, LANES), F32),
            rows, rows,
            pltpu.VMEM((E_PART, 512), BF16), pltpu.VMEM((512, E_PART), BF16),
            block, block, block,
            pltpu.VMEM((GROUP, 512), BF16), pltpu.VMEM((GROUP, E_PART), BF16), pltpu.VMEM((512, E_PART), F32),
            pltpu.SMEM((2 * SLOTS,), I32), pltpu.SMEM((2 * SLOTS,), I32), pltpu.SMEM((2 * SLOTS,), I32),
            pltpu.VMEM((6 * SLOTS,), I32),
            pltpu.SemaphoreType.DMA((3,)), pltpu.SemaphoreType.DMA((3,)),
        ],
        compiler_params=pltpu.CompilerParams(vmem_limit_bytes=LIMIT),
        cost_estimate=pl.CostEstimate(flops=20 * 10**9, bytes_accessed=10**8, transcendentals=10**6),
        name="blocks",
    )(spot, counted, src, rel, dst, neg, left, right, left_sent, right_sent, rels)


def exchange_kernel(
    left_grad, right_grad, rel_grad,
    left_sum, right_sum, rel_mine,
    left_own, left_sib, right_own, right_sib, acc, from_core,
    on_up0, on_down0, came_up0, came_down0, on_up2, on_down2, came_up2, came_down2, from_x0, from_x2, from_z0, from_z2, low_z, low_y, low_x,
    ls, lr, ss, sr, cs, cr, ys, yr, xs, xr, zs, zr, local,
):
    y, z, xh, core, xl = place()
    sib, xdev, ydev, zdev = neighbours()
    _, partner, diagonal = family()
    dom = lax.axis_index("dom")
    n_dom = 4 * Y * Z
    pair = dom - core
    barrier = pltpu.get_barrier_semaphore()
    peers = [sib, partner, diagonal] + xdev + ydev + zdev
    for peer in peers:
        pl.semaphore_signal(barrier, inc=1, device_id=peer, device_id_type=MESH)

    @pl.when(core == 0)
    def _():
        for k in (2, 1):
            behind = {"dom": lax.rem(dom + n_dom - k, n_dom), "rep": 1}
            pl.semaphore_signal(barrier, inc=1, device_id=behind, device_id_type=MESH)

    pl.semaphore_wait(barrier, len(peers) + 2 * xl)

    cut = [pl.ds(0, 24), pl.ds(24, 8), pl.ds(32, 16)]
    down = [
        remote(rel_grad.at[:, :, :, 1 - core, :, c], from_core.at[:, :, :, :, c], cs.at[i], cr.at[i], sib)
        for i, c in enumerate(cut)
    ]
    keep_rel = pltpu.make_async_copy(rel_grad.at[:, :, :, core], acc, local.at[2])
    keep_rel.start()
    half = D // 2
    mine, other = pl.ds(core * half, half), pl.ds((1 - core) * half, half)
    pairs = []
    for i, (grad, own, recv) in enumerate(((left_grad, left_own, left_sib), (right_grad, right_own, right_sib))):
        keep = pltpu.make_async_copy(grad.at[mine], own, local.at[i])
        keep.start()
        pairs.append((remote(grad.at[other], recv, ss.at[i], sr.at[i], sib), keep))

    keep_rel.wait()
    by_y, by_x, by_z = {0: [], 2: []}, {}, {}
    on_up, on_down = (on_up0, None, on_up2), (on_down0, None, on_down2)
    came_up, came_down = (came_up0, None, came_up2), (came_down0, None, came_down2)
    up, far, below = (lax.rem(y + k, Y) for k in range(1, Y))
    lo, hi = pl.ds(0, 4), pl.ds(4, 4)

    def passing(i, src, dst, to):
        n = 3 * i + len(by_y[i])
        by_y[i].append(remote(src, dst, ys.at[n], yr.at[n], to))

    middle = (from_x0, None, from_x2)
    last = (from_z0, None, from_z2)
    for i, c in enumerate(cut):
        down[i].wait()

        def add_core(n, _):
            at = (n // Z, lax.rem(n, Z), slice(None), slice(None), c)
            acc[at] += from_core[at]
            return 0

        lax.fori_loop(0, Y * Z, add_core, 0)
        if i == 1:
            by_z[i] = [
                remote(acc.at[:, lax.rem(z + k, Z), :, :, c], low_z.at[k - 1], zs.at[6 + k], zr.at[6 + k], zdev[k - 1])
                for k in range(1, Z)
            ]
            continue
        passing(i, acc.at[far, lo, :, :, c], on_up[i], ydev[0])
        passing(i, acc.at[far, hi, :, :, c], on_down[i], ydev[2])
        passing(i, acc.at[up, hi, :, :, c], came_up[i].at[hi], ydev[0])
        passing(i, acc.at[below, lo, :, :, c], came_down[i].at[lo], ydev[2])
    left_to = pair + xl
    right_to = lax.rem(pair + xl + 1, n_dom)
    sends, stays = [], []
    for i, (own, recv, out, to) in enumerate(
        ((left_own, left_sib, left_sum, left_to), (right_own, right_sib, right_sum, right_to))
    ):
        for copy in pairs[i]:
            copy.wait()

        def add(j, _):
            at = pl.ds(pl.multiple_of(8 * j, 8), 8)
            own[at, :] += recv[at, :]
            return 0

        lax.fori_loop(0, half // 8, add, 0)
        part = out.at[mine]
        far = prepared(own, part, ls.at[i, 0], lr.at[i, core, 0], {"dom": to, "rep": 1 - xl})
        near = prepared(own, part, ls.at[i, 1], lr.at[i, core, 1], {"dom": to, "rep": xl})
        stay = pltpu.make_async_copy(own, part, local.at[3 + i])
        far.start()
        self_too = to == dom

        @pl.when(self_too)
        def _():
            stay.start()

        @pl.when(jnp.logical_not(self_too))
        def _():
            near.start()

        sends.append((far, near, stay, self_too))

    for i in (0, 2):
        c, one, two = cut[i], on_up[i], on_down[i]
        by_y[i][0].wait()

        def add_up(n, _):
            acc[up, n, :, :, c] += one[n]
            return 0

        lax.fori_loop(0, 4, add_up, 0)
        passing(i, acc.at[up, lo, :, :, c], came_up[i].at[lo], ydev[0])
        by_y[i][1].wait()

        def add_down(n, _):
            acc[below, 4 + n, :, :, c] += two[n]
            return 0

        lax.fori_loop(0, 4, add_down, 0)
        passing(i, acc.at[below, hi, :, :, c], came_down[i].at[hi], ydev[2])
    for i in (0, 2):
        c, one, two = cut[i], came_up[i], came_down[i]
        for copy in by_y[i][2:]:
            copy.wait()

        def add_y(n, _):
            acc[y, n, :, :, c] += one[n] + two[n]
            return 0

        lax.fori_loop(0, Z, add_y, 0)
        by_x[i] = []
        for k in range(1, X):
            (a, b), n = shift_x(xh, xl, k), 3 * i + k - 1
            by_x[i].append(remote(acc.at[y, :, a, b, c], middle[i].at[k - 1], xs.at[n], xr.at[n], xdev[k - 1]))
    c = cut[1]
    for copy in by_z[1]:
        copy.wait()

    def add_z(n, _):
        total = acc[n, z, :, :, c]
        for k in range(Z - 1):
            total = total + low_z[k, n]
        acc[n, z, :, :, c] = total
        return 0

    lax.fori_loop(0, Y, add_z, 0)
    by_y[1] = [
        remote(acc.at[lax.rem(y + k, Y), z, :, :, c], low_y.at[k - 1], ys.at[11 + k], yr.at[11 + k], ydev[k - 1])
        for k in range(1, Y)
    ]
    for i in (0, 2):
        c, came = cut[i], middle[i]
        for copy in by_x[i]:
            copy.wait()

        def add_x(n, _):
            acc[y, n, xh, xl, c] += came[0, n] + came[1, n] + came[2, n]
            return 0

        lax.fori_loop(0, Z, add_x, 0)
        by_z[i] = []
        for k in range(1, Z):
            t, n = lax.rem(z + k, Z), 7 * i + k - 1
            by_z[i].append(remote(acc.at[y, t, xh, xl, c], last[i].at[k - 1], zs.at[n], zr.at[n], zdev[k - 1]))
    c = cut[1]
    for copy in by_y[1]:
        copy.wait()
    acc[y, z, :, :, c] += low_y[0] + low_y[1] + low_y[2]
    by_x[1] = []
    for k in range(1, X):
        a, b = shift_x(xh, xl, k)
        by_x[1].append(remote(acc.at[y, z, a, b, c], low_x.at[k - 1], xs.at[2 + k], xr.at[2 + k], xdev[k - 1]))
    for i in (0, 2):
        c = cut[i]
        for copy in by_z[i]:
            copy.wait()
        total = acc[y, z, xh, xl, c]
        for k in range(Z - 1):
            total = total + last[i][k]
        rel_mine[c, :] = total
    for copy in by_x[1]:
        copy.wait()
    rel_mine[cut[1], :] = acc[y, z, xh, xl, cut[1]] + low_x[0] + low_x[1] + low_x[2]

    for far, near, stay, self_too in sends:
        far.wait_send()

        @pl.when(self_too)
        def _():
            stay.wait()

        @pl.when(jnp.logical_not(self_too))
        def _():
            near.wait_send()

    for i, owner in ((0, core), (1, 1 - core)):
        own, out = ((left_own, left_sum), (right_own, right_sum))[i]
        for sender in range(2):
            part = out.at[pl.ds(sender * half, half)]
            local_chip = owner == xl
            to_self = jnp.logical_and(local_chip, jnp.logical_and(sender == core, jnp.logical_or(i == 0, core == 1)))
            came = lambda kind: prepared(own, part, ls.at[i, 0], lr.at[i, sender, kind], sib)

            @pl.when(jnp.logical_not(local_chip))
            def _():
                came(0).wait_recv()

            @pl.when(jnp.logical_and(local_chip, jnp.logical_not(to_self)))
            def _():
                came(1).wait_recv()


def exchange(left_grad, right_grad, rel_grad):
    dma = lambda *n: pltpu.SemaphoreType.DMA(n)
    shape = jax.ShapeDtypeStruct
    table = shape((D, E_PART), F32)
    half = pltpu.VMEM((D // 2, E_PART), F32)
    return pl.pallas_call(
        exchange_kernel,
        out_shape=(table, table, shape((SHARD, LANES), F32)),
        in_specs=[HBM] * 3,
        out_specs=(HBM, HBM, VMEM),
        scratch_shapes=[half] * 4
        + [
            pltpu.VMEM((Y, Z, 2, 2, SHARD, LANES), F32),
            pltpu.VMEM((Y, Z, 2, 2, SHARD, LANES), F32),
            *(pltpu.VMEM((n, 2, 2, rows, LANES), F32) for rows in (24, 16) for n in (4, 4, Z, Z)),
            pltpu.VMEM((3, Z, 24, LANES), F32), pltpu.VMEM((3, Z, 16, LANES), F32),
            pltpu.VMEM((7, 24, LANES), F32), pltpu.VMEM((7, 16, LANES), F32),
            pltpu.VMEM((7, Y, 2, 2, 8, LANES), F32), pltpu.VMEM((3, 2, 2, 8, LANES), F32), pltpu.VMEM((3, 8, LANES), F32),
            dma(2, 2), dma(2, 2, 2), dma(2), dma(2),
            dma(3), dma(3), dma(15), dma(15), dma(9), dma(9), dma(21), dma(21), dma(5),
        ],
        compiler_params=pltpu.CompilerParams(collective_id=1, has_side_effects=True, vmem_limit_bytes=LIMIT),
        name="exchange_gradients",
    )(left_grad, right_grad, rel_grad)


def update_kernel(
    left, left_state, left_sum, right, right_state, right_sum, rel, rel_state, rel_grad,
    left_next, left_state_next, right_next, right_state_next, rel_next, rel_state_next,
):
    for table, state, total, after, state_after in (
        (left, left_state, left_sum, left_next, left_state_next),
        (right, right_state, right_sum, right_next, right_state_next),
    ):
        grad = total[...]
        fresh = state[...] + jnp.sum(grad * grad, axis=0, keepdims=True) * (1.0 / D)
        state_after[...] = fresh
        after[...] = table[...] - grad * (RATE / jnp.sqrt(fresh))

    @pl.when(pl.program_id(0) == 0)
    def _():
        n = rel.shape[0]
        same = lax.broadcasted_iota(I32, (n, n), 0) == lax.broadcasted_iota(I32, (n, n), 1)
        column = lambda row: jnp.sum(jnp.where(same, jnp.broadcast_to(row, (n, n)), 0.0), axis=1, keepdims=True)
        across = lambda col: jnp.sum(jnp.where(same, jnp.broadcast_to(col, (n, n)), 0.0), axis=0, keepdims=True)
        grad = [rel_grad[pl.ds(j, n, stride=4), :] for j in range(4)]
        square = jnp.sum(sum(v * v for v in grad), axis=1, keepdims=True) * (1.0 / D)
        fresh = column(rel_state[...]) + square
        rel_state_next[...] = across(fresh)
        scale = RATE / jnp.sqrt(fresh)
        for j, change in enumerate(natural_of([v * scale for v in grad])):
            cols = pl.ds(j * LANES, change.shape[1])
            rel_next[:, cols] = rel[:, cols] - change


def update(left, left_state, left_sum, right, right_state, right_sum, rel, rel_state, rel_grad):
    wide = 4 * LANES
    table = pl.BlockSpec((D, wide), lambda g: (0, g))
    state = pl.BlockSpec((1, wide), lambda g: (0, g))
    whole = lambda shape: pl.BlockSpec(shape, lambda g: (0, 0))
    shape = jax.ShapeDtypeStruct
    big, row = shape((D, E_PART), F32), shape((1, E_PART), F32)
    return pl.pallas_call(
        update_kernel,
        grid=(E_PART // wide,),
        out_shape=(big, row, big, row, shape(rel.shape, F32), shape(rel_state.shape, F32)),
        in_specs=[table, state, table] * 2 + [whole(rel.shape), whole(rel_state.shape), whole((SHARD, LANES))],
        out_specs=(table, state, table, state, whole(rel.shape), whole(rel_state.shape)),
        compiler_params=pltpu.CompilerParams(vmem_limit_bytes=LIMIT),
        name="adagrad",
    )(left, left_state, left_sum, right, right_state, right_sum, rel, rel_state, rel_grad)


def shards(
    left_table, left_state, right_table, right_state, rel_table, rel_state,
    sources, relations, targets, bucket_counts, negatives,
):
    left, right = left_table.T, right_table.T
    rels, src, rel, dst, neg, counted, spot, left_use, right_use = gather(
        rel_table, sources, relations, targets, negatives, bucket_counts, left, right
    )
    n_dom = 4 * Y * Z
    route = [((i - 1) % n_dom, i) for i in range(n_dom)]
    held, held_state, rels = lax.optimization_barrier((right_table, right_state, rels))
    held = lax.ppermute(held, "dom", route)
    held_state = lax.ppermute(held_state, "dom", route)
    left_grad, right_grad, rel_grad = compute(
        spot, counted, src, rel, dst, neg, left, right, left_use, right_use, rels.reshape(-1, LANES)
    )
    held, held_state, rel_grad = lax.optimization_barrier((held, held_state, rel_grad))
    left_sum, right_sum, rel_mine = exchange(
        left_grad, right_grad, rel_grad.reshape(Y, Z, 2, 2, 2, SHARD, LANES)
    )
    left_next, left_after, right_next, right_after, rel_next, rel_after = update(
        left, left_state[None], left_sum, held.T, held_state[None], right_sum, rel_table, rel_state[None], rel_mine
    )
    return left_next.T, left_after[0], right_next.T, right_after[0], rel_next, rel_after[0]


def solution(mesh):
    both = P(("dom", "rep"))
    rows = P(("dom", "rep"), None)
    table, state = P("dom", None), P("dom")
    return jax.shard_map(
        shards,
        mesh=mesh,
        in_specs=(table, state, table, state, rows, both, both, both, both, state, rows),
        out_specs=(table, state, table, state, rows, both),
        check_vma=False,
    )
```

```python
import jax
import jax.numpy as jnp
from jax import lax
from jax.experimental import pallas as pl
from jax.experimental.pallas import tpu as pltpu
from jax.sharding import PartitionSpec as P

RATE = 0.3
D, LANES = 400, 128
E_PART, GROUP, NEG = 1024, 512, 1024
CHUNK = 512
Y, Z, X = 4, 8, 4
SHARD = 48
SLOTS = 4096
F32, BF16, I32 = jnp.float32, jnp.bfloat16, jnp.int32
MESH = pl.DeviceIdType.MESH
VMEM = pl.BlockSpec(memory_space=pltpu.VMEM)
SMEM = pl.BlockSpec(memory_space=pltpu.SMEM)
HBM = pl.BlockSpec(memory_space=pltpu.HBM)
LIMIT = 63 * 2**20


def tiles_of(ref, first, n):
    rows = pl.ds(first, n)
    lane = lax.broadcasted_iota(I32, (n, LANES), 1)
    a, b, c = (ref[rows, pl.ds(j * LANES, LANES)] for j in range(3))
    d = jnp.concatenate([ref[rows, pl.ds(384, 16)], jnp.zeros((n, LANES - 16), F32)], axis=1)
    b1, c1, d1 = (pltpu.roll(v, 56, 1) for v in (b, c, d))
    zero = jnp.zeros((n, LANES), F32)
    return (
        a,
        jnp.where(lane < 72, b, zero),
        jnp.where(lane < 56, b1, c1),
        jnp.where(lane < 56, c1, jnp.where(lane < 72, d1, zero)),
    )


def natural_of(tiles):
    a, b, c, d = tiles
    lane = lax.broadcasted_iota(I32, a.shape, 1)
    c1, d1 = (pltpu.roll(v, 72, 1) for v in (c, d))
    return (a, jnp.where(lane < 72, b, c1), jnp.where(lane < 72, c1, d1), d1[:, :16])


def place():
    dom, xl = lax.axis_index("dom"), lax.axis_index("rep")
    core = lax.rem(dom, 2)
    xh = lax.rem(dom // 2, 2)
    z = lax.rem(dom // 4, Z)
    y = dom // (4 * Z)
    return y, z, xh, core, xl


def device(y, z, xh, core, xl):
    return {"dom": ((y * Z + z) * 2 + xh) * 2 + core, "rep": xl}


def shift_x(xh, xl, k):
    x = lax.rem(xh * 2 + xl + k, X)
    return x // 2, lax.rem(x, 2)


def greet(peers):
    barrier = pltpu.get_barrier_semaphore()
    for peer in peers:
        pl.semaphore_signal(barrier, inc=1, device_id=peer, device_id_type=MESH)
    pl.semaphore_wait(barrier, len(peers))


def neighbours():
    y, z, xh, core, xl = place()
    sib = device(y, z, xh, 1 - core, xl)
    xs = [(*shift_x(xh, xl, k),) for k in range(1, X)]
    xdev = [device(y, z, a, core, b) for a, b in xs]
    ydev = [device(lax.rem(y + k, Y), z, xh, core, xl) for k in range(1, Y)]
    zdev = [device(y, lax.rem(z + k, Z), xh, core, xl) for k in range(1, Z)]
    return sib, xdev, ydev, zdev


def remote(src, dst, send, recv, to):
    copy = pltpu.make_async_remote_copy(
        src_ref=src, dst_ref=dst, send_sem=send, recv_sem=recv, device_id=to, device_id_type=MESH
    )
    copy.start()
    return copy


def family():
    y, z, xh, core, xl = place()
    dom = lax.axis_index("dom")
    twin = dom + 1 - 2 * core
    return {"dom": twin, "rep": xl}, {"dom": dom, "rep": 1 - xl}, {"dom": twin, "rep": 1 - xl}


def prepared(src, dst, send, recv, to):
    return pltpu.make_async_remote_copy(
        src_ref=src, dst_ref=dst, send_sem=send, recv_sem=recv, device_id=to, device_id_type=MESH
    )


def gather_kernel(
    shard, src, rel, dst, neg, count, left, right,
    full, src_all, rel_all, dst_all, neg_all, count_use, spot, left_use, right_use,
    rows, count_rows, zs, zr, ps, pr, cs, cr, es, ea, eb, ts, tr, local,
):
    y, z, xh, core, xl = place()
    sib, xdev, ydev, zdev = neighbours()
    _, partner, diagonal = family()
    greet([sib, partner, diagonal] + xdev + ydev + zdev)
    for j, tile in enumerate(tiles_of(shard, 0, 12)):
        rows[pl.ds(j, 12, stride=4), :] = tile
    first = [remote(rows, full.at[y, z, xh, core, xl], zs.at[k], zr.at[k], zdev[k]) for k in range(Z - 1)]
    own = pltpu.make_async_copy(rows, full.at[y, z, xh, core, xl], local.at[0])
    own.start()
    count_rows[...] = jnp.full((8, LANES), count[0], I32)
    line = lax.broadcasted_iota(I32, (8, LANES), 0)
    spot[...] = jnp.where(line == 0, core, jnp.where(core == xl, 1, 0))

    lists = [
        (v, w.at[pl.ds(xl * n, n)])
        for v, w, n in ((src, src_all, SLOTS), (rel, rel_all, SLOTS), (dst, dst_all, SLOTS), (neg, neg_all, 8))
    ]
    twin = {"dom": sib["dom"], "rep": core}
    same = {"dom": lax.axis_index("dom"), "rep": core}
    cross = [prepared(v, w, es.at[i], eb.at[i, xl], twin) for i, (v, w) in enumerate(lists)]
    straight = [prepared(v, w, es.at[4 + i], ea.at[i], same) for i, (v, w) in enumerate(lists)]
    stay = [pltpu.make_async_copy(v, w, local.at[1 + i]) for i, (v, w) in enumerate(lists)]
    things = ((count_rows, count_use), (left, left_use), (right, right_use))
    tables = [prepared(v, w, ts.at[i], tr.at[i], sib) for i, (v, w) in enumerate(things)]
    stay.append(pltpu.make_async_copy(count_rows, count_use, local.at[5]))
    for copy in cross:
        copy.start()

    @pl.when(core == xl)
    def _():
        for copy in tables + stay:
            copy.start()

    @pl.when(core != xl)
    def _():
        for copy in straight:
            copy.start()

    own.wait()
    for copy in first:
        copy.wait()
    halves = [pl.ds(0, SHARD // 2), pl.ds(SHARD // 2, SHARD // 2)]
    down = []

    def below(ref):
        i = len(down)
        down.append(remote(ref, ref, cs.at[i], cr.at[i], sib))

    below(full.at[y, :, xh, core, xl])
    second = []
    for half, devs in enumerate((ydev, xdev)):
        part = full.at[y, :, xh, core, xl, halves[half]]
        for k in range(3):
            i = half * 3 + k
            second.append(remote(part, part, ps.at[i], pr.at[i], devs[k]))
    for i, copy in enumerate(second):
        copy.wait()
    low, high = 0, 1

    def part(half, k, which):
        if half == 0:
            a, b = shift_x(xh, xl, k)
            return full.at[pl.ds(2 * which, 2), :, a, core, b, halves[0]]
        return full.at[lax.rem(y + k, Y), pl.ds(4 * which, 4), :, core, :, halves[1]]

    third = {}
    ends = ((xdev[0], xdev[2]), (ydev[0], ydev[2]))

    def ring(half, k, which, up):
        i = 6 + len(third)
        ref = part(half, k, which)
        third[half, k, which, up] = remote(ref, ref, ps.at[i], pr.at[i], ends[half][1 - up])

    for up, which in ((1, low), (0, high), (1, high), (0, low)):
        for half in range(2):
            ring(half, 0, which, up)
    for k in range(1, 4):
        below(full.at[lax.rem(y + 4 - k, Y), :, xh, core, xl, halves[0]])
        a, b = shift_x(xh, xl, X - k)
        below(full.at[y, :, a, core, b, halves[1]])
    for half in range(2):
        third[half, 0, low, 1].wait()
        ring(half, 3, low, 1)
        third[half, 0, high, 0].wait()
        ring(half, 1, high, 0)
        below(part(half, 3, low))
        below(part(half, 1, high))
    for half in range(2):
        third[half, 0, high, 1].wait()
        below(part(half, 3, high))
        third[half, 0, low, 0].wait()
        below(part(half, 1, low))
    for half in range(2):
        third[half, 3, low, 1].wait()
        below(part(half, 2, low))
        third[half, 1, high, 0].wait()
        below(part(half, 2, high))
    for copy in down:
        copy.wait()
    for copy in cross:
        copy.wait_send()

    @pl.when(core == xl)
    def _():
        for copy in tables:
            copy.wait_send()
        for copy in straight:
            copy.wait_recv()
        for copy in stay:
            copy.wait()

    @pl.when(core != xl)
    def _():
        for copy in tables:
            copy.wait_recv()
        for copy in straight:
            copy.wait_send()
        for i, (v, w) in enumerate(lists):
            for sender in range(2):
                prepared(v, w, es.at[i], eb.at[i, sender], twin).wait_recv()


def gather(shard, src, rel, dst, neg, count, left, right):
    dma = lambda *n: pltpu.SemaphoreType.DMA(n)
    shape = jax.ShapeDtypeStruct
    return pl.pallas_call(
        gather_kernel,
        out_shape=(
            shape((Y, Z, 2, 2, 2, SHARD, LANES), F32),
            shape((2 * SLOTS,), I32), shape((2 * SLOTS,), I32), shape((2 * SLOTS,), I32),
            shape((16, NEG), I32), shape((8, LANES), I32), shape((8, LANES), I32),
            shape((D, E_PART), F32), shape((D, E_PART), F32),
        ),
        in_specs=[VMEM] + [HBM] * 4 + [SMEM] + [HBM] * 2,
        out_specs=(HBM,) * 6 + (VMEM,) + (HBM,) * 2,
        scratch_shapes=[
            pltpu.VMEM((SHARD, LANES), F32), pltpu.VMEM((8, LANES), I32),
            dma(7), dma(7), dma(18), dma(18), dma(19), dma(19),
            dma(8), dma(4), dma(4, 2), dma(3), dma(3), dma(6),
        ],
        compiler_params=pltpu.CompilerParams(collective_id=0, has_side_effects=True, vmem_limit_bytes=LIMIT),
        name="gather_relations",
    )(shard, src, rel, dst, neg, count, left, right)


def product(a, b, conjugate):
    if conjugate:
        re = lambda i, j: a[i] * b[i] + a[j] * b[j]
        im = lambda i, j: a[j] * b[i] - a[i] * b[j]
    else:
        re = lambda i, j: a[i] * b[i] - a[j] * b[j]
        im = lambda i, j: a[i] * b[j] + a[j] * b[i]
    return (re(0, 2), re(1, 3), im(0, 2), im(1, 3))


def embedding_tiles(ref, g):
    at = pl.ds(pl.multiple_of(g * LANES, LANES), LANES)
    zero = jnp.zeros((56, LANES), F32)
    full = lambda i: ref[pl.ds(i, LANES), at]
    part = lambda i: jnp.concatenate([ref[pl.ds(i, 72), at], zero], axis=0)
    return full(0), part(128), full(200), part(328)


def compute_kernel(
    spot, counted, src_hbm, rel_hbm, dst_hbm, neg, left_here, right_here, left_sent, right_sent, rels_hbm,
    left_hbm_grad, right_hbm_grad, rel_hbm_grad,
    left, right, rels, left_turned, right_turned, left_grad, right_grad, rel_grad,
    left_rows, right_rows, right_low, heads, relat, tails, q_low, prob, neg_t, src, rel, dst, ids_in, sems, id_sems,
):
    count, core, at_home = counted[0, 0], spot[0, 0], spot[1, 0]
    n_blocks = (((count + GROUP - 1) >> 9) + 1 - core) >> 1
    tables = ((left_here, left_sent, left), (right_here, right_sent, right))
    loads = [pltpu.make_async_copy(v, w, sems.at[i]) for i, (v, _, w) in enumerate(tables)]
    loads.append(pltpu.make_async_copy(rels_hbm, rels, sems.at[2]))

    @pl.when(at_home == 1)
    def _():
        for copy in loads[:2]:
            copy.start()

    @pl.when(at_home == 0)
    def _():
        for i, (_, v, w) in enumerate(tables):
            pltpu.make_async_copy(v, w, sems.at[i]).start()

    loads[2].start()
    scaled = []
    for i, (v, w) in enumerate(((src_hbm, src), (rel_hbm, rel), (dst_hbm, dst))):
        held = ids_in.at[pl.ds(2 * SLOTS * i, 2 * SLOTS)]
        scaled.append((held, pltpu.make_async_copy(v, held, id_sems.at[i]), pltpu.make_async_copy(held, w, id_sems.at[i])))
        scaled[i][1].start()
    for held, came, goes in scaled:
        came.wait()
        held[...] = held[...] * 4
        goes.start()
    left_grad[...] = jnp.zeros_like(left_grad)
    right_grad[...] = jnp.zeros_like(right_grad)
    rel_grad[...] = jnp.zeros_like(rel_grad)
    neg_t[...] = jnp.zeros_like(neg_t)
    loads[0].wait()
    loads[1].wait()

    def prepare(g, _):
        first = pl.multiple_of(g * LANES, LANES)
        for j, tile in enumerate(embedding_tiles(left, g)):
            left_rows[pl.ds(4 * first + j, LANES, stride=4), :] = tile.T
        for j, tile in enumerate(embedding_tiles(right, g)):
            tile = tile.T
            right_rows[pl.ds(4 * first + j, LANES, stride=4), :] = tile
            right_low[pl.ds(first, LANES), pl.ds(j * LANES, LANES)] = tile.astype(BF16)
        return 0

    lax.fori_loop(0, E_PART // LANES, prepare, 0, unroll=True)
    loads[2].wait()
    unroll = 32

    def rows_of(b, e):
        return [pl.ds(pl.multiple_of(ids[b * GROUP + e], 4), 4) for ids in (src, rel, dst)]

    def fetch(b, slot, e):
        s, r, t = rows_of(b, e)
        to = pl.ds(pl.multiple_of(slot + 4 * e, 4), 4)
        heads[to, :] = left_rows[s, :]
        relat[to, :] = rels[r, :]
        tails[to, :] = right_rows[t, :]

    for _, _, goes in scaled:
        goes.wait()

    def first_fetch(n, _):
        for u in range(unroll):
            fetch(core, 0, n * unroll + u)
        return 0

    lax.fori_loop(0, GROUP // unroll, first_fetch, 0)

    def block(i, _):
        b = 2 * i + core
        slot = pl.multiple_of(lax.rem(i, 2) * 4 * GROUP, 4 * GROUP)
        after = pl.multiple_of(4 * GROUP - slot, 4 * GROUP)

        named = neg[pl.ds(b, 1), :]
        high = (lax.broadcasted_iota(I32, (16, NEG), 0) == (named >> 7)).astype(F32).astype(BF16)
        low = (lax.broadcasted_iota(I32, (LANES, NEG), 0) == (named & 127)).astype(F32).astype(BF16)
        table = lax.dot_general(high, low, (((1,), (1,)), ((), ())), preferred_element_type=F32)
        counts = jnp.concatenate([table[h : h + 1, :] for h in range(E_PART // LANES)], axis=1)
        bias = jnp.where(counts > 0, 0.0, -jnp.inf)

        for ch in range(GROUP // CHUNK):
            rows = pl.ds(ch * CHUNK, CHUNK)
            at = [pl.ds(slot + 4 * ch * CHUNK + j, CHUNK, stride=4) for j in range(4)]
            h = [heads[a, :] for a in at]
            r = [relat[a, :] for a in at]
            t = [tails[a, :] for a in at]
            q = product(h, r, False)
            positive = jnp.sum(q[0] * t[0] + q[1] * t[1] + q[2] * t[2] + q[3] * t[3], axis=1, keepdims=True)
            ql = jnp.concatenate([x.astype(BF16) for x in q], axis=1)
            q_low[rows, :] = ql
            scores = lax.dot_general(
                ql, right_low[...], (((1,), (1,)), ((), ())), preferred_element_type=F32
            ) + bias
            place_in = b * GROUP + ch * CHUNK + lax.broadcasted_iota(I32, (CHUNK, 1), 0)
            live = (place_in < count).astype(F32)
            top = jnp.maximum(positive, jnp.max(scores, axis=1, keepdims=True))
            pos_exp = jnp.exp(positive - top)
            neg_exp = jnp.exp(scores - top)
            total = pos_exp + jnp.sum(neg_exp * counts, axis=1, keepdims=True)
            weight = live / total
            pos_coef = pos_exp * weight - live
            p = (neg_exp * weight).astype(BF16)
            prob[rows, :] = p
            many = p.astype(F32) * counts
            many_high = many.astype(BF16)
            many_low = (many - many_high.astype(F32)).astype(BF16)
            d = jnp.dot(many_high, right_low[...], preferred_element_type=F32) + jnp.dot(
                many_low, right_low[...], preferred_element_type=F32
            )
            dq = [d[:, j * LANES : (j + 1) * LANES] + pos_coef * t[j] for j in range(4)]
            for a, x, y, z in zip(at, product(dq, r, True), product(dq, h, True), q):
                heads[a, :] = x
                relat[a, :] = y
                tails[a, :] = pos_coef * z

        neg_t[...] += counts * lax.dot_general(
            q_low[...], prob[...], (((0,), (0,)), ((), ())), preferred_element_type=F32
        )

        def scatter(n, _):
            for u in range(unroll):
                e = n * unroll + u
                of = pl.ds(pl.multiple_of(slot + 4 * e, 4), 4)
                for to, total, terms in zip(rows_of(b, e), (left_grad, rel_grad, right_grad), (heads, relat, tails)):
                    total[to, :] += terms[of, :]
                fetch(b + 2, after, e)
            return 0

        lax.fori_loop(0, GROUP // unroll, scatter, 0)
        return 0

    lax.fori_loop(0, n_blocks, block, 0)
    rel_out = pltpu.make_async_copy(rel_grad, rel_hbm_grad, sems.at[2])
    rel_out.start()

    outs = [
        pltpu.make_async_copy(left_turned, left_hbm_grad, sems.at[0]),
        pltpu.make_async_copy(right_turned, right_hbm_grad, sems.at[1]),
    ]
    for grad, turned, copy in ((left_grad, left_turned, outs[0]), (right_grad, right_turned, outs[1])):
        for g in range(E_PART // LANES):
            to = pl.ds(g * LANES, LANES)
            for j, (start, size) in enumerate(((0, 128), (128, 72), (200, 128), (328, 72))):
                part = grad[pl.ds(4 * g * LANES + j, LANES, stride=4), :].T[:size]
                if grad is right_grad:
                    part += neg_t[pl.ds(j * LANES, size), to]
                turned[pl.ds(start, size), to] = part
        copy.start()
    for copy in outs:
        copy.wait()
    rel_out.wait()


def compute(spot, counted, src, rel, dst, neg, left, right, left_sent, right_sent, rels):
    shape = jax.ShapeDtypeStruct
    n = rels.shape[0]
    table = pltpu.VMEM((D, E_PART), F32)
    rows = pltpu.VMEM((4 * E_PART, LANES), F32)
    block = pltpu.VMEM((8 * GROUP, LANES), F32)
    return pl.pallas_call(
        compute_kernel,
        out_shape=(shape((D, E_PART), F32), shape((D, E_PART), F32), shape((n, LANES), F32)),
        in_specs=[SMEM] * 2 + [HBM] * 3 + [VMEM] + [HBM] * 5,
        out_specs=(HBM,) * 3,
        scratch_shapes=[
            table, table, pltpu.VMEM((n, LANES), F32), table, table, rows, rows, pltpu.VMEM((n, LANES), F32),
            rows, rows,
            pltpu.VMEM((E_PART, 512), BF16),
            block, block, block,
            pltpu.VMEM((GROUP, 512), BF16), pltpu.VMEM((GROUP, E_PART), BF16), pltpu.VMEM((512, E_PART), F32),
            pltpu.SMEM((2 * SLOTS,), I32), pltpu.SMEM((2 * SLOTS,), I32), pltpu.SMEM((2 * SLOTS,), I32),
            pltpu.VMEM((6 * SLOTS,), I32),
            pltpu.SemaphoreType.DMA((3,)), pltpu.SemaphoreType.DMA((3,)),
        ],
        compiler_params=pltpu.CompilerParams(vmem_limit_bytes=LIMIT),
        cost_estimate=pl.CostEstimate(flops=20 * 10**9, bytes_accessed=10**8, transcendentals=10**6),
        name="blocks",
    )(spot, counted, src, rel, dst, neg, left, right, left_sent, right_sent, rels)


def exchange_kernel(
    left_grad, right_grad, rel_grad,
    left_sum, right_sum, rel_mine,
    left_own, left_sib, right_own, right_sib, acc, from_core,
    on_up0, on_down0, came_up0, came_down0, on_up2, on_down2, came_up2, came_down2, from_x0, from_x2, from_z0, from_z2, low_z, low_y, low_x,
    ls, lr, ss, sr, cs, cr, ys, yr, xs, xr, zs, zr, local,
):
    y, z, xh, core, xl = place()
    sib, xdev, ydev, zdev = neighbours()
    _, partner, diagonal = family()
    dom = lax.axis_index("dom")
    n_dom = 4 * Y * Z
    pair = dom - core
    barrier = pltpu.get_barrier_semaphore()
    peers = [sib, partner, diagonal] + xdev + ydev + zdev
    for peer in peers:
        pl.semaphore_signal(barrier, inc=1, device_id=peer, device_id_type=MESH)

    @pl.when(core == 0)
    def _():
        for k in (2, 1):
            behind = {"dom": lax.rem(dom + n_dom - k, n_dom), "rep": 1}
            pl.semaphore_signal(barrier, inc=1, device_id=behind, device_id_type=MESH)

    pl.semaphore_wait(barrier, len(peers) + 2 * xl)

    cut = [pl.ds(0, 24), pl.ds(24, 8), pl.ds(32, 16)]
    down = [
        remote(rel_grad.at[:, :, :, 1 - core, :, c], from_core.at[:, :, :, :, c], cs.at[i], cr.at[i], sib)
        for i, c in enumerate(cut)
    ]
    keep_rel = pltpu.make_async_copy(rel_grad.at[:, :, :, core], acc, local.at[2])
    keep_rel.start()
    half = D // 2
    mine, other = pl.ds(core * half, half), pl.ds((1 - core) * half, half)
    pairs = []
    for i, (grad, own, recv) in enumerate(((left_grad, left_own, left_sib), (right_grad, right_own, right_sib))):
        keep = pltpu.make_async_copy(grad.at[mine], own, local.at[i])
        keep.start()
        pairs.append((remote(grad.at[other], recv, ss.at[i], sr.at[i], sib), keep))

    keep_rel.wait()
    by_y, by_x, by_z = {0: [], 2: []}, {}, {}
    on_up, on_down = (on_up0, None, on_up2), (on_down0, None, on_down2)
    came_up, came_down = (came_up0, None, came_up2), (came_down0, None, came_down2)
    up, far, below = (lax.rem(y + k, Y) for k in range(1, Y))
    lo, hi = pl.ds(0, 4), pl.ds(4, 4)

    def passing(i, src, dst, to):
        n = 3 * i + len(by_y[i])
        by_y[i].append(remote(src, dst, ys.at[n], yr.at[n], to))

    middle = (from_x0, None, from_x2)
    last = (from_z0, None, from_z2)
    for i, c in enumerate(cut):
        down[i].wait()

        def add_core(n, _):
            at = (n // Z, lax.rem(n, Z), slice(None), slice(None), c)
            acc[at] += from_core[at]
            return 0

        lax.fori_loop(0, Y * Z, add_core, 0)
        if i == 1:
            by_z[i] = [
                remote(acc.at[:, lax.rem(z + k, Z), :, :, c], low_z.at[k - 1], zs.at[6 + k], zr.at[6 + k], zdev[k - 1])
                for k in range(1, Z)
            ]
            continue
        passing(i, acc.at[far, lo, :, :, c], on_up[i], ydev[0])
        passing(i, acc.at[far, hi, :, :, c], on_down[i], ydev[2])
        passing(i, acc.at[up, hi, :, :, c], came_up[i].at[hi], ydev[0])
        passing(i, acc.at[below, lo, :, :, c], came_down[i].at[lo], ydev[2])
    left_to = pair + xl
    right_to = lax.rem(pair + xl + 1, n_dom)
    sends, stays = [], []
    for i, (own, recv, out, to) in enumerate(
        ((left_own, left_sib, left_sum, left_to), (right_own, right_sib, right_sum, right_to))
    ):
        for copy in pairs[i]:
            copy.wait()

        def add(j, _):
            at = pl.ds(pl.multiple_of(8 * j, 8), 8)
            own[at, :] += recv[at, :]
            return 0

        lax.fori_loop(0, half // 8, add, 0)
        part = out.at[mine]
        far = prepared(own, part, ls.at[i, 0], lr.at[i, core, 0], {"dom": to, "rep": 1 - xl})
        near = prepared(own, part, ls.at[i, 1], lr.at[i, core, 1], {"dom": to, "rep": xl})
        stay = pltpu.make_async_copy(own, part, local.at[3 + i])
        far.start()
        self_too = to == dom

        @pl.when(self_too)
        def _():
            stay.start()

        @pl.when(jnp.logical_not(self_too))
        def _():
            near.start()

        sends.append((far, near, stay, self_too))

    for i in (0, 2):
        c, one, two = cut[i], on_up[i], on_down[i]
        by_y[i][0].wait()

        def add_up(n, _):
            acc[up, n, :, :, c] += one[n]
            return 0

        lax.fori_loop(0, 4, add_up, 0)
        passing(i, acc.at[up, lo, :, :, c], came_up[i].at[lo], ydev[0])
        by_y[i][1].wait()

        def add_down(n, _):
            acc[below, 4 + n, :, :, c] += two[n]
            return 0

        lax.fori_loop(0, 4, add_down, 0)
        passing(i, acc.at[below, hi, :, :, c], came_down[i].at[hi], ydev[2])
    for i in (0, 2):
        c, one, two = cut[i], came_up[i], came_down[i]
        for copy in by_y[i][2:]:
            copy.wait()

        def add_y(n, _):
            acc[y, n, :, :, c] += one[n] + two[n]
            return 0

        lax.fori_loop(0, Z, add_y, 0)
        by_x[i] = []
        for k in range(1, X):
            (a, b), n = shift_x(xh, xl, k), 3 * i + k - 1
            by_x[i].append(remote(acc.at[y, :, a, b, c], middle[i].at[k - 1], xs.at[n], xr.at[n], xdev[k - 1]))
    c = cut[1]
    for copy in by_z[1]:
        copy.wait()

    def add_z(n, _):
        total = acc[n, z, :, :, c]
        for k in range(Z - 1):
            total = total + low_z[k, n]
        acc[n, z, :, :, c] = total
        return 0

    lax.fori_loop(0, Y, add_z, 0)
    by_y[1] = [
        remote(acc.at[lax.rem(y + k, Y), z, :, :, c], low_y.at[k - 1], ys.at[11 + k], yr.at[11 + k], ydev[k - 1])
        for k in range(1, Y)
    ]
    for i in (0, 2):
        c, came = cut[i], middle[i]
        for copy in by_x[i]:
            copy.wait()

        def add_x(n, _):
            acc[y, n, xh, xl, c] += came[0, n] + came[1, n] + came[2, n]
            return 0

        lax.fori_loop(0, Z, add_x, 0)
        by_z[i] = []
        for k in range(1, Z):
            t, n = lax.rem(z + k, Z), 7 * i + k - 1
            by_z[i].append(remote(acc.at[y, t, xh, xl, c], last[i].at[k - 1], zs.at[n], zr.at[n], zdev[k - 1]))
    c = cut[1]
    for copy in by_y[1]:
        copy.wait()
    acc[y, z, :, :, c] += low_y[0] + low_y[1] + low_y[2]
    by_x[1] = []
    for k in range(1, X):
        a, b = shift_x(xh, xl, k)
        by_x[1].append(remote(acc.at[y, z, a, b, c], low_x.at[k - 1], xs.at[2 + k], xr.at[2 + k], xdev[k - 1]))
    for i in (0, 2):
        c = cut[i]
        for copy in by_z[i]:
            copy.wait()
        total = acc[y, z, xh, xl, c]
        for k in range(Z - 1):
            total = total + last[i][k]
        rel_mine[c, :] = total
    for copy in by_x[1]:
        copy.wait()
    rel_mine[cut[1], :] = acc[y, z, xh, xl, cut[1]] + low_x[0] + low_x[1] + low_x[2]

    for far, near, stay, self_too in sends:
        far.wait_send()

        @pl.when(self_too)
        def _():
            stay.wait()

        @pl.when(jnp.logical_not(self_too))
        def _():
            near.wait_send()

    for i, owner in ((0, core), (1, 1 - core)):
        own, out = ((left_own, left_sum), (right_own, right_sum))[i]
        for sender in range(2):
            part = out.at[pl.ds(sender * half, half)]
            local_chip = owner == xl
            to_self = jnp.logical_and(local_chip, jnp.logical_and(sender == core, jnp.logical_or(i == 0, core == 1)))
            came = lambda kind: prepared(own, part, ls.at[i, 0], lr.at[i, sender, kind], sib)

            @pl.when(jnp.logical_not(local_chip))
            def _():
                came(0).wait_recv()

            @pl.when(jnp.logical_and(local_chip, jnp.logical_not(to_self)))
            def _():
                came(1).wait_recv()


def exchange(left_grad, right_grad, rel_grad):
    dma = lambda *n: pltpu.SemaphoreType.DMA(n)
    shape = jax.ShapeDtypeStruct
    table = shape((D, E_PART), F32)
    half = pltpu.VMEM((D // 2, E_PART), F32)
    return pl.pallas_call(
        exchange_kernel,
        out_shape=(table, table, shape((SHARD, LANES), F32)),
        in_specs=[HBM] * 3,
        out_specs=(HBM, HBM, VMEM),
        scratch_shapes=[half] * 4
        + [
            pltpu.VMEM((Y, Z, 2, 2, SHARD, LANES), F32),
            pltpu.VMEM((Y, Z, 2, 2, SHARD, LANES), F32),
            *(pltpu.VMEM((n, 2, 2, rows, LANES), F32) for rows in (24, 16) for n in (4, 4, Z, Z)),
            pltpu.VMEM((3, Z, 24, LANES), F32), pltpu.VMEM((3, Z, 16, LANES), F32),
            pltpu.VMEM((7, 24, LANES), F32), pltpu.VMEM((7, 16, LANES), F32),
            pltpu.VMEM((7, Y, 2, 2, 8, LANES), F32), pltpu.VMEM((3, 2, 2, 8, LANES), F32), pltpu.VMEM((3, 8, LANES), F32),
            dma(2, 2), dma(2, 2, 2), dma(2), dma(2),
            dma(3), dma(3), dma(15), dma(15), dma(9), dma(9), dma(21), dma(21), dma(5),
        ],
        compiler_params=pltpu.CompilerParams(collective_id=1, has_side_effects=True, vmem_limit_bytes=LIMIT),
        name="exchange_gradients",
    )(left_grad, right_grad, rel_grad)


def update_kernel(
    left, left_state, left_sum, right, right_state, right_sum, rel, rel_state, rel_grad,
    left_next, left_state_next, right_next, right_state_next, rel_next, rel_state_next,
):
    for table, state, total, after, state_after in (
        (left, left_state, left_sum, left_next, left_state_next),
        (right, right_state, right_sum, right_next, right_state_next),
    ):
        grad = total[...]
        fresh = state[...] + jnp.sum(grad * grad, axis=0, keepdims=True) * (1.0 / D)
        state_after[...] = fresh
        after[...] = table[...] - grad * (RATE / jnp.sqrt(fresh))

    @pl.when(pl.program_id(0) == 0)
    def _():
        n = rel.shape[0]
        same = lax.broadcasted_iota(I32, (n, n), 0) == lax.broadcasted_iota(I32, (n, n), 1)
        column = lambda row: jnp.sum(jnp.where(same, jnp.broadcast_to(row, (n, n)), 0.0), axis=1, keepdims=True)
        across = lambda col: jnp.sum(jnp.where(same, jnp.broadcast_to(col, (n, n)), 0.0), axis=0, keepdims=True)
        grad = [rel_grad[pl.ds(j, n, stride=4), :] for j in range(4)]
        square = jnp.sum(sum(v * v for v in grad), axis=1, keepdims=True) * (1.0 / D)
        fresh = column(rel_state[...]) + square
        rel_state_next[...] = across(fresh)
        scale = RATE / jnp.sqrt(fresh)
        for j, change in enumerate(natural_of([v * scale for v in grad])):
            cols = pl.ds(j * LANES, change.shape[1])
            rel_next[:, cols] = rel[:, cols] - change


def update(left, left_state, left_sum, right, right_state, right_sum, rel, rel_state, rel_grad):
    wide = 4 * LANES
    table = pl.BlockSpec((D, wide), lambda g: (0, g))
    state = pl.BlockSpec((1, wide), lambda g: (0, g))
    whole = lambda shape: pl.BlockSpec(shape, lambda g: (0, 0))
    shape = jax.ShapeDtypeStruct
    big, row = shape((D, E_PART), F32), shape((1, E_PART), F32)
    return pl.pallas_call(
        update_kernel,
        grid=(E_PART // wide,),
        out_shape=(big, row, big, row, shape(rel.shape, F32), shape(rel_state.shape, F32)),
        in_specs=[table, state, table] * 2 + [whole(rel.shape), whole(rel_state.shape), whole((SHARD, LANES))],
        out_specs=(table, state, table, state, whole(rel.shape), whole(rel_state.shape)),
        compiler_params=pltpu.CompilerParams(vmem_limit_bytes=LIMIT),
        name="adagrad",
    )(left, left_state, left_sum, right, right_state, right_sum, rel, rel_state, rel_grad)


def shards(
    left_table, left_state, right_table, right_state, rel_table, rel_state,
    sources, relations, targets, bucket_counts, negatives,
):
    left, right = left_table.T, right_table.T
    rels, src, rel, dst, neg, counted, spot, left_use, right_use = gather(
        rel_table, sources, relations, targets, negatives, bucket_counts, left, right
    )
    n_dom = 4 * Y * Z
    route = [((i - 1) % n_dom, i) for i in range(n_dom)]
    held, held_state, rels = lax.optimization_barrier((right_table, right_state, rels))
    held = lax.ppermute(held, "dom", route)
    held_state = lax.ppermute(held_state, "dom", route)
    left_grad, right_grad, rel_grad = compute(
        spot, counted, src, rel, dst, neg, left, right, left_use, right_use, rels.reshape(-1, LANES)
    )
    held, held_state, rel_grad = lax.optimization_barrier((held, held_state, rel_grad))
    left_sum, right_sum, rel_mine = exchange(
        left_grad, right_grad, rel_grad.reshape(Y, Z, 2, 2, 2, SHARD, LANES)
    )
    left_next, left_after, right_next, right_after, rel_next, rel_after = update(
        left, left_state[None], left_sum, held.T, held_state[None], right_sum, rel_table, rel_state[None], rel_mine
    )
    return left_next.T, left_after[0], right_next.T, right_after[0], rel_next, rel_after[0]


def solution(mesh):
    both = P(("dom", "rep"))
    rows = P(("dom", "rep"), None)
    table, state = P("dom", None), P("dom")
    return jax.shard_map(
        shards,
        mesh=mesh,
        in_specs=(table, state, table, state, rows, both, both, both, both, state, rows),
        out_specs=(table, state, table, state, rows, both),
        check_vma=False,
    )
```
